32 devices in a mesh: seq: 16 (over z, y, x), tp: 2 (over core).
Axes of the slice: x: 2, y: 2, z: 4, core: 2. Of those that a mesh axis runs over, the one named last changes fastest.
Arguments:
- queries: bfloat16 [4096, 1024], P('seq', 'tp'), may hold values from -10 to 10
- key_vectors: bfloat16 [4096, 1024], P('seq', 'tp'), may hold values from -4 to 4
- value_vectors: bfloat16 [4096, 1024], P('seq', 'tp'), may hold values from -10 to 10
- out_grad: bfloat16 [4096, 1024], P('seq', 'tp'), may hold values from -6 to 6
Outputs:
- normed_out: bfloat16 [4096, 1024], P('seq', 'tp')
- query_grad: bfloat16 [4096, 1024], P('seq', 'tp')
- key_grad: bfloat16 [4096, 1024], P('seq', 'tp')
- value_grad: bfloat16 [4096, 1024], P('seq', 'tp')
The draws below stay inside these ranges and needn't reach their ends.
All inputs are finite; a program needn't handle non-finite values.
Results may differ from the reference program's by a relative error of at most 0.017.
Values may be sent and summed in bfloat16 or wider, within the bound.
No kernel may reach another device: no remote copies, remote signals or barrier semaphores. Data moves between devices by JAX's collectives and lax.ppermute only.
A program may use at most 128 MiB of HBM per device.

```python
import jax
import jax.numpy as jnp
from jax import lax

DH = 128
TOK_DEV = 256
GROUPS = 16
HEADS = 8
FEATURES = 1024
SEQLEN = 4096


def draw_queries(key, part):
    key = jax.random.fold_in(key, 11)
    first = jax.random.fold_in(key, 0)
    base = jax.random.normal(first, (SEQLEN, FEATURES), jnp.float32)
    return jnp.clip(2.0 * base, -10.0, 10.0).astype(jnp.bfloat16)


def draw_value_vectors(key, part):
    key = jax.random.fold_in(key, 23)
    first = jax.random.fold_in(key, 0)
    head_rank = (jnp.arange(FEATURES) // DH).astype(jnp.float32) / max(HEADS - 1, 1)
    scales = 2.0 ** head_rank[None, :]
    base = jnp.clip(jax.random.normal(first, (SEQLEN, FEATURES), jnp.float32), -5.0, 5.0)
    return (base * scales).astype(jnp.bfloat16)


def steps_of(stream_key, extent, cuts, low, largest):
    factor_of, own = 1.0, jax.random.fold_in(stream_key, 6)
    for dim, parts in cuts:
        draws = jnp.exp(jax.random.uniform(jax.random.fold_in(own, dim), (parts,), jnp.float32, low / len(cuts), largest / len(cuts)))
        factor_of = factor_of * jnp.repeat(draws, extent[dim] // parts).reshape([-1 if axis == dim else 1 for axis in range(len(extent))])
    return factor_of


def scatter_about(rng, dims, scale, limit, shards=(), kind=jnp.bfloat16):
    drawn = scale * jax.random.normal(rng, dims, jnp.float32)
    if shards:
        drawn = drawn * steps_of(rng, dims, shards, -0.22, 0.18)
    return jnp.clip(drawn, -limit, limit).astype(kind)


def setup_inputs(seed: int = 0) -> dict:
    keys = jax.random.split(jax.random.key(seed), 5)
    queries = draw_queries(jax.random.fold_in(keys[4], 71), 0)
    key_vectors = scatter_about(keys[1], (SEQLEN, FEATURES), 1.0, 4.0, ((0, 16), (1, 2)))
    value_vectors = draw_value_vectors(jax.random.fold_in(keys[4], 71), 0)
    out_grad = scatter_about(keys[3], (SEQLEN, FEATURES), 1.0, 6.0, ((0, 16), (1, 2)))
    return {"queries": queries, "key_vectors": key_vectors, "value_vectors": value_vectors, "out_grad": out_grad}


EPSILON = 1e-06

def round_trip(value):
    return lax.optimization_barrier(value.astype(jnp.bfloat16)).astype(jnp.float32)

def reference(queries, key_vectors, value_vectors, out_grad):
    block_shape = (GROUPS, TOK_DEV, HEADS, DH)
    query_blocks = queries.reshape(block_shape)
    key_blocks = key_vectors.reshape(block_shape)
    value_blocks = value_vectors.reshape(block_shape)
    cotangent_blocks = out_grad.reshape(GROUPS, TOK_DEV, FEATURES)
    causal = jnp.arange(TOK_DEV)[:, None] >= jnp.arange(TOK_DEV)[None, :]
    empty_state = jnp.zeros((HEADS, DH, DH), jnp.float32)

    def forward(prefix, blocks):
        query_block, key_block, value_block, cotangent = blocks
        query_full = query_block.astype(jnp.float32)
        key_full = key_block.astype(jnp.float32)
        value_full = value_block.astype(jnp.float32)
        cotangent_full = cotangent.astype(jnp.float32)
        group_state = round_trip(jnp.einsum('thd,the->hde', key_full, value_full))
        prefix_low = round_trip(prefix)
        raw_scores = jnp.einsum('thd,shd->hts', query_full, key_full)
        scores = round_trip(jnp.where(causal[None], raw_scores, jnp.zeros_like(raw_scores)))
        mixed = jnp.einsum('hts,she->the', scores, value_full) + jnp.einsum('thd,hde->the', query_full, prefix_low)
        mixed = mixed.reshape(TOK_DEV, FEATURES)
        inverse = lax.rsqrt(lax.optimization_barrier(jnp.mean(mixed * mixed, axis=1, keepdims=True)) + EPSILON)
        normed = mixed * inverse
        projection = lax.optimization_barrier(jnp.mean(cotangent_full * normed, axis=1, keepdims=True))
        mixed_grad = (inverse * (cotangent_full - normed * projection)).astype(jnp.bfloat16)
        return (prefix + group_state, (normed.astype(jnp.bfloat16), mixed_grad, prefix_low.astype(jnp.bfloat16)))
    _, (normed_blocks, grad_blocks, prefix_blocks) = lax.scan(forward, empty_state, (query_blocks, key_blocks, value_blocks, cotangent_blocks))

    def backward(suffix, blocks):
        query_block, key_block, value_block, grad_block, prefix_block = blocks
        query_full = query_block.astype(jnp.float32)
        key_full = key_block.astype(jnp.float32)
        value_full = value_block.astype(jnp.float32)
        mixed_grad = grad_block.reshape(TOK_DEV, HEADS, DH).astype(jnp.float32)
        prefix_low = prefix_block.astype(jnp.float32)
        grad_term = round_trip(jnp.einsum('thd,the->hde', query_full, mixed_grad))
        suffix_low = round_trip(suffix)
        raw_scores = jnp.einsum('thd,shd->hts', query_full, key_full)
        scores = round_trip(jnp.where(causal[None], raw_scores, jnp.zeros_like(raw_scores)))
        raw_coefs = jnp.einsum('the,she->hts', mixed_grad, value_full)
        coefs = round_trip(jnp.where(causal[None], raw_coefs, jnp.zeros_like(raw_coefs)))
        query_part = jnp.einsum('hts,shd->thd', coefs, key_full) + jnp.einsum('the,hde->thd', mixed_grad, prefix_low)
        key_part = jnp.einsum('hts,thd->shd', coefs, query_full) + jnp.einsum('she,hde->shd', value_full, suffix_low)
        value_part = jnp.einsum('hts,the->she', scores, mixed_grad) + jnp.einsum('shd,hde->she', key_full, suffix_low)
        outputs = (query_part.reshape(TOK_DEV, FEATURES).astype(jnp.bfloat16), key_part.reshape(TOK_DEV, FEATURES).astype(jnp.bfloat16), value_part.reshape(TOK_DEV, FEATURES).astype(jnp.bfloat16))
        return (suffix + grad_term, outputs)
    _, (query_grads, key_grads, value_grads) = lax.scan(backward, empty_state, (query_blocks, key_blocks, value_blocks, grad_blocks, prefix_blocks), reverse=True)
    return (normed_blocks.reshape(SEQLEN, FEATURES), query_grads.reshape(SEQLEN, FEATURES), key_grads.reshape(SEQLEN, FEATURES), value_grads.reshape(SEQLEN, FEATURES))
```

```python
import jax
import jax.numpy as jnp
from jax import lax
from jax.sharding import PartitionSpec as P

DH = 128
EPSILON = 1e-06


def exclusive_sum(state, before):
    size = lax.axis_size("seq")
    pieces = state.reshape(size, -1, DH)
    pieces = lax.all_to_all(pieces, "seq", 0, 0, tiled=True)
    index = jnp.arange(size)
    if before:
        mask = index[None, :] < index[:, None]
    else:
        mask = index[None, :] > index[:, None]
    sums = jnp.einsum("cj,jrd->crd", mask.astype(jnp.bfloat16), pieces, preferred_element_type=jnp.float32)
    sums = lax.all_to_all(sums.astype(jnp.bfloat16), "seq", 0, 0, tiled=True)
    return sums.reshape(state.shape)


def body(queries, key_vectors, value_vectors, out_grad):
    token_count, feature_count = queries.shape
    heads = feature_count // DH
    all_features = feature_count * lax.axis_size("tp")
    head_shape = (token_count, heads, DH)
    query_heads = queries.reshape(head_shape)
    key_heads = key_vectors.reshape(head_shape)
    value_heads = value_vectors.reshape(head_shape)
    causal = jnp.arange(token_count)[:, None] >= jnp.arange(token_count)[None, :]
    group_state = jnp.einsum(
        "thd,the->hde", key_heads, value_heads, preferred_element_type=jnp.float32
    ).astype(jnp.bfloat16)
    prefix_low = exclusive_sum(group_state, True)
    raw_scores = jnp.einsum(
        "thd,shd->hts", query_heads, key_heads, preferred_element_type=jnp.float32
    )
    scores = jnp.where(causal[None], raw_scores, jnp.zeros_like(raw_scores)).astype(jnp.bfloat16)
    mixed = jnp.einsum("hts,she->the", scores, value_heads, preferred_element_type=jnp.float32)
    mixed = mixed + jnp.einsum(
        "thd,hde->the", query_heads, prefix_low, preferred_element_type=jnp.float32
    )
    mixed = mixed.reshape(token_count, feature_count)
    cotangent = out_grad.astype(jnp.float32)
    sums = jnp.stack([jnp.sum(mixed * mixed, axis=1), jnp.sum(cotangent * mixed, axis=1)])
    sums = lax.psum(sums, "tp")
    inverse = lax.rsqrt(sums[0] / all_features + EPSILON)
    normed = mixed * inverse[:, None]
    projection = inverse * sums[1] / all_features
    normed_out = normed.astype(jnp.bfloat16)
    mixed_grad = (inverse[:, None] * (cotangent - normed * projection[:, None])).astype(
        jnp.bfloat16
    )
    mixed_grad = mixed_grad.reshape(head_shape)
    grad_term = jnp.einsum(
        "thd,the->hde", query_heads, mixed_grad, preferred_element_type=jnp.float32
    ).astype(jnp.bfloat16)
    suffix_low = exclusive_sum(grad_term, False)
    raw_coefs = jnp.einsum(
        "the,she->hts", mixed_grad, value_heads, preferred_element_type=jnp.float32
    )
    coefs = jnp.where(causal[None], raw_coefs, jnp.zeros_like(raw_coefs)).astype(jnp.bfloat16)
    query_part = jnp.einsum("hts,shd->thd", coefs, key_heads, preferred_element_type=jnp.float32)
    query_part = query_part + jnp.einsum(
        "the,hde->thd", mixed_grad, prefix_low, preferred_element_type=jnp.float32
    )
    key_part = jnp.einsum("hts,thd->shd", coefs, query_heads, preferred_element_type=jnp.float32)
    key_part = key_part + jnp.einsum(
        "she,hde->shd", value_heads, suffix_low, preferred_element_type=jnp.float32
    )
    value_part = jnp.einsum("hts,the->she", scores, mixed_grad, preferred_element_type=jnp.float32)
    value_part = value_part + jnp.einsum(
        "shd,hde->she", key_heads, suffix_low, preferred_element_type=jnp.float32
    )
    query_grad = query_part.reshape(token_count, feature_count).astype(jnp.bfloat16)
    key_grad = key_part.reshape(token_count, feature_count).astype(jnp.bfloat16)
    value_grad = value_part.reshape(token_count, feature_count).astype(jnp.bfloat16)
    return (normed_out, query_grad, key_grad, value_grad)


def solution(mesh):
    spec = P("seq", "tp")
    return jax.shard_map(body, mesh=mesh, in_specs=(spec,) * 4, out_specs=(spec,) * 4, check_vma=False)
```

```python
import functools

import jax
import jax.numpy as jnp
from jax import lax
from jax.experimental import pallas as pl
from jax.experimental.pallas import tpu as pltpu
from jax.sharding import PartitionSpec as P

DH = 128
EPSILON = 1e-06
QUAD = 4
LOW, WIDE = jnp.bfloat16, jnp.float32


def dot(a, b, contract):
    return lax.dot_general(a, b, ((contract[0], contract[1]), ((), ())), preferred_element_type=WIDE)


def head(ref, h):
    return ref.at[:, pl.ds(pl.multiple_of(h * DH, DH), DH)]


def fixed(ref, h):
    return ref.at[:, h * DH : (h + 1) * DH]


def causal_mask(count):
    row = lax.broadcasted_iota(jnp.int32, (count, count), 0)
    col = lax.broadcasted_iota(jnp.int32, (count, count), 1)
    return row >= col


def member_of_quad():
    return lax.axis_index("seq") % QUAD


def odd_place():
    return lax.axis_index("tp") % 2 == 1


def call(kernel, outs, args, flops, in_specs=None):
    size = sum(x.size * x.dtype.itemsize for x in list(args) + list(outs))
    return pl.pallas_call(
        kernel,
        out_shape=outs,
        in_specs=in_specs or vmem(len(args)),
        out_specs=[pl.BlockSpec(memory_space=pltpu.VMEM)] * len(outs),
        cost_estimate=pl.CostEstimate(flops=flops, bytes_accessed=size, transcendentals=0),
        compiler_params=pltpu.CompilerParams(vmem_limit_bytes=32 * 1024 * 1024),
    )(*args)


def state_kernel(k_ref, v_ref, out_ref):
    for h in range(QUAD):
        out_ref[h] = dot(fixed(k_ref, h)[...], fixed(v_ref, h)[...], ((0,), (0,))).astype(LOW)


def pair_kernel(own_ref, k_ref, v_ref, *outs):
    m = member_of_quad()
    for d in range(QUAD):
        h = m ^ d
        outs[d][0] = own_ref[h]
        outs[d][1] = dot(head(k_ref, h)[...], head(v_ref, h)[...], ((0,), (0,))).astype(LOW)


def local_kernel(q_ref, k_ref, v_ref, scores_ref, mixed_ref):
    mask = causal_mask(q_ref.shape[0])
    for h in range(QUAD):
        raw = dot(fixed(q_ref, h)[...], fixed(k_ref, h)[...], ((1,), (1,)))
        scores = jnp.where(mask, raw, 0.0).astype(LOW)
        scores_ref[h] = scores
        fixed(mixed_ref, h)[...] = dot(scores, fixed(v_ref, h)[...], ((1,), (0,)))


def mixed_kernel(local1, q1, c1, local2, q2, c2, p0, p1, p2, p3, mixed_ref, sums_ref):
    m = member_of_quad()
    count = q1.shape[0]
    square = jnp.zeros((count, DH), WIDE)
    product = jnp.zeros((count, DH), WIDE)
    for core, (local, q_ref, c_ref) in enumerate(((local1, q1, c1), (local2, q2, c2))):
        for e, p_ref in enumerate((p0, p1, p2, p3)):
            h = m ^ e
            mixed = head(local, h)[...] + dot(head(q_ref, h)[...], p_ref[core], ((1,), (0,)))
            mixed_ref[core, e] = mixed
            square = square + mixed * mixed
            product = product + mixed * head(c_ref, h)[...].astype(WIDE)
    sums_ref[0:1, :] = jnp.sum(square.T, axis=0, keepdims=True)
    sums_ref[1:2, :] = jnp.sum(product.T, axis=0, keepdims=True)


def token_scales(sums_ref, features, count):
    inverse = lax.rsqrt(sums_ref[0:1, :] * (1.0 / features) + EPSILON)
    projection = inverse * sums_ref[1:2, :] * (1.0 / features)
    inverse = jnp.broadcast_to(inverse, (DH, count)).T
    projection = jnp.broadcast_to(projection, (DH, count)).T
    return inverse, projection


def term_kernel(features, mixed_ref, q1, c1, q2, c2, sums_ref, *outs):
    m = member_of_quad()
    inverse, projection = token_scales(sums_ref, features, q1.shape[0])
    for core, (q_ref, c_ref) in enumerate(((q1, c1), (q2, c2))):
        for d in range(QUAD):
            h = m ^ d
            normed = mixed_ref[core, d] * inverse
            grad = (inverse * (head(c_ref, h)[...].astype(WIDE) - normed * projection)).astype(LOW)
            outs[d][core] = dot(head(q_ref, h)[...], grad, ((0,), (0,))).astype(LOW)


def query_kernel(features, q_ref, k_ref, v_ref, c_ref, local_ref, own_ref, got_ref, sums_ref,
                 normed_ref, query_ref, g_ref, coefs_ref):
    m = member_of_quad()
    count = q_ref.shape[0]
    mask = causal_mask(count)
    inverse, projection = token_scales(sums_ref, features, count)
    odd = odd_place()
    for e in range(QUAD):
        h = m ^ e
        prefix = jnp.where(odd, own_ref[e], got_ref[e])
        mixed = head(local_ref, h)[...] + dot(head(q_ref, h)[...], prefix, ((1,), (0,)))
        normed = mixed * inverse
        head(normed_ref, h)[...] = normed.astype(LOW)
        grad = (inverse * (head(c_ref, h)[...].astype(WIDE) - normed * projection)).astype(LOW)
        head(g_ref, h)[...] = grad
        raw = dot(grad, head(v_ref, h)[...], ((1,), (1,)))
        coefs = jnp.where(mask, raw, 0.0).astype(LOW)
        coefs_ref[h] = coefs
        query = dot(coefs, head(k_ref, h)[...], ((1,), (0,))) + dot(grad, prefix, ((1,), (1,)))
        head(query_ref, h)[...] = query.astype(LOW)


def inner_kernel(q_ref, g_ref, scores_ref, coefs_ref, key_ref, value_ref):
    for h in range(QUAD):
        fixed(key_ref, h)[...] = dot(coefs_ref[h], fixed(q_ref, h)[...], ((0,), (0,)))
        fixed(value_ref, h)[...] = dot(scores_ref[h], fixed(g_ref, h)[...], ((0,), (0,)))


def last_kernel(k_ref, v_ref, key_local, value_local, own_ref, got_ref, key_ref, value_ref):
    m = member_of_quad()
    odd = odd_place()
    for e in range(QUAD):
        h = m ^ e
        suffix = jnp.where(odd, own_ref[e], got_ref[e])
        key = head(key_local, h)[...] + dot(head(v_ref, h)[...], suffix, ((1,), (1,)))
        head(key_ref, h)[...] = key.astype(LOW)
        value = head(value_local, h)[...] + dot(head(k_ref, h)[...], suffix, ((1,), (0,)))
        head(value_ref, h)[...] = value.astype(LOW)


def exchange(value, bits):
    size = lax.axis_size("tp")
    return lax.ppermute(value, "tp", [(i, i ^ bits) for i in range(size)])


def send(value, bits):
    cores = lax.axis_size("tp")
    idle = QUAD if bits < QUAD else 1
    pairs = [
        (i * cores + t, (i ^ (bits if t % 2 else idle)) * cores + t)
        for i in range(lax.axis_size("seq"))
        for t in range(cores)
    ]
    return lax.ppermute(value, ("seq", "tp"), pairs)


def sums_kernel(before, count, *refs):
    index = lax.axis_index("seq")
    m = index % QUAD
    held, got, outs = refs[:QUAD], refs[QUAD : QUAD + count], refs[-QUAD:]

    def counts(a, b):
        return jnp.where(a < b if before else a > b, 1.0, 0.0).astype(WIDE)

    outer = jnp.zeros(held[0].shape, WIDE)
    for n in range(count):
        outer = outer + got[n][...].astype(WIDE) * counts(index ^ (QUAD * (n + 1)), index)
    pieces = [piece[...].astype(WIDE) for piece in held]
    for e in range(QUAD):
        inner = outer
        for d in range(QUAD):
            if d != e:
                inner = inner + pieces[d] * counts(m ^ d, m ^ e)
        outs[e][...] = inner.astype(LOW)


def stack_kernel(core, p0, p1, p2, p3, *refs):
    for e, p_ref in enumerate((p0, p1, p2, p3)):
        refs[-1][e] = p_ref[core]


def vmem(count):
    return [pl.BlockSpec(memory_space=pltpu.VMEM)] * count


def unused(count):
    return [pl.BlockSpec(memory_space=pl.ANY)] * count


def exclusive_sum(held, before, after=()):
    held = [held[0]] + [send(held[d], d) for d in range(1, QUAD)]
    total = sum(piece.astype(WIDE) for piece in held).astype(LOW)
    got = [send(total, bits) for bits in range(QUAD, lax.axis_size("seq"), QUAD)]
    sums = call(
        functools.partial(sums_kernel, before, len(got)),
        [jax.ShapeDtypeStruct(x.shape, x.dtype) for x in held],
        (*held, *got, *after),
        0,
        in_specs=vmem(QUAD + len(got)) + unused(len(after)),
    )
    return [sums[0]] + [send(sums[e], e) for e in range(1, QUAD)]


def body(q, k, v, c):
    count, width = q.shape
    features = width * lax.axis_size("tp")
    shape = jax.ShapeDtypeStruct
    states = shape((QUAD, DH, DH), LOW)
    pair = shape((2, DH, DH), LOW)
    wide = shape((count, width), WIDE)
    low = shape((count, width), LOW)
    square = shape((QUAD, count, count), LOW)
    unit = 2 * count * DH * DH * QUAD
    odd = odd_place()

    def share(arrays, *after):
        own, other = [
            call(
                functools.partial(stack_kernel, core), [states], (*arrays, *after), 0,
                in_specs=vmem(QUAD) + unused(len(after)),
            )[0]
            for core in range(2)
        ]
        return own, exchange(other, 1)

    k2, v2, q2, c2 = [exchange(x, 1) for x in (k, v, q, c)]
    own = call(state_kernel, [states], (k, v), unit)[0]
    held = call(pair_kernel, [pair] * QUAD, (own, k2, v2), unit)
    scores, local = call(local_kernel, [square, wide], (q, k, v), 4 * unit)
    _, local2 = call(local_kernel, [square, wide], (q2, k2, v2), 4 * unit)
    prefix = exclusive_sum(held, True)
    mixed, sums = call(
        mixed_kernel,
        [shape((2, QUAD, count, DH), WIDE), shape((2, count), WIDE)],
        (local, q, c, local2, q2, c2, *prefix),
        2 * unit,
    )
    bits = 2
    while bits < lax.axis_size("tp"):
        sums = sums + exchange(sums, bits)
        bits *= 2
    terms = call(
        functools.partial(term_kernel, features), [pair] * QUAD, (mixed, q, c, q2, c2, sums), 2 * unit
    )
    own_sums = jnp.where(odd, sums, exchange(sums, 1))
    normed_out, query_grad, g, coefs = call(
        functools.partial(query_kernel, features),
        [low, low, low, square],
        (q, k, v, c, local, *share(prefix), own_sums),
        6 * unit,
    )
    suffix = exclusive_sum(terms, False, (g,))
    key_local, value_local = call(inner_kernel, [wide, wide], (q, g, scores, coefs), 4 * unit)
    key_grad, value_grad = call(
        last_kernel, [low, low], (k, v, key_local, value_local, *share(suffix, key_local)), 2 * unit
    )
    return (normed_out, query_grad, key_grad, value_grad)


def solution(mesh):
    spec = P("seq", "tp")
    return jax.shard_map(body, mesh=mesh, in_specs=(spec,) * 4, out_specs=(spec,) * 4, check_vma=False)
```

```python
import functools

import jax
import jax.numpy as jnp
from jax import lax
from jax.experimental import pallas as pl
from jax.experimental.pallas import tpu as pltpu
from jax.sharding import PartitionSpec as P

DH = 128
EPSILON = 1e-06
QUAD = 4
ORDER = (3, 2, 1, 0)
CHUNKS = 4
LOW, WIDE = jnp.bfloat16, jnp.float32


def dot(a, b, contract):
    return lax.dot_general(a, b, ((contract[0], contract[1]), ((), ())), preferred_element_type=WIDE)


def head(ref, h):
    return ref.at[:, pl.ds(pl.multiple_of(h * DH, DH), DH)]


def fixed(ref, h):
    return ref.at[:, h * DH : (h + 1) * DH]


def causal_mask(count):
    row = lax.broadcasted_iota(jnp.int32, (count, count), 0)
    col = lax.broadcasted_iota(jnp.int32, (count, count), 1)
    return row >= col


def member_of_quad():
    return lax.axis_index("seq") % QUAD


def call(kernel, outs, args, flops, in_specs=None, scratch_shapes=(), room=32):
    size = sum(x.size * x.dtype.itemsize for x in list(args) + list(outs))
    return pl.pallas_call(
        kernel,
        out_shape=outs,
        in_specs=in_specs or [pl.BlockSpec(memory_space=pltpu.VMEM)] * len(args),
        out_specs=[pl.BlockSpec(memory_space=pltpu.VMEM)] * len(outs),
        scratch_shapes=scratch_shapes,
        cost_estimate=pl.CostEstimate(flops=flops, bytes_accessed=size, transcendentals=0),
        compiler_params=pltpu.CompilerParams(vmem_limit_bytes=int(room * 1024 * 1024)),
    )(*args)


def state_kernel(k_ref, v_ref, o0, o1, o2, o3, k_buf, v_buf, sems):
    rows = k_ref.shape[0] // CHUNKS
    copies = []
    for i in range(CHUNKS):
        for n, (ref, buf) in enumerate(((k_ref, k_buf), (v_ref, v_buf))):
            part = pl.ds(i * rows, rows)
            copies.append(pltpu.make_async_copy(ref.at[part], buf.at[part], sems.at[n, i]))
            copies[-1].start()
    for copy in copies:
        copy.wait()
    m = member_of_quad()
    for d, out in enumerate((o0, o1, o2, o3)):
        h = m ^ d
        out[...] = dot(head(k_buf, h)[...], head(v_buf, h)[...], ((0,), (0,))).astype(LOW)


def local_kernel(q_ref, k_ref, v_ref, scores_ref, mixed_ref):
    mask = causal_mask(q_ref.shape[0])
    for h in range(QUAD):
        raw = dot(fixed(q_ref, h)[...], fixed(k_ref, h)[...], ((1,), (1,)))
        scores = jnp.where(mask, raw, 0.0).astype(LOW)
        scores_ref[h] = scores
        fixed(mixed_ref, h)[...] = dot(scores, fixed(v_ref, h)[...], ((1,), (0,)))


def mixed_kernel(local_ref, q_ref, c_ref, p0, p1, p2, p3, mixed_ref, sums_ref):
    m = member_of_quad()
    count = q_ref.shape[0]
    square = jnp.zeros((count, DH), WIDE)
    product = jnp.zeros((count, DH), WIDE)
    for e, p_ref in enumerate((p0, p1, p2, p3)):
        h = m ^ e
        mixed = head(local_ref, h)[...] + dot(head(q_ref, h)[...], p_ref[...], ((1,), (0,)))
        head(mixed_ref, h)[...] = mixed
        square = square + mixed * mixed
        product = product + mixed * head(c_ref, h)[...].astype(WIDE)
    sums_ref[0:1, :] = jnp.sum(square.T, axis=0, keepdims=True)
    sums_ref[1:2, :] = jnp.sum(product.T, axis=0, keepdims=True)


def token_scales(sums_ref, features, count):
    inverse = lax.rsqrt(sums_ref[0:1, :] * (1.0 / features) + EPSILON)
    projection = inverse * sums_ref[1:2, :] * (1.0 / features)
    inverse = jnp.broadcast_to(inverse, (DH, count)).T
    projection = jnp.broadcast_to(projection, (DH, count)).T
    return inverse, projection


def grad_kernel(features, mixed_ref, c_ref, q_ref, sums_ref, g_ref, *outs):
    m = member_of_quad()
    inverse, projection = token_scales(sums_ref, features, q_ref.shape[0])
    for d in range(QUAD):
        h = m ^ d
        normed = head(mixed_ref, h)[...] * inverse
        grad = (inverse * (head(c_ref, h)[...].astype(WIDE) - normed * projection)).astype(LOW)
        head(g_ref, h)[...] = grad
        outs[d][...] = dot(head(q_ref, h)[...], grad, ((0,), (0,))).astype(LOW)


def back_kernel(features, q_ref, k_ref, v_ref, g_ref, scores_ref, mixed_ref, sums_ref, p0, p1, p2, p3,
                normed_ref, query_ref, key_ref, value_ref):
    m = member_of_quad()
    count = q_ref.shape[0]
    mask = causal_mask(count)
    inverse, _ = token_scales(sums_ref, features, count)
    for e, p_ref in enumerate((p0, p1, p2, p3)):
        h = m ^ e
        grad = head(g_ref, h)[...]
        head(normed_ref, h)[...] = (head(mixed_ref, h)[...] * inverse).astype(LOW)
        raw = dot(grad, head(v_ref, h)[...], ((1,), (1,)))
        coefs = jnp.where(mask, raw, 0.0).astype(LOW)
        query = dot(coefs, head(k_ref, h)[...], ((1,), (0,))) + dot(grad, p_ref[...], ((1,), (1,)))
        head(query_ref, h)[...] = query.astype(LOW)
        head(key_ref, h)[...] = dot(coefs, head(q_ref, h)[...], ((0,), (0,)))
        head(value_ref, h)[...] = dot(scores_ref[h], grad, ((0,), (0,)))


def last_kernel(k_ref, v_ref, key_local, value_local, p0, p1, p2, p3, key_ref, value_ref):
    m = member_of_quad()
    for e, p_ref in enumerate((p0, p1, p2, p3)):
        h = m ^ e
        suffix = p_ref[...]
        key = head(key_local, h)[...] + dot(head(v_ref, h)[...], suffix, ((1,), (1,)))
        head(key_ref, h)[...] = key.astype(LOW)
        value = head(value_local, h)[...] + dot(head(k_ref, h)[...], suffix, ((1,), (0,)))
        head(value_ref, h)[...] = value.astype(LOW)


def exchange(value, axis, bits):
    size = lax.axis_size(axis)
    return lax.ppermute(value, axis, [(i, i ^ bits) for i in range(size)])


def cross(value, bits):
    cores = lax.axis_size("tp")
    places = [(i, t) for i in range(lax.axis_size("seq")) for t in range(cores)]
    pairs = [(i * cores + t, (i ^ bits) * cores + (t ^ 1)) for i, t in places]
    return lax.ppermute(value, ("seq", "tp"), pairs)


def exclusive_sum(held, before):
    index = lax.axis_index("seq")
    m = index % QUAD
    held = [cross(held[d], d) for d in ORDER]
    held = [held[ORDER.index(d)].astype(WIDE) for d in range(QUAD)]
    total = (held[0] + held[1] + held[2] + held[3]).astype(LOW)

    def counts(a, b):
        return a < b if before else a > b

    outer = jnp.zeros_like(held[0])
    for bits in range(QUAD, lax.axis_size("seq"), QUAD):
        got = exchange(total, "seq", bits).astype(WIDE)
        outer = outer + jnp.where(counts(index ^ bits, index), got, 0.0)
    sums = []
    for e in range(QUAD):
        inner = outer
        for d in range(QUAD):
            if d != e:
                inner = inner + jnp.where(counts(m ^ d, m ^ e), held[d], 0.0)
        sums.append(inner.astype(LOW))
    sums = [cross(sums[e], e) for e in ORDER]
    return [sums[ORDER.index(e)] for e in range(QUAD)]


def sum_over_heads(value):
    bit = 1
    while bit < lax.axis_size("tp"):
        value = value + exchange(value, "tp", bit)
        bit *= 2
    return value


def body(q, k, v, c):
    count, width = q.shape
    features = width * lax.axis_size("tp")
    shape = jax.ShapeDtypeStruct
    state = shape((DH, DH), LOW)
    wide = shape((count, width), WIDE)
    low = shape((count, width), LOW)
    unit = 2 * count * DH * DH * QUAD
    held = call(
        state_kernel, [state] * QUAD, (k, v), unit, room=53.75,
        in_specs=[pl.BlockSpec(memory_space=pltpu.HBM)] * 2,
        scratch_shapes=[pltpu.VMEM(k.shape, LOW)] * 2 + [pltpu.SemaphoreType.DMA((2, CHUNKS))],
    )
    scores, local = call(
        local_kernel, [shape((QUAD, count, count), LOW), wide], (q, k, v), 4 * unit
    )
    prefix = exclusive_sum(held, True)
    mixed, sums = call(
        mixed_kernel, [wide, shape((2, count), WIDE)], (local, q, c, *prefix), unit
    )
    sums = sum_over_heads(sums)
    g, *terms = call(
        functools.partial(grad_kernel, features), [low] + [state] * QUAD, (mixed, c, q, sums), unit
    )
    normed_out, query_grad, key_local, value_local = call(
        functools.partial(back_kernel, features),
        [low, low, wide, wide],
        (q, k, v, g, scores, mixed, sums, *prefix),
        9 * unit,
    )
    suffix = exclusive_sum(terms, False)
    key_grad, value_grad = call(
        last_kernel, [low, low], (k, v, key_local, value_local, *suffix), 2 * unit
    )
    return (normed_out, query_grad, key_grad, value_grad)


def solution(mesh):
    spec = P("seq", "tp")
    return jax.shard_map(body, mesh=mesh, in_specs=(spec,) * 4, out_specs=(spec,) * 4, check_vma=False)
```

```python
import functools

import jax
import jax.numpy as jnp
from jax import lax
from jax.experimental import pallas as pl
from jax.experimental.pallas import tpu as pltpu
from jax.sharding import PartitionSpec as P

DH = 128
EPSILON = 1e-06
QUAD = 4
ORDER = (3, 2, 1, 0)
BACK = (2, 1, 0, 3)
CHUNKS = 4
LOW, WIDE = jnp.bfloat16, jnp.float32


def dot(a, b, contract):
    return lax.dot_general(a, b, ((contract[0], contract[1]), ((), ())), preferred_element_type=WIDE)


def head(ref, h):
    return ref.at[:, pl.ds(pl.multiple_of(h * DH, DH), DH)]


def fixed(ref, h):
    return ref.at[:, h * DH : (h + 1) * DH]


def causal_mask(count):
    row = lax.broadcasted_iota(jnp.int32, (count, count), 0)
    col = lax.broadcasted_iota(jnp.int32, (count, count), 1)
    return row >= col


def member_of_quad():
    return lax.axis_index("seq") % QUAD


def call(kernel, outs, args, flops, in_specs=None, out_specs=None, scratch_shapes=(), room=32):
    size = sum(x.size * x.dtype.itemsize for x in list(args) + list(outs))
    return pl.pallas_call(
        kernel,
        out_shape=outs,
        in_specs=in_specs or [pl.BlockSpec(memory_space=pltpu.VMEM)] * len(args),
        out_specs=out_specs or [pl.BlockSpec(memory_space=pltpu.VMEM)] * len(outs),
        scratch_shapes=scratch_shapes,
        cost_estimate=pl.CostEstimate(flops=flops, bytes_accessed=size, transcendentals=0),
        compiler_params=pltpu.CompilerParams(vmem_limit_bytes=int(room * 1024 * 1024)),
    )(*args)


def state_kernel(k_ref, v_ref, o3, o2, o1, o0, k_buf, v_buf, sems):
    rows = k_ref.shape[0] // CHUNKS
    copies = []
    for i in range(CHUNKS):
        for n, (ref, buf) in enumerate(((k_ref, k_buf), (v_ref, v_buf))):
            part = pl.ds(i * rows, rows)
            copies.append(pltpu.make_async_copy(ref.at[part], buf.at[part], sems.at[n, i]))
            copies[-1].start()
    for copy in copies:
        copy.wait()
    m = member_of_quad()
    for d, out in zip(ORDER, (o3, o2, o1, o0)):
        h = m ^ d
        out[...] = dot(head(k_buf, h)[...], head(v_buf, h)[...], ((0,), (0,))).astype(LOW)


def local_kernel(q_ref, k_ref, v_ref, scores_ref, mixed_ref):
    mask = causal_mask(q_ref.shape[0])
    for h in range(QUAD):
        raw = dot(fixed(q_ref, h)[...], fixed(k_ref, h)[...], ((1,), (1,)))
        scores = jnp.where(mask, raw, 0.0).astype(LOW)
        scores_ref[h] = scores
        fixed(mixed_ref, h)[...] = dot(scores, fixed(v_ref, h)[...], ((1,), (0,)))


def pack_kernel(q_ref, k_ref, v_ref, c_ref, *outs):
    m = member_of_quad()
    for d, out in zip(ORDER, outs):
        for n, ref in enumerate((q_ref, k_ref, v_ref, c_ref)):
            out[n] = head(ref, m ^ d)[...]


def owner_local_kernel(*refs):
    mask = causal_mask(refs[0].shape[1])
    for pack, out in zip(refs[:QUAD], refs[QUAD:]):
        raw = dot(pack[0], pack[1], ((1,), (1,)))
        scores = jnp.where(mask, raw, 0.0).astype(LOW)
        out[...] = dot(scores, pack[2], ((1,), (0,)))


def exclusive_sums(before, held, got):
    index = lax.axis_index("seq")
    m = index % QUAD

    def counts(a, b):
        return jnp.where(a < b if before else a > b, 1.0, 0.0).astype(WIDE)

    outer = jnp.zeros((DH, DH), WIDE)
    for n, total in enumerate(got):
        outer = outer + total[...].astype(WIDE) * counts(index ^ (QUAD * (n + 1)), index)
    pieces = [piece[...].astype(WIDE) for piece in held]
    sums = []
    for e in ORDER:
        inner = outer
        for d, piece in zip(ORDER, pieces):
            if d != e:
                inner = inner + piece * counts(m ^ d, m ^ e)
        sums.append(inner.astype(LOW))
    return sums


def mixed_kernel(quads, *refs):
    packs, locals_, held = refs[:QUAD], refs[QUAD : 2 * QUAD], refs[2 * QUAD : 3 * QUAD]
    got = refs[3 * QUAD : 3 * QUAD + quads]
    mixed_ref, *prefixes, sums_ref = refs[3 * QUAD + quads :]
    m = member_of_quad()
    count = packs[0].shape[1]
    lane = lax.broadcasted_iota(jnp.int32, (count, DH), 1)
    columns = jnp.zeros((count, DH), WIDE)
    for n, prefix in enumerate(exclusive_sums(True, held, got)):
        prefixes[n][...] = prefix
        mixed = locals_[n][...] + dot(packs[n][0], prefix, ((1,), (0,)))
        mixed_ref[n] = mixed
        square = jnp.sum(mixed * mixed, axis=1, keepdims=True)
        product = jnp.sum(mixed * packs[n][3].astype(WIDE), axis=1, keepdims=True)
        columns = jnp.where(lane == 2 * n, square, jnp.where(lane == 2 * n + 1, product, columns))
    rows = columns.T
    for n, d in enumerate(ORDER):
        sums_ref[pl.ds(2 * (m ^ d), 1), :] = rows[2 * n : 2 * n + 1, :]
        sums_ref[pl.ds(2 * (m ^ d) + 1, 1), :] = rows[2 * n + 1 : 2 * n + 2, :]


def scales(sums_ref, member, features):
    square = sums_ref[pl.ds(2 * member, 1), :]
    product = sums_ref[pl.ds(2 * member + 1, 1), :]
    inverse = lax.rsqrt(square * (1.0 / features) + EPSILON)
    return inverse, inverse * product * (1.0 / features)


def term_kernel(features, *refs):
    packs, mixed_ref, sums_ref = refs[:QUAD], refs[QUAD], refs[QUAD + 1]
    *terms, total_ref, rows_ref = refs[QUAD + 3 :]
    m = member_of_quad()
    for n, d in enumerate(ORDER):
        inverse, projection = scales(sums_ref, m ^ d, features)
        rows_ref[2 * n : 2 * n + 1, :] = inverse
        rows_ref[2 * n + 1 : 2 * n + 2, :] = projection
    columns = rows_ref[...].T
    total = jnp.zeros((DH, DH), WIDE)
    for n in range(QUAD):
        inverse = columns[:, 2 * n : 2 * n + 1]
        projection = columns[:, 2 * n + 1 : 2 * n + 2]
        normed = mixed_ref[n] * inverse
        grad = (inverse * (packs[n][3].astype(WIDE) - normed * projection)).astype(LOW)
        term = dot(packs[n][0], grad, ((0,), (0,))).astype(LOW)
        terms[n][...] = term
        total = total + term.astype(WIDE)
    total_ref[...] = total.astype(LOW)


def suffix_kernel(quads, *refs):
    outs = refs[QUAD + quads :]
    for out, suffix in zip(outs, exclusive_sums(False, refs[:QUAD], refs[QUAD : QUAD + quads])):
        out[...] = suffix


def back_kernel(features, q_ref, k_ref, v_ref, c_ref, scores_ref, local_ref, sums_ref, p2, p1, p0, p3,
                normed_ref, query_ref, key_ref, value_ref):
    m = member_of_quad()
    count = q_ref.shape[0]
    mask = causal_mask(count)
    inverse, projection = scales(sums_ref, m, features)
    inverse = jnp.broadcast_to(inverse, (DH, count)).T
    projection = jnp.broadcast_to(projection, (DH, count)).T
    for e, p_ref in zip(BACK, (p2, p1, p0, p3)):
        h = m ^ e
        prefix = p_ref[...]
        normed = (head(local_ref, h)[...] + dot(head(q_ref, h)[...], prefix, ((1,), (0,)))) * inverse
        head(normed_ref, h)[...] = normed.astype(LOW)
        grad = (inverse * (head(c_ref, h)[...].astype(WIDE) - normed * projection)).astype(LOW)
        raw = dot(grad, head(v_ref, h)[...], ((1,), (1,)))
        coefs = jnp.where(mask, raw, 0.0).astype(LOW)
        query = dot(coefs, head(k_ref, h)[...], ((1,), (0,))) + dot(grad, prefix, ((1,), (1,)))
        head(query_ref, h)[...] = query.astype(LOW)
        head(key_ref, h)[...] = dot(coefs, head(q_ref, h)[...], ((0,), (0,)))
        head(value_ref, h)[...] = dot(scores_ref[h], grad, ((0,), (0,)))


def last_kernel(k_ref, v_ref, key_local, value_local, p2, p1, p0, p3, key_ref, value_ref):
    m = member_of_quad()
    for e, p_ref in zip(BACK, (p2, p1, p0, p3)):
        h = m ^ e
        suffix = p_ref[...]
        key = head(key_local, h)[...] + dot(head(v_ref, h)[...], suffix, ((1,), (1,)))
        head(key_ref, h)[...] = key.astype(LOW)
        value = head(value_local, h)[...] + dot(head(k_ref, h)[...], suffix, ((1,), (0,)))
        head(value_ref, h)[...] = value.astype(LOW)


def exchange(value, axis, bits):
    size = lax.axis_size(axis)
    return lax.ppermute(value, axis, [(i, i ^ bits) for i in range(size)])


def cross(value, bits):
    cores = lax.axis_size("tp")
    places = [(i, t) for i in range(lax.axis_size("seq")) for t in range(cores)]
    pairs = [(i * cores + t, (i ^ bits) * cores + (t ^ 1)) for i, t in places]
    return lax.ppermute(value, ("seq", "tp"), pairs)


def to_owners(pieces):
    return [cross(piece, d) for piece, d in zip(pieces, ORDER)]


def from_owners(pieces):
    pieces = dict(zip(ORDER, pieces))
    return [cross(pieces[d], d) for d in BACK]


def other_quads(total):
    return [exchange(total, "seq", bits) for bits in range(QUAD, lax.axis_size("seq"), QUAD)]


def add_over_heads(sums):
    bit = 1
    while bit < lax.axis_size("tp"):
        sums = sums + exchange(sums, "tp", bit)
        bit *= 2
    got = [exchange(sums, "seq", d) for d in ORDER[:-1]]
    return got[0] + got[1] + got[2] + sums


def body(q, k, v, c):
    count, width = q.shape
    features = width * lax.axis_size("tp")
    quads = lax.axis_size("seq") // QUAD - 1
    shape = jax.ShapeDtypeStruct
    state = shape((DH, DH), LOW)
    wide = shape((count, width), WIDE)
    low = shape((count, width), LOW)
    unit = 2 * count * DH * DH * QUAD
    held = call(
        state_kernel, [state] * QUAD, (k, v), unit, room=53.75,
        in_specs=[pl.BlockSpec(memory_space=pltpu.HBM)] * 2,
        scratch_shapes=[pltpu.VMEM(k.shape, LOW)] * 2 + [pltpu.SemaphoreType.DMA((2, CHUNKS))],
    )
    held = to_owners(held)
    packs = to_owners(call(pack_kernel, [shape((4, count, DH), LOW)] * QUAD, (q, k, v, c), 0))
    total = sum(piece.astype(WIDE) for piece in held).astype(LOW)
    got = other_quads(total)
    owner_local = call(owner_local_kernel, [shape((count, DH), WIDE)] * QUAD, packs, 4 * unit)
    mixed, *prefixes, sums = call(
        functools.partial(mixed_kernel, quads),
        [shape((QUAD, count, DH), WIDE)] + [state] * QUAD + [shape((2 * QUAD, count), WIDE)],
        (*packs, *owner_local, *held, *got),
        unit,
    )
    sums = add_over_heads(sums)
    scores, local = call(local_kernel, [shape((QUAD, count, count), LOW), wide], (q, k, v), 4 * unit)
    *terms, total = call(
        functools.partial(term_kernel, features),
        [state] * (QUAD + 1),
        (*packs, mixed, sums, local),
        unit,
        in_specs=[pl.BlockSpec(memory_space=pltpu.VMEM)] * (QUAD + 2) + [pl.BlockSpec(memory_space=pl.ANY)],
        scratch_shapes=[pltpu.VMEM((DH, count), WIDE)],
    )
    got = other_quads(total)
    prefixes = from_owners(prefixes)
    suffixes = call(functools.partial(suffix_kernel, quads), [state] * QUAD, (*terms, *got), 0)
    suffixes = from_owners(suffixes)
    normed_out, query_grad, key_local, value_local = call(
        functools.partial(back_kernel, features),
        [low, low, wide, wide],
        (q, k, v, c, scores, local, sums, *prefixes),
        10 * unit,
    )
    key_grad, value_grad = call(
        last_kernel, [low, low], (k, v, key_local, value_local, *suffixes), 2 * unit
    )
    return (normed_out, query_grad, key_grad, value_grad)


def solution(mesh):
    spec = P("seq", "tp")
    return jax.shard_map(body, mesh=mesh, in_specs=(spec,) * 4, out_specs=(spec,) * 4, check_vma=False)
```

```python
import functools

import jax
import jax.numpy as jnp
from jax import lax
from jax.experimental import pallas as pl
from jax.experimental.pallas import tpu as pltpu
from jax.sharding import PartitionSpec as P

DH = 128
EPSILON = 1e-06
QUAD = 4
OPS = (0, 1, 2, 3)
CHUNKS = 4
LOW, WIDE = jnp.bfloat16, jnp.float32


def dot(a, b, contract):
    return lax.dot_general(a, b, ((contract[0], contract[1]), ((), ())), preferred_element_type=WIDE)


def head(ref, h):
    return ref.at[:, pl.ds(pl.multiple_of(h * DH, DH), DH)]


def fixed(ref, h):
    return ref.at[:, h * DH : (h + 1) * DH]


def causal_mask(count):
    row = lax.broadcasted_iota(jnp.int32, (count, count), 0)
    col = lax.broadcasted_iota(jnp.int32, (count, count), 1)
    return row >= col


def member_of_quad():
    return lax.axis_index("seq") % QUAD


def sent(op):
    odd = lax.axis_index("tp") % 2
    return (3, 2 - odd, 1 + odd, 0)[op]


def came(op):
    odd = lax.axis_index("tp") % 2
    return (3, 1 + odd, 2 - odd, 0)[op]


def call(kernel, outs, args, flops, in_specs=None, out_specs=None, scratch_shapes=(), room=32):
    size = sum(x.size * x.dtype.itemsize for x in list(args) + list(outs))
    return pl.pallas_call(
        kernel,
        out_shape=outs,
        in_specs=in_specs or [pl.BlockSpec(memory_space=pltpu.VMEM)] * len(args),
        out_specs=out_specs or [pl.BlockSpec(memory_space=pltpu.VMEM)] * len(outs),
        scratch_shapes=scratch_shapes,
        cost_estimate=pl.CostEstimate(flops=flops, bytes_accessed=size, transcendentals=0),
        compiler_params=pltpu.CompilerParams(vmem_limit_bytes=int(room * 1024 * 1024)),
    )(*args)


def state_kernel(k_ref, v_ref, o0, o1, o2, o3, k_buf, v_buf, sems):
    rows = k_ref.shape[0] // CHUNKS
    copies = []
    for i in range(CHUNKS):
        for n, (ref, buf) in enumerate(((k_ref, k_buf), (v_ref, v_buf))):
            part = pl.ds(i * rows, rows)
            copies.append(pltpu.make_async_copy(ref.at[part], buf.at[part], sems.at[n, i]))
            copies[-1].start()
    for copy in copies:
        copy.wait()
    m = member_of_quad()
    for op, out in enumerate((o0, o1, o2, o3)):
        h = m ^ sent(op)
        out[...] = dot(head(k_buf, h)[...], head(v_buf, h)[...], ((0,), (0,))).astype(LOW)


def local_kernel(q_ref, k_ref, v_ref, scores_ref, mixed_ref):
    mask = causal_mask(q_ref.shape[0])
    for h in range(QUAD):
        raw = dot(fixed(q_ref, h)[...], fixed(k_ref, h)[...], ((1,), (1,)))
        scores = jnp.where(mask, raw, 0.0).astype(LOW)
        scores_ref[h] = scores
        fixed(mixed_ref, h)[...] = dot(scores, fixed(v_ref, h)[...], ((1,), (0,)))


def mixed_kernel(local_ref, q_ref, c_ref, p0, p1, p2, p3, mixed_ref, sums_ref):
    m = member_of_quad()
    count = q_ref.shape[0]
    square = jnp.zeros((count, DH), WIDE)
    product = jnp.zeros((count, DH), WIDE)
    for op, p_ref in enumerate((p0, p1, p2, p3)):
        h = m ^ came(op)
        mixed = head(local_ref, h)[...] + dot(head(q_ref, h)[...], p_ref[...], ((1,), (0,)))
        head(mixed_ref, h)[...] = mixed
        square = square + mixed * mixed
        product = product + mixed * head(c_ref, h)[...].astype(WIDE)
    sums_ref[0:1, :] = jnp.sum(square.T, axis=0, keepdims=True)
    sums_ref[1:2, :] = jnp.sum(product.T, axis=0, keepdims=True)


def token_scales(sums_ref, features, count):
    inverse = lax.rsqrt(sums_ref[0:1, :] * (1.0 / features) + EPSILON)
    projection = inverse * sums_ref[1:2, :] * (1.0 / features)
    inverse = jnp.broadcast_to(inverse, (DH, count)).T
    projection = jnp.broadcast_to(projection, (DH, count)).T
    return inverse, projection


def grad_kernel(features, mixed_ref, c_ref, q_ref, sums_ref, o0, o1, o2, o3, g_ref):
    m = member_of_quad()
    inverse, projection = token_scales(sums_ref, features, q_ref.shape[0])
    for op, out in enumerate((o0, o1, o2, o3)):
        h = m ^ sent(op)
        normed = head(mixed_ref, h)[...] * inverse
        grad = (inverse * (head(c_ref, h)[...].astype(WIDE) - normed * projection)).astype(LOW)
        head(g_ref, h)[...] = grad
        out[...] = dot(head(q_ref, h)[...], grad, ((0,), (0,))).astype(LOW)


def back_kernel(features, q_ref, k_ref, v_ref, g_ref, scores_ref, mixed_ref, sums_ref, p0, p1, p2, p3,
                normed_ref, query_ref, key_ref, value_ref):
    m = member_of_quad()
    count = q_ref.shape[0]
    mask = causal_mask(count)
    inverse, _ = token_scales(sums_ref, features, count)
    for op, p_ref in enumerate((p0, p1, p2, p3)):
        h = m ^ came(op)
        grad = head(g_ref, h)[...]
        head(normed_ref, h)[...] = (head(mixed_ref, h)[...] * inverse).astype(LOW)
        raw = dot(grad, head(v_ref, h)[...], ((1,), (1,)))
        coefs = jnp.where(mask, raw, 0.0).astype(LOW)
        query = dot(coefs, head(k_ref, h)[...], ((1,), (0,))) + dot(grad, p_ref[...], ((1,), (1,)))
        head(query_ref, h)[...] = query.astype(LOW)
        head(key_ref, h)[...] = dot(coefs, head(q_ref, h)[...], ((0,), (0,)))
        head(value_ref, h)[...] = dot(scores_ref[h], grad, ((0,), (0,)))


def last_kernel(k_ref, v_ref, key_local, value_local, p0, p1, p2, p3, key_ref, value_ref):
    m = member_of_quad()
    for op, p_ref in enumerate((p0, p1, p2, p3)):
        h = m ^ came(op)
        suffix = p_ref[...]
        key = head(key_local, h)[...] + dot(head(v_ref, h)[...], suffix, ((1,), (1,)))
        head(key_ref, h)[...] = key.astype(LOW)
        value = head(value_local, h)[...] + dot(head(k_ref, h)[...], suffix, ((1,), (0,)))
        head(value_ref, h)[...] = value.astype(LOW)


def sums_kernel(before, far, *refs):
    index = lax.axis_index("seq")
    m = index % QUAD
    held, got, outs = refs[:QUAD], refs[QUAD : QUAD + len(far)], refs[-QUAD:]

    def counts(a, b):
        return jnp.where(a < b if before else a > b, 1.0, 0.0).astype(WIDE)

    outer = jnp.zeros((DH, DH), WIDE)
    for bits, total in zip(far, got):
        outer = outer + total[...].astype(WIDE) * counts(index ^ bits, index)
    pieces = [piece[...].astype(WIDE) for piece in held]
    for to in OPS:
        inner = outer
        for op in OPS:
            inner = inner + pieces[op] * counts(m ^ came(op), m ^ sent(to))
        outs[to][...] = inner.astype(LOW)


def exchange(value, axis, bits):
    size = lax.axis_size(axis)
    return lax.ppermute(value, axis, [(i, i ^ bits) for i in range(size)])


def cross(value, op):
    cores = lax.axis_size("tp")
    places = [(i, t) for i in range(lax.axis_size("seq")) for t in range(cores)]
    bits = (3, 2, 1, 0), (3, 1, 2, 0)
    pairs = [(i * cores + t, (i ^ bits[t % 2][op]) * cores + (t ^ 1)) for i, t in places]
    return lax.ppermute(value, ("seq", "tp"), pairs)


def exclusive_sum(held, before, *after):
    held = [cross(held[op], op) for op in OPS]
    total = sum(piece.astype(WIDE) for piece in held).astype(LOW)
    far = range(lax.axis_size("seq") - QUAD, 0, -QUAD)
    got = [exchange(total, "seq", bits) for bits in far]
    vmem = [pl.BlockSpec(memory_space=pltpu.VMEM)] * (QUAD + len(got))
    sums = call(
        functools.partial(sums_kernel, before, far),
        [jax.ShapeDtypeStruct(x.shape, x.dtype) for x in held],
        (*held, *got, *after),
        0,
        in_specs=vmem + [pl.BlockSpec(memory_space=pl.ANY)] * len(after),
    )
    return [cross(sums[op], op) for op in OPS]


def sum_over_heads(value):
    bit = 1
    while bit < lax.axis_size("tp"):
        value = value + exchange(value, "tp", bit)
        bit *= 2
    return value


def body(q, k, v, c):
    count, width = q.shape
    features = width * lax.axis_size("tp")
    shape = jax.ShapeDtypeStruct
    state = shape((DH, DH), LOW)
    wide = shape((count, width), WIDE)
    low = shape((count, width), LOW)
    unit = 2 * count * DH * DH * QUAD
    buffers = [pltpu.VMEM(k.shape, LOW)] * 2 + [pltpu.SemaphoreType.DMA((2, CHUNKS))]
    held = call(
        state_kernel, [state] * QUAD, (k, v), unit, room=53.75,
        in_specs=[pl.BlockSpec(memory_space=pltpu.HBM)] * 2,
        scratch_shapes=buffers,
    )
    scores, local = call(
        local_kernel, [shape((QUAD, count, count), LOW), wide], (q, k, v), 4 * unit
    )
    prefix = exclusive_sum(held, True)
    mixed, sums = call(
        mixed_kernel, [wide, shape((2, count), WIDE)], (local, q, c, *prefix), unit
    )
    sums = sum_over_heads(sums)
    *terms, g = call(
        functools.partial(grad_kernel, features), [state] * QUAD + [low], (mixed, c, q, sums), unit
    )
    normed_out, query_grad, key_local, value_local = call(
        functools.partial(back_kernel, features),
        [low, low, wide, wide],
        (q, k, v, g, scores, mixed, sums, *prefix),
        9 * unit,
    )
    suffix = exclusive_sum(terms, False, key_local)
    key_grad, value_grad = call(
        last_kernel, [low, low], (k, v, key_local, value_local, *suffix), 2 * unit
    )
    return (normed_out, query_grad, key_grad, value_grad)


def solution(mesh):
    spec = P("seq", "tp")
    return jax.shard_map(body, mesh=mesh, in_specs=(spec,) * 4, out_specs=(spec,) * 4, check_vma=False)
```

```python
import functools

import jax
import jax.numpy as jnp
from jax import lax
from jax.experimental import pallas as pl
from jax.experimental.pallas import tpu as pltpu
from jax.sharding import PartitionSpec as P

DH = 128
EPSILON = 1e-06
QUAD = 4
OPS = (0, 1, 2, 3)
CHUNKS = 4
LOW, WIDE = jnp.bfloat16, jnp.float32


def dot(a, b, contract):
    return lax.dot_general(a, b, ((contract[0], contract[1]), ((), ())), preferred_element_type=WIDE)


def head(ref, h):
    return ref.at[:, pl.ds(pl.multiple_of(h * DH, DH), DH)]


def fixed(ref, h):
    return ref.at[:, h * DH : (h + 1) * DH]


def causal_mask(count):
    row = lax.broadcasted_iota(jnp.int32, (count, count), 0)
    col = lax.broadcasted_iota(jnp.int32, (count, count), 1)
    return row >= col


def member_of_quad():
    return lax.axis_index("seq") % QUAD


def sent(op):
    odd = lax.axis_index("tp") % 2
    return (3, 2 - odd, 1 + odd, 0)[op]


def came(op):
    odd = lax.axis_index("tp") % 2
    return (3, 1 + odd, 2 - odd, 0)[op]


def call(kernel, outs, args, flops, in_specs=None, out_specs=None, scratch_shapes=(), room=32):
    size = sum(x.size * x.dtype.itemsize for x in list(args) + list(outs))
    return pl.pallas_call(
        kernel,
        out_shape=outs,
        in_specs=in_specs or [pl.BlockSpec(memory_space=pltpu.VMEM)] * len(args),
        out_specs=out_specs or [pl.BlockSpec(memory_space=pltpu.VMEM)] * len(outs),
        scratch_shapes=scratch_shapes,
        cost_estimate=pl.CostEstimate(flops=flops, bytes_accessed=size, transcendentals=0),
        compiler_params=pltpu.CompilerParams(vmem_limit_bytes=int(room * 1024 * 1024)),
    )(*args)


def state_kernel(k_ref, v_ref, o0, o1, o2, o3, k_buf, v_buf, sems):
    rows = k_ref.shape[0] // CHUNKS
    copies = []
    for i in range(CHUNKS):
        for n, (ref, buf) in enumerate(((k_ref, k_buf), (v_ref, v_buf))):
            part = pl.ds(i * rows, rows)
            copies.append(pltpu.make_async_copy(ref.at[part], buf.at[part], sems.at[n, i]))
            copies[-1].start()
    m = member_of_quad()
    states = [0.0] * QUAD
    half = rows * CHUNKS // 2
    for part in range(2):
        for copy in copies[part * CHUNKS : (part + 1) * CHUNKS]:
            copy.wait()
        tokens = pl.ds(part * half, half)
        for op in OPS:
            cols = pl.ds(pl.multiple_of((m ^ sent(op)) * DH, DH), DH)
            states[op] = states[op] + dot(k_buf[tokens, cols], v_buf[tokens, cols], ((0,), (0,)))
    for op, out in enumerate((o0, o1, o2, o3)):
        out[...] = states[op].astype(LOW)


def local_kernel(q_ref, k_ref, v_ref, scores_ref, mixed_ref):
    mask = causal_mask(q_ref.shape[0])
    for h in range(QUAD):
        raw = dot(fixed(q_ref, h)[...], fixed(k_ref, h)[...], ((1,), (1,)))
        scores = jnp.where(mask, raw, 0.0).astype(LOW)
        scores_ref[h] = scores
        fixed(mixed_ref, h)[...] = dot(scores, fixed(v_ref, h)[...], ((1,), (0,)))


def mixed_kernel(local_ref, q_ref, c_ref, p0, p1, p2, p3, mixed_ref, sums_ref):
    m = member_of_quad()
    count = q_ref.shape[0]
    square = jnp.zeros((count, DH), WIDE)
    product = jnp.zeros((count, DH), WIDE)
    for op, p_ref in enumerate((p0, p1, p2, p3)):
        h = m ^ came(op)
        mixed = head(local_ref, h)[...] + dot(head(q_ref, h)[...], p_ref[...], ((1,), (0,)))
        head(mixed_ref, h)[...] = mixed
        square = square + mixed * mixed
        product = product + mixed * head(c_ref, h)[...].astype(WIDE)
    sums_ref[0:1, :] = jnp.sum(square.T, axis=0, keepdims=True)
    sums_ref[1:2, :] = jnp.sum(product.T, axis=0, keepdims=True)


def token_scales(sums_ref, features, count):
    inverse = lax.rsqrt(sums_ref[0:1, :] * (1.0 / features) + EPSILON)
    projection = inverse * sums_ref[1:2, :] * (1.0 / features)
    inverse = jnp.broadcast_to(inverse, (DH, count)).T
    projection = jnp.broadcast_to(projection, (DH, count)).T
    return inverse, projection


def grad_kernel(features, mixed_ref, c_ref, q_ref, sums_ref, o0, o1, o2, o3, g_ref):
    m = member_of_quad()
    inverse, projection = token_scales(sums_ref, features, q_ref.shape[0])
    for op, out in enumerate((o0, o1, o2, o3)):
        h = m ^ sent(op)
        normed = head(mixed_ref, h)[...] * inverse
        grad = (inverse * (head(c_ref, h)[...].astype(WIDE) - normed * projection)).astype(LOW)
        head(g_ref, h)[...] = grad
        out[...] = dot(head(q_ref, h)[...], grad, ((0,), (0,))).astype(LOW)


def back_kernel(features, q_ref, k_ref, v_ref, g_ref, scores_ref, mixed_ref, sums_ref, p0, p1, p2, p3,
                normed_ref, query_ref, key_ref, value_ref):
    m = member_of_quad()
    count = q_ref.shape[0]
    mask = causal_mask(count)
    inverse, _ = token_scales(sums_ref, features, count)
    for op, p_ref in enumerate((p0, p1, p2, p3)):
        h = m ^ came(op)
        grad = head(g_ref, h)[...]
        head(normed_ref, h)[...] = (head(mixed_ref, h)[...] * inverse).astype(LOW)
        raw = dot(grad, head(v_ref, h)[...], ((1,), (1,)))
        coefs = jnp.where(mask, raw, 0.0).astype(LOW)
        query = dot(coefs, head(k_ref, h)[...], ((1,), (0,))) + dot(grad, p_ref[...], ((1,), (1,)))
        head(query_ref, h)[...] = query.astype(LOW)
        head(key_ref, h)[...] = dot(coefs, head(q_ref, h)[...], ((0,), (0,)))
        head(value_ref, h)[...] = dot(scores_ref[h], grad, ((0,), (0,)))


def last_kernel(k_ref, v_ref, key_local, value_local, p0, p1, p2, p3, key_ref, value_ref):
    m = member_of_quad()
    for op, p_ref in enumerate((p0, p1, p2, p3)):
        h = m ^ came(op)
        suffix = p_ref[...]
        key = head(key_local, h)[...] + dot(head(v_ref, h)[...], suffix, ((1,), (1,)))
        head(key_ref, h)[...] = key.astype(LOW)
        value = head(value_local, h)[...] + dot(head(k_ref, h)[...], suffix, ((1,), (0,)))
        head(value_ref, h)[...] = value.astype(LOW)


def quad_targets(quads, step, before):
    targets = [z ^ step for z in range(quads)]
    if quads == 4 and step == 3:
        targets = [3, 2, 0, 1] if before else [2, 3, 1, 0]
    return targets


def sums_kernel(before, quads, *refs):
    index = lax.axis_index("seq")
    m, quad = index % QUAD, index // QUAD
    held, got, outs = refs[:QUAD], refs[QUAD : QUAD + quads - 1], refs[-QUAD:]

    def counts(a, b):
        return jnp.where(a < b if before else a > b, 1.0, 0.0).astype(WIDE)

    outer = jnp.zeros((DH, DH), WIDE)
    for step, total in zip(range(quads - 1, 0, -1), got):
        outer = outer + total[...].astype(WIDE) * counts(quad ^ step, quad)
    pieces = [piece[...].astype(WIDE) for piece in held]
    for to in OPS:
        inner = outer
        for op in OPS:
            inner = inner + pieces[op] * counts(m ^ came(op), m ^ sent(to))
        outs[to][...] = inner.astype(LOW)


def exchange(value, axis, bits):
    size = lax.axis_size(axis)
    return lax.ppermute(value, axis, [(i, i ^ bits) for i in range(size)])


def cross(value, op):
    cores = lax.axis_size("tp")
    places = [(i, t) for i in range(lax.axis_size("seq")) for t in range(cores)]
    bits = (3, 2, 1, 0), (3, 1, 2, 0)
    pairs = [(i * cores + t, (i ^ bits[t % 2][op]) * cores + (t ^ 1)) for i, t in places]
    return lax.ppermute(value, ("seq", "tp"), pairs)


def exclusive_sum(held, before, *after):
    held = [cross(held[op], op) for op in OPS]
    total = sum(piece.astype(WIDE) for piece in held).astype(LOW)
    quads = lax.axis_size("seq") // QUAD
    got = []
    for step in range(quads - 1, 0, -1):
        targets = quad_targets(quads, step, before)
        pairs = [(z * QUAD + i, targets[z] * QUAD + i) for z in range(quads) for i in range(QUAD)]
        got.append(lax.ppermute(total, "seq", pairs))
    vmem = [pl.BlockSpec(memory_space=pltpu.VMEM)] * (QUAD + len(got))
    sums = call(
        functools.partial(sums_kernel, before, quads),
        [jax.ShapeDtypeStruct(x.shape, x.dtype) for x in held],
        (*held, *got, *after),
        0,
        in_specs=vmem + [pl.BlockSpec(memory_space=pl.ANY)] * len(after),
    )
    return [cross(sums[op], op) for op in OPS]


def sum_over_heads(value):
    bit = 1
    while bit < lax.axis_size("tp"):
        value = value + exchange(value, "tp", bit)
        bit *= 2
    return value


def body(q, k, v, c):
    count, width = q.shape
    features = width * lax.axis_size("tp")
    shape = jax.ShapeDtypeStruct
    state = shape((DH, DH), LOW)
    wide = shape((count, width), WIDE)
    low = shape((count, width), LOW)
    unit = 2 * count * DH * DH * QUAD
    buffers = [pltpu.VMEM(k.shape, LOW)] * 2 + [pltpu.SemaphoreType.DMA((2, CHUNKS))]
    held = call(
        state_kernel, [state] * QUAD, (k, v), unit, room=53.75,
        in_specs=[pl.BlockSpec(memory_space=pltpu.HBM)] * 2,
        scratch_shapes=buffers,
    )
    scores, local = call(
        local_kernel, [shape((QUAD, count, count), LOW), wide], (q, k, v), 4 * unit
    )
    prefix = exclusive_sum(held, True)
    mixed, sums = call(
        mixed_kernel, [wide, shape((2, count), WIDE)], (local, q, c, *prefix), unit
    )
    sums = sum_over_heads(sums)
    *terms, g = call(
        functools.partial(grad_kernel, features), [state] * QUAD + [low], (mixed, c, q, sums), unit
    )
    normed_out, query_grad, key_local, value_local = call(
        functools.partial(back_kernel, features),
        [low, low, wide, wide],
        (q, k, v, g, scores, mixed, sums, *prefix),
        9 * unit,
    )
    suffix = exclusive_sum(terms, False, key_local)
    key_grad, value_grad = call(
        last_kernel, [low, low], (k, v, key_local, value_local, *suffix), 2 * unit
    )
    return (normed_out, query_grad, key_grad, value_grad)


def solution(mesh):
    spec = P("seq", "tp")
    return jax.shard_map(body, mesh=mesh, in_specs=(spec,) * 4, out_specs=(spec,) * 4, check_vma=False)
```

```python
import functools

import jax
import jax.numpy as jnp
from jax import lax
from jax.experimental import pallas as pl
from jax.experimental.pallas import tpu as pltpu
from jax.sharding import PartitionSpec as P

DH = 128
EPSILON = 1e-06
QUAD = 4
OPS = (0, 1, 2, 3)
BACK = (3, 2, 1, 0)
CHUNKS = 4
LOW, WIDE = jnp.bfloat16, jnp.float32


def dot(a, b, contract):
    return lax.dot_general(a, b, ((contract[0], contract[1]), ((), ())), preferred_element_type=WIDE)


def head(ref, h):
    return ref.at[:, pl.ds(pl.multiple_of(h * DH, DH), DH)]


def fixed(ref, h):
    return ref.at[:, h * DH : (h + 1) * DH]


def causal_mask(count):
    row = lax.broadcasted_iota(jnp.int32, (count, count), 0)
    col = lax.broadcasted_iota(jnp.int32, (count, count), 1)
    return row >= col


def member_of_quad():
    return lax.axis_index("seq") % QUAD


def sent(op):
    odd = lax.axis_index("tp") % 2
    return (3, 2 - odd, 1 + odd, 0)[op]


def call(kernel, outs, args, flops, in_specs=None, out_specs=None, scratch_shapes=(), room=32):
    size = sum(x.size * x.dtype.itemsize for x in list(args) + list(outs))
    return pl.pallas_call(
        kernel,
        out_shape=outs,
        in_specs=in_specs or [pl.BlockSpec(memory_space=pltpu.VMEM)] * len(args),
        out_specs=out_specs or [pl.BlockSpec(memory_space=pltpu.VMEM)] * len(outs),
        scratch_shapes=scratch_shapes,
        cost_estimate=pl.CostEstimate(flops=flops, bytes_accessed=size, transcendentals=0),
        compiler_params=pltpu.CompilerParams(vmem_limit_bytes=int(room * 1024 * 1024)),
    )(*args)


def state_kernel(k_ref, v_ref, o0, o1, o2, o3, k_buf, v_buf, sems):
    rows = k_ref.shape[0] // CHUNKS
    copies = []
    for i in range(CHUNKS):
        for n, (ref, buf) in enumerate(((k_ref, k_buf), (v_ref, v_buf))):
            part = pl.ds(i * rows, rows)
            copies.append(pltpu.make_async_copy(ref.at[part], buf.at[part], sems.at[n, i]))
            copies[-1].start()
    m = member_of_quad()
    states = [0.0] * QUAD
    half = rows * CHUNKS // 2
    for part in range(2):
        for copy in copies[part * CHUNKS : (part + 1) * CHUNKS]:
            copy.wait()
        tokens = pl.ds(part * half, half)
        for op in OPS:
            cols = pl.ds(pl.multiple_of((m ^ sent(op)) * DH, DH), DH)
            states[op] = states[op] + dot(k_buf[tokens, cols], v_buf[tokens, cols], ((0,), (0,)))
    for op, out in enumerate((o0, o1, o2, o3)):
        out[...] = states[op].astype(LOW)


def local_kernel(q_ref, k_ref, v_ref, scores_ref, mixed_ref):
    mask = causal_mask(q_ref.shape[0])
    for h in range(QUAD):
        raw = dot(fixed(q_ref, h)[...], fixed(k_ref, h)[...], ((1,), (1,)))
        scores = jnp.where(mask, raw, 0.0).astype(LOW)
        scores_ref[h] = scores
        fixed(mixed_ref, h)[...] = dot(scores, fixed(v_ref, h)[...], ((1,), (0,)))


def mixed_kernel(local_ref, q_ref, c_ref, p3, p2, p1, p0, mixed_ref, sums_ref):
    m = member_of_quad()
    count = q_ref.shape[0]
    square = jnp.zeros((count, DH), WIDE)
    product = jnp.zeros((count, DH), WIDE)
    for d, p_ref in zip(BACK, (p3, p2, p1, p0)):
        h = m ^ d
        mixed = head(local_ref, h)[...] + dot(head(q_ref, h)[...], p_ref[...], ((1,), (0,)))
        head(mixed_ref, h)[...] = mixed
        square = square + mixed * mixed
        product = product + mixed * head(c_ref, h)[...].astype(WIDE)
    sums_ref[0:1, :] = jnp.sum(square.T, axis=0, keepdims=True)
    sums_ref[1:2, :] = jnp.sum(product.T, axis=0, keepdims=True)


def token_scales(sums_ref, features, count):
    inverse = lax.rsqrt(sums_ref[0:1, :] * (1.0 / features) + EPSILON)
    projection = inverse * sums_ref[1:2, :] * (1.0 / features)
    inverse = jnp.broadcast_to(inverse, (DH, count)).T
    projection = jnp.broadcast_to(projection, (DH, count)).T
    return inverse, projection


def grad_kernel(features, mixed_ref, c_ref, q_ref, sums_ref, o0, o1, o2, o3, g_ref):
    m = member_of_quad()
    inverse, projection = token_scales(sums_ref, features, q_ref.shape[0])
    for op, out in enumerate((o0, o1, o2, o3)):
        h = m ^ sent(op)
        normed = head(mixed_ref, h)[...] * inverse
        grad = (inverse * (head(c_ref, h)[...].astype(WIDE) - normed * projection)).astype(LOW)
        head(g_ref, h)[...] = grad
        out[...] = dot(head(q_ref, h)[...], grad, ((0,), (0,))).astype(LOW)


def back_kernel(features, q_ref, k_ref, v_ref, g_ref, scores_ref, mixed_ref, sums_ref, p3, p2, p1, p0,
                normed_ref, query_ref, key_ref, value_ref):
    m = member_of_quad()
    count = q_ref.shape[0]
    mask = causal_mask(count)
    inverse, _ = token_scales(sums_ref, features, count)
    for d, p_ref in zip(BACK, (p3, p2, p1, p0)):
        h = m ^ d
        grad = head(g_ref, h)[...]
        head(normed_ref, h)[...] = (head(mixed_ref, h)[...] * inverse).astype(LOW)
        raw = dot(grad, head(v_ref, h)[...], ((1,), (1,)))
        coefs = jnp.where(mask, raw, 0.0).astype(LOW)
        query = dot(coefs, head(k_ref, h)[...], ((1,), (0,))) + dot(grad, p_ref[...], ((1,), (1,)))
        head(query_ref, h)[...] = query.astype(LOW)
        head(key_ref, h)[...] = dot(coefs, head(q_ref, h)[...], ((0,), (0,)))
        head(value_ref, h)[...] = dot(scores_ref[h], grad, ((0,), (0,)))


def last_kernel(k_ref, v_ref, key_local, value_local, p3, p2, p1, p0, key_ref, value_ref):
    m = member_of_quad()
    for d, p_ref in zip(BACK, (p3, p2, p1, p0)):
        h = m ^ d
        suffix = p_ref[...]
        key = head(key_local, h)[...] + dot(head(v_ref, h)[...], suffix, ((1,), (1,)))
        head(key_ref, h)[...] = key.astype(LOW)
        value = head(value_local, h)[...] + dot(head(k_ref, h)[...], suffix, ((1,), (0,)))
        head(value_ref, h)[...] = value.astype(LOW)


def quad_targets(quads, step, before):
    targets = [z ^ step for z in range(quads)]
    if quads == 4 and step == 3:
        targets = [3, 2, 0, 1] if before else [2, 3, 1, 0]
    return targets


def sums_kernel(before, quads, *refs):
    index = lax.axis_index("seq")
    m, quad = index % QUAD, index // QUAD
    got, held, outs = refs[: quads - 1], refs[quads - 1], refs[-QUAD:]

    def counts(a, b):
        return jnp.where(a < b if before else a > b, 1.0, 0.0).astype(WIDE)

    outer = jnp.zeros((DH, DH), WIDE)
    for step, total in zip(range(quads - 1, 0, -1), got):
        outer = outer + total[...].astype(WIDE) * counts(quad ^ step, quad)
    pieces = [held[op].astype(WIDE) for op in OPS]
    for out, to in zip(outs, BACK):
        inner = outer
        for op in OPS:
            inner = inner + pieces[op] * counts(m ^ sent(op), m ^ to)
        out[...] = inner.astype(LOW)


def total_kernel(*refs):
    total_ref, stack_ref = refs[QUAD:]
    total = jnp.zeros((DH, DH), WIDE)
    for n, ref in enumerate(refs[:QUAD]):
        stack_ref[n] = ref[...]
        total = total + ref[...].astype(WIDE)
    total_ref[...] = total.astype(LOW)


def exchange(value, axis, bits):
    size = lax.axis_size(axis)
    return lax.ppermute(value, axis, [(i, i ^ bits) for i in range(size)])


def cross(value, op):
    cores = lax.axis_size("tp")
    places = [(i, t) for i in range(lax.axis_size("seq")) for t in range(cores)]
    bits = (3, 2, 1, 0), (3, 1, 2, 0)
    pairs = [(i * cores + t, (i ^ bits[t % 2][op]) * cores + (t ^ 1)) for i, t in places]
    return lax.ppermute(value, ("seq", "tp"), pairs)


def exclusive_sum(held, before, *after):
    held = [cross(held[op], op) for op in OPS]
    state = jax.ShapeDtypeStruct((DH, DH), LOW)
    total, held = call(total_kernel, [state, jax.ShapeDtypeStruct((QUAD, DH, DH), LOW)], held, 0)
    quads, cores = lax.axis_size("seq") // QUAD, lax.axis_size("tp")
    got = []
    for step in range(quads - 1, 0, -1):
        targets = quad_targets(quads, step, before)
        places = [(z, i, t) for z in range(quads) for i in range(QUAD) for t in range(cores)]
        pairs = [((z * QUAD + i) * cores + t, (targets[z] * QUAD + i) * cores + (t ^ 1)) for z, i, t in places]
        got.append(lax.ppermute(total, ("seq", "tp"), pairs))
    held = exchange(held, "tp", 1)
    sums = call(
        functools.partial(sums_kernel, before, quads),
        [state] * QUAD,
        (*got, held, *after),
        0,
        in_specs=[pl.BlockSpec(memory_space=pltpu.VMEM)] * quads + [pl.BlockSpec(memory_space=pl.ANY)] * len(after),
    )
    return [exchange(x, "seq", d) for x, d in zip(sums, BACK) if d] + [sums[-1]]


def sum_over_heads(value):
    bit = 1
    while bit < lax.axis_size("tp"):
        value = value + exchange(value, "tp", bit)
        bit *= 2
    return value


def body(q, k, v, c):
    count, width = q.shape
    features = width * lax.axis_size("tp")
    shape = jax.ShapeDtypeStruct
    state = shape((DH, DH), LOW)
    wide = shape((count, width), WIDE)
    low = shape((count, width), LOW)
    unit = 2 * count * DH * DH * QUAD
    buffers = [pltpu.VMEM(k.shape, LOW)] * 2 + [pltpu.SemaphoreType.DMA((2, CHUNKS))]
    held = call(
        state_kernel, [state] * QUAD, (k, v), unit, room=53.75,
        in_specs=[pl.BlockSpec(memory_space=pltpu.HBM)] * 2,
        scratch_shapes=buffers,
    )
    scores, local = call(
        local_kernel, [shape((QUAD, count, count), LOW), wide], (q, k, v), 4 * unit
    )
    prefix = exclusive_sum(held, True)
    mixed, sums = call(
        mixed_kernel, [wide, shape((2, count), WIDE)], (local, q, c, *prefix), unit
    )
    sums = sum_over_heads(sums)
    *terms, g = call(
        functools.partial(grad_kernel, features), [state] * QUAD + [low], (mixed, c, q, sums), unit
    )
    normed_out, query_grad, key_local, value_local = call(
        functools.partial(back_kernel, features),
        [low, low, wide, wide],
        (q, k, v, g, scores, mixed, sums, *prefix),
        9 * unit,
    )
    suffix = exclusive_sum(terms, False, key_local)
    key_grad, value_grad = call(
        last_kernel, [low, low], (k, v, key_local, value_local, *suffix), 2 * unit
    )
    return (normed_out, query_grad, key_grad, value_grad)


def solution(mesh):
    spec = P("seq", "tp")
    return jax.shard_map(body, mesh=mesh, in_specs=(spec,) * 4, out_specs=(spec,) * 4, check_vma=False)
```

```python
import functools

import jax
import jax.numpy as jnp
from jax import lax
from jax.experimental import pallas as pl
from jax.experimental.pallas import tpu as pltpu
from jax.sharding import PartitionSpec as P

DH = 128
EPSILON = 1e-06
QUAD = 4
OPS = (0, 1, 2, 3)
CHUNKS = 4
LOW, WIDE = jnp.bfloat16, jnp.float32


def dot(a, b, contract):
    return lax.dot_general(a, b, ((contract[0], contract[1]), ((), ())), preferred_element_type=WIDE)


def head(ref, h):
    return ref.at[:, pl.ds(pl.multiple_of(h * DH, DH), DH)]


def fixed(ref, h):
    return ref.at[:, h * DH : (h + 1) * DH]


def causal_mask(count):
    row = lax.broadcasted_iota(jnp.int32, (count, count), 0)
    col = lax.broadcasted_iota(jnp.int32, (count, count), 1)
    return row >= col


def member_of_quad():
    return lax.axis_index("seq") % QUAD


def sent(op):
    odd = lax.axis_index("tp") % 2
    return (3, 2 - odd, 1 + odd, 0)[op]


def came(op):
    odd = lax.axis_index("tp") % 2
    return (3, 1 + odd, 2 - odd, 0)[op]


def call(kernel, outs, args, flops, in_specs=None, out_specs=None, scratch_shapes=(), room=32):
    size = sum(x.size * x.dtype.itemsize for x in list(args) + list(outs))
    return pl.pallas_call(
        kernel,
        out_shape=outs,
        in_specs=in_specs or [pl.BlockSpec(memory_space=pltpu.VMEM)] * len(args),
        out_specs=out_specs or [pl.BlockSpec(memory_space=pltpu.VMEM)] * len(outs),
        scratch_shapes=scratch_shapes,
        cost_estimate=pl.CostEstimate(flops=flops, bytes_accessed=size, transcendentals=0),
        compiler_params=pltpu.CompilerParams(vmem_limit_bytes=int(room * 1024 * 1024)),
    )(*args)


def state_kernel(k_ref, v_ref, o0, o1, o2, o3, k_buf, v_buf, sems):
    rows = k_ref.shape[0] // CHUNKS
    copies = []
    for i in range(CHUNKS):
        for n, (ref, buf) in enumerate(((k_ref, k_buf), (v_ref, v_buf))):
            part = pl.ds(i * rows, rows)
            copies.append(pltpu.make_async_copy(ref.at[part], buf.at[part], sems.at[n, i]))
            copies[-1].start()
    m = member_of_quad()
    states = [0.0] * QUAD
    half = rows * CHUNKS // 2
    for part in range(2):
        for copy in copies[part * CHUNKS : (part + 1) * CHUNKS]:
            copy.wait()
        tokens = pl.ds(part * half, half)
        for op in OPS:
            cols = pl.ds(pl.multiple_of((m ^ sent(op)) * DH, DH), DH)
            states[op] = states[op] + dot(k_buf[tokens, cols], v_buf[tokens, cols], ((0,), (0,)))
    for op, out in enumerate((o0, o1, o2, o3)):
        out[...] = states[op].astype(LOW)


def local_kernel(q_ref, k_ref, v_ref, scores_ref, mixed_ref):
    mask = causal_mask(q_ref.shape[0])
    for h in range(QUAD):
        raw = dot(fixed(q_ref, h)[...], fixed(k_ref, h)[...], ((1,), (1,)))
        scores = jnp.where(mask, raw, 0.0).astype(LOW)
        scores_ref[h] = scores
        fixed(mixed_ref, h)[...] = dot(scores, fixed(v_ref, h)[...], ((1,), (0,)))


def mixed_kernel(local_ref, q_ref, c_ref, p0, p1, p2, p3, mixed_ref, sums_ref):
    m = member_of_quad()
    count = q_ref.shape[0]
    square = jnp.zeros((count, DH), WIDE)
    product = jnp.zeros((count, DH), WIDE)
    for op, p_ref in enumerate((p0, p1, p2, p3)):
        h = m ^ came(op)
        mixed = head(local_ref, h)[...] + dot(head(q_ref, h)[...], p_ref[...], ((1,), (0,)))
        head(mixed_ref, h)[...] = mixed
        square = square + mixed * mixed
        product = product + mixed * head(c_ref, h)[...].astype(WIDE)
    sums_ref[0:1, :] = jnp.sum(square.T, axis=0, keepdims=True)
    sums_ref[1:2, :] = jnp.sum(product.T, axis=0, keepdims=True)


def token_scales(sums_ref, features, count):
    inverse = lax.rsqrt(sums_ref[0:1, :] * (1.0 / features) + EPSILON)
    projection = inverse * sums_ref[1:2, :] * (1.0 / features)
    inverse = jnp.broadcast_to(inverse, (DH, count)).T
    projection = jnp.broadcast_to(projection, (DH, count)).T
    return inverse, projection


def grad_kernel(features, mixed_ref, c_ref, q_ref, sums_ref, o0, o1, o2, o3, g_ref):
    m = member_of_quad()
    inverse, projection = token_scales(sums_ref, features, q_ref.shape[0])
    for op, out in enumerate((o0, o1, o2, o3)):
        h = m ^ sent(op)
        normed = head(mixed_ref, h)[...] * inverse
        grad = (inverse * (head(c_ref, h)[...].astype(WIDE) - normed * projection)).astype(LOW)
        head(g_ref, h)[...] = grad
        out[...] = dot(head(q_ref, h)[...], grad, ((0,), (0,))).astype(LOW)


def back_kernel(features, q_ref, k_ref, v_ref, g_ref, scores_ref, mixed_ref, sums_ref, p0, p1, p2, p3,
                normed_ref, query_ref, key_ref, value_ref):
    m = member_of_quad()
    count = q_ref.shape[0]
    mask = causal_mask(count)
    inverse, _ = token_scales(sums_ref, features, count)
    for op, p_ref in enumerate((p0, p1, p2, p3)):
        h = m ^ came(op)
        grad = head(g_ref, h)[...]
        head(normed_ref, h)[...] = (head(mixed_ref, h)[...] * inverse).astype(LOW)
        raw = dot(grad, head(v_ref, h)[...], ((1,), (1,)))
        coefs = jnp.where(mask, raw, 0.0).astype(LOW)
        query = dot(coefs, head(k_ref, h)[...], ((1,), (0,))) + dot(grad, p_ref[...], ((1,), (1,)))
        head(query_ref, h)[...] = query.astype(LOW)
        head(key_ref, h)[...] = dot(coefs, head(q_ref, h)[...], ((0,), (0,)))
        head(value_ref, h)[...] = dot(scores_ref[h], grad, ((0,), (0,)))


def last_kernel(k_ref, v_ref, key_local, value_local, p0, p1, p2, p3, key_ref, value_ref, key_buf, value_buf, sems):
    m = member_of_quad()
    rows = k_ref.shape[0] // CHUNKS
    copies = []
    parts = (key_local, v_ref, 1, key_buf, key_ref), (value_local, k_ref, 0, value_buf, value_ref)
    for n, (local, other, side, buf, out) in enumerate(parts):
        for op, p_ref in enumerate((p0, p1, p2, p3)):
            h = m ^ came(op)
            total = head(local, h)[...] + dot(head(other, h)[...], p_ref[...], ((1,), (side,)))
            head(buf, h)[...] = total.astype(LOW)
        for i in range(CHUNKS):
            part = pl.ds(i * rows, rows)
            copies.append(pltpu.make_async_copy(buf.at[part], out.at[part], sems.at[n, i]))
            copies[-1].start()
    for copy in copies:
        copy.wait()


def quad_steps(quads, before):
    return (2, 3, 1) if quads == 4 and before else range(quads - 1, 0, -1)


def quad_targets(quads, step, before):
    targets = [z ^ step for z in range(quads)]
    if quads == 4 and step == 3:
        targets = [3, 2, 0, 1] if before else [2, 3, 1, 0]
    return targets


def sums_kernel(before, quads, *refs):
    index = lax.axis_index("seq")
    m, quad = index % QUAD, index // QUAD
    held, got, outs = refs[:QUAD], refs[QUAD : QUAD + quads - 1], refs[-QUAD:]

    def counts(a, b):
        return jnp.where(a < b if before else a > b, 1.0, 0.0).astype(WIDE)

    outer = jnp.zeros((DH, DH), WIDE)
    for step, total in zip(quad_steps(quads, before), got):
        outer = outer + total[...].astype(WIDE) * counts(quad ^ step, quad)
    pieces = [piece[...].astype(WIDE) for piece in held]
    for to in OPS:
        inner = outer
        for op in OPS:
            inner = inner + pieces[op] * counts(m ^ came(op), m ^ sent(to))
        outs[to][...] = inner.astype(LOW)


def exchange(value, axis, bits):
    size = lax.axis_size(axis)
    return lax.ppermute(value, axis, [(i, i ^ bits) for i in range(size)])


def cross(value, op):
    cores = lax.axis_size("tp")
    places = [(i, t) for i in range(lax.axis_size("seq")) for t in range(cores)]
    bits = (3, 2, 1, 0), (3, 1, 2, 0)
    pairs = [(i * cores + t, (i ^ bits[t % 2][op]) * cores + (t ^ 1)) for i, t in places]
    return lax.ppermute(value, ("seq", "tp"), pairs)


def exclusive_sum(held, before, *after):
    held = [cross(held[op], op) for op in OPS]
    total = sum(piece.astype(WIDE) for piece in held).astype(LOW)
    quads = lax.axis_size("seq") // QUAD
    got = []
    for step in quad_steps(quads, before):
        targets = quad_targets(quads, step, before)
        pairs = [(z * QUAD + i, targets[z] * QUAD + i) for z in range(quads) for i in range(QUAD)]
        got.append(lax.ppermute(total, "seq", pairs))
    vmem = [pl.BlockSpec(memory_space=pltpu.VMEM)] * (QUAD + len(got))
    sums = call(
        functools.partial(sums_kernel, before, quads),
        [jax.ShapeDtypeStruct(x.shape, x.dtype) for x in held],
        (*held, *got, *after),
        0,
        in_specs=vmem + [pl.BlockSpec(memory_space=pl.ANY)] * len(after),
    )
    return [cross(sums[op], op) for op in OPS]


def sum_over_heads(value):
    bit = 1
    while bit < lax.axis_size("tp"):
        value = value + exchange(value, "tp", bit)
        bit *= 2
    return value


def body(q, k, v, c):
    count, width = q.shape
    features = width * lax.axis_size("tp")
    shape = jax.ShapeDtypeStruct
    state = shape((DH, DH), LOW)
    wide = shape((count, width), WIDE)
    low = shape((count, width), LOW)
    unit = 2 * count * DH * DH * QUAD
    buffers = [pltpu.VMEM(k.shape, LOW)] * 2 + [pltpu.SemaphoreType.DMA((2, CHUNKS))]
    held = call(
        state_kernel, [state] * QUAD, (k, v), unit, room=53.75,
        in_specs=[pl.BlockSpec(memory_space=pltpu.HBM)] * 2,
        scratch_shapes=buffers,
    )
    scores, local = call(
        local_kernel, [shape((QUAD, count, count), LOW), wide], (q, k, v), 4 * unit
    )
    prefix = exclusive_sum(held, True)
    mixed, sums = call(
        mixed_kernel, [wide, shape((2, count), WIDE)], (local, q, c, *prefix), unit
    )
    sums = sum_over_heads(sums)
    *terms, g = call(
        functools.partial(grad_kernel, features), [state] * QUAD + [low], (mixed, c, q, sums), unit
    )
    normed_out, query_grad, key_local, value_local = call(
        functools.partial(back_kernel, features),
        [low, low, wide, wide],
        (q, k, v, g, scores, mixed, sums, *prefix),
        9 * unit,
    )
    suffix = exclusive_sum(terms, False, key_local)
    key_grad, value_grad = call(
        last_kernel, [low, low], (k, v, key_local, value_local, *suffix), 2 * unit,
        out_specs=[pl.BlockSpec(memory_space=pltpu.HBM)] * 2,
        scratch_shapes=buffers,
    )
    return (normed_out, query_grad, key_grad, value_grad)


def solution(mesh):
    spec = P("seq", "tp")
    return jax.shard_map(body, mesh=mesh, in_specs=(spec,) * 4, out_specs=(spec,) * 4, check_vma=False)
```

```python
import functools

import jax
import jax.numpy as jnp
from jax import lax
from jax.experimental import pallas as pl
from jax.experimental.pallas import tpu as pltpu
from jax.sharding import PartitionSpec as P

DH = 128
EPSILON = 1e-06
QUAD = 4
OPS = (0, 1, 2, 3)
CHUNKS = 4
LOW, WIDE = jnp.bfloat16, jnp.float32


def dot(a, b, contract):
    return lax.dot_general(a, b, ((contract[0], contract[1]), ((), ())), preferred_element_type=WIDE)


def head(ref, h):
    return ref.at[:, pl.ds(pl.multiple_of(h * DH, DH), DH)]


def fixed(ref, h):
    return ref.at[:, h * DH : (h + 1) * DH]


def causal_mask(count):
    row = lax.broadcasted_iota(jnp.int32, (count, count), 0)
    col = lax.broadcasted_iota(jnp.int32, (count, count), 1)
    return row >= col


def member_of_quad():
    return lax.axis_index("seq") % QUAD


FIRST = (((3, 2, 1, 0), (1, 3, 0, 2), (2, 0, 3, 1)), ((2, 3, 1, 0), (3, 2, 0, 1), (1, 0, 3, 2)))
BACK = (((3, 2, 1, 0), (2, 3, 0, 1), (1, 0, 3, 2)), ((3, 2, 0, 1), (2, 3, 1, 0), (1, 0, 3, 2)))
FIRST_GRAD = (((3, 2, 1, 0), (2, 3, 0, 1), (1, 0, 3, 2)), ((3, 2, 1, 0), (1, 0, 3, 2), (2, 3, 0, 1)))
BACK_GRAD = (((3, 2, 1, 0), (2, 3, 0, 1), (1, 0, 3, 2)), ((2, 3, 0, 1), (1, 2, 3, 0), (3, 0, 1, 2)))
SAME = (0, 1, 2, 3)


def targets(wave, odd, op):
    return SAME if op == 3 else wave[odd][op]


def look_up(table):
    packed = 0
    for odd in range(2):
        for member in range(QUAD):
            packed |= table[odd][member] << 2 * (QUAD * odd + member)
    place = QUAD * (lax.axis_index("tp") % 2) + member_of_quad()
    return (packed >> (2 * place)) & 3


def sent(wave, op):
    return look_up([targets(wave, odd, op) for odd in range(2)])


def came(wave, op):
    return look_up([[targets(wave, 1 - odd, op).index(m) for m in SAME] for odd in range(2)])


def call(kernel, outs, args, flops, in_specs=None, out_specs=None, scratch_shapes=(), room=32):
    size = sum(x.size * x.dtype.itemsize for x in list(args) + list(outs))
    return pl.pallas_call(
        kernel,
        out_shape=outs,
        in_specs=in_specs or [pl.BlockSpec(memory_space=pltpu.VMEM)] * len(args),
        out_specs=out_specs or [pl.BlockSpec(memory_space=pltpu.VMEM)] * len(outs),
        scratch_shapes=scratch_shapes,
        cost_estimate=pl.CostEstimate(flops=flops, bytes_accessed=size, transcendentals=0),
        compiler_params=pltpu.CompilerParams(vmem_limit_bytes=int(room * 1024 * 1024)),
    )(*args)


def state_kernel(k_ref, v_ref, o0, o1, o2, o3, k_buf, v_buf, sems):
    rows = k_ref.shape[0] // CHUNKS
    copies = []
    for i in range(CHUNKS):
        for n, (ref, buf) in enumerate(((k_ref, k_buf), (v_ref, v_buf))):
            part = pl.ds(i * rows, rows)
            copies.append(pltpu.make_async_copy(ref.at[part], buf.at[part], sems.at[n, i]))
            copies[-1].start()
    states = [0.0] * QUAD
    half = rows * CHUNKS // 2
    for part in range(2):
        for copy in copies[part * CHUNKS : (part + 1) * CHUNKS]:
            copy.wait()
        tokens = pl.ds(part * half, half)
        for op in OPS:
            cols = pl.ds(pl.multiple_of(sent(FIRST, op) * DH, DH), DH)
            states[op] = states[op] + dot(k_buf[tokens, cols], v_buf[tokens, cols], ((0,), (0,)))
    for op, out in enumerate((o0, o1, o2, o3)):
        out[...] = states[op].astype(LOW)


def local_kernel(q_ref, k_ref, v_ref, scores_ref, mixed_ref):
    mask = causal_mask(q_ref.shape[0])
    for h in range(QUAD):
        raw = dot(fixed(q_ref, h)[...], fixed(k_ref, h)[...], ((1,), (1,)))
        scores = jnp.where(mask, raw, 0.0).astype(LOW)
        scores_ref[h] = scores
        fixed(mixed_ref, h)[...] = dot(scores, fixed(v_ref, h)[...], ((1,), (0,)))


def mixed_kernel(local_ref, q_ref, c_ref, p0, p1, p2, p3, mixed_ref, sums_ref):
    count = q_ref.shape[0]
    square = jnp.zeros((count, DH), WIDE)
    product = jnp.zeros((count, DH), WIDE)
    for op, p_ref in enumerate((p0, p1, p2, p3)):
        h = came(BACK, op)
        mixed = head(local_ref, h)[...] + dot(head(q_ref, h)[...], p_ref[...], ((1,), (0,)))
        head(mixed_ref, h)[...] = mixed
        square = square + mixed * mixed
        product = product + mixed * head(c_ref, h)[...].astype(WIDE)
    sums_ref[0:1, :] = jnp.sum(square.T, axis=0, keepdims=True)
    sums_ref[1:2, :] = jnp.sum(product.T, axis=0, keepdims=True)


def token_scales(sums_ref, features, count):
    inverse = lax.rsqrt(sums_ref[0:1, :] * (1.0 / features) + EPSILON)
    projection = inverse * sums_ref[1:2, :] * (1.0 / features)
    inverse = jnp.broadcast_to(inverse, (DH, count)).T
    projection = jnp.broadcast_to(projection, (DH, count)).T
    return inverse, projection


def grad_kernel(features, mixed_ref, c_ref, q_ref, sums_ref, o0, o1, o2, o3, g_ref):
    inverse, projection = token_scales(sums_ref, features, q_ref.shape[0])
    for op, out in enumerate((o0, o1, o2, o3)):
        h = sent(FIRST_GRAD, op)
        normed = head(mixed_ref, h)[...] * inverse
        grad = (inverse * (head(c_ref, h)[...].astype(WIDE) - normed * projection)).astype(LOW)
        head(g_ref, h)[...] = grad
        out[...] = dot(head(q_ref, h)[...], grad, ((0,), (0,))).astype(LOW)


def back_kernel(features, q_ref, k_ref, v_ref, g_ref, scores_ref, mixed_ref, sums_ref, p0, p1, p2, p3,
                normed_ref, query_ref, key_ref, value_ref):
    count = q_ref.shape[0]
    mask = causal_mask(count)
    inverse, _ = token_scales(sums_ref, features, count)
    for op, p_ref in enumerate((p0, p1, p2, p3)):
        h = came(BACK, op)
        grad = head(g_ref, h)[...]
        head(normed_ref, h)[...] = (head(mixed_ref, h)[...] * inverse).astype(LOW)
        raw = dot(grad, head(v_ref, h)[...], ((1,), (1,)))
        coefs = jnp.where(mask, raw, 0.0).astype(LOW)
        query = dot(coefs, head(k_ref, h)[...], ((1,), (0,))) + dot(grad, p_ref[...], ((1,), (1,)))
        head(query_ref, h)[...] = query.astype(LOW)
        head(key_ref, h)[...] = dot(coefs, head(q_ref, h)[...], ((0,), (0,)))
        head(value_ref, h)[...] = dot(scores_ref[h], grad, ((0,), (0,)))


def last_kernel(k_ref, v_ref, key_local, value_local, p0, p1, p2, p3, key_ref, value_ref):
    for op, p_ref in enumerate((p0, p1, p2, p3)):
        h = came(BACK_GRAD, op)
        suffix = p_ref[...]
        key = head(key_local, h)[...] + dot(head(v_ref, h)[...], suffix, ((1,), (1,)))
        head(key_ref, h)[...] = key.astype(LOW)
        value = head(value_local, h)[...] + dot(head(k_ref, h)[...], suffix, ((1,), (0,)))
        head(value_ref, h)[...] = value.astype(LOW)


def quad_steps(quads, before):
    return (2, 3, 1) if quads == 4 and before else range(quads - 1, 0, -1)


def quad_targets(quads, step, before):
    targets = [z ^ step for z in range(quads)]
    if quads == 4 and step == 3:
        targets = [3, 2, 0, 1] if before else [2, 3, 1, 0]
    return targets


def sums_kernel(before, quads, *refs):
    index = lax.axis_index("seq")
    quad = index // QUAD
    first, back = (FIRST, BACK) if before else (FIRST_GRAD, BACK_GRAD)
    held, got, outs = refs[:QUAD], refs[QUAD : QUAD + quads - 1], refs[-QUAD:]

    def counts(a, b):
        return jnp.where(a < b if before else a > b, 1.0, 0.0).astype(WIDE)

    outer = jnp.zeros((DH, DH), WIDE)
    for step, total in zip(quad_steps(quads, before), got):
        outer = outer + total[...].astype(WIDE) * counts(quad ^ step, quad)
    pieces = [piece[...].astype(WIDE) for piece in held]
    for to in OPS:
        inner = outer
        for op in OPS:
            inner = inner + pieces[op] * counts(came(first, op), sent(back, to))
        outs[to][...] = inner.astype(LOW)


def exchange(value, axis, bits):
    size = lax.axis_size(axis)
    return lax.ppermute(value, axis, [(i, i ^ bits) for i in range(size)])


def cross(value, wave, op):
    cores = lax.axis_size("tp")
    pairs = []
    for i in range(lax.axis_size("seq")):
        for t in range(cores):
            member = targets(wave, t % 2, op)[i % QUAD]
            pairs.append((i * cores + t, (i - i % QUAD + member) * cores + (t ^ 1)))
    return lax.ppermute(value, ("seq", "tp"), pairs)


def exclusive_sum(held, before, *after):
    first, back = (FIRST, BACK) if before else (FIRST_GRAD, BACK_GRAD)
    held = [cross(held[op], first, op) for op in OPS]
    total = sum(piece.astype(WIDE) for piece in held).astype(LOW)
    quads = lax.axis_size("seq") // QUAD
    got = []
    for step in quad_steps(quads, before):
        targets = quad_targets(quads, step, before)
        pairs = [(z * QUAD + i, targets[z] * QUAD + i) for z in range(quads) for i in range(QUAD)]
        got.append(lax.ppermute(total, "seq", pairs))
    vmem = [pl.BlockSpec(memory_space=pltpu.VMEM)] * (QUAD + len(got))
    sums = call(
        functools.partial(sums_kernel, before, quads),
        [jax.ShapeDtypeStruct(x.shape, x.dtype) for x in held],
        (*held, *got, *after),
        0,
        in_specs=vmem + [pl.BlockSpec(memory_space=pl.ANY)] * len(after),
    )
    return [cross(sums[op], back, op) for op in OPS]


def sum_over_heads(value):
    bit = 1
    while bit < lax.axis_size("tp"):
        value = value + exchange(value, "tp", bit)
        bit *= 2
    return value


def body(q, k, v, c):
    count, width = q.shape
    features = width * lax.axis_size("tp")
    shape = jax.ShapeDtypeStruct
    state = shape((DH, DH), LOW)
    wide = shape((count, width), WIDE)
    low = shape((count, width), LOW)
    unit = 2 * count * DH * DH * QUAD
    buffers = [pltpu.VMEM(k.shape, LOW)] * 2 + [pltpu.SemaphoreType.DMA((2, CHUNKS))]
    held = call(
        state_kernel, [state] * QUAD, (k, v), unit, room=53.75,
        in_specs=[pl.BlockSpec(memory_space=pltpu.HBM)] * 2,
        scratch_shapes=buffers,
    )
    scores, local = call(
        local_kernel, [shape((QUAD, count, count), LOW), wide], (q, k, v), 4 * unit
    )
    prefix = exclusive_sum(held, True)
    mixed, sums = call(
        mixed_kernel, [wide, shape((2, count), WIDE)], (local, q, c, *prefix), unit
    )
    sums = sum_over_heads(sums)
    *terms, g = call(
        functools.partial(grad_kernel, features), [state] * QUAD + [low], (mixed, c, q, sums), unit
    )
    normed_out, query_grad, key_local, value_local = call(
        functools.partial(back_kernel, features),
        [low, low, wide, wide],
        (q, k, v, g, scores, mixed, sums, *prefix),
        9 * unit,
    )
    suffix = exclusive_sum(terms, False, key_local)
    key_grad, value_grad = call(
        last_kernel, [low, low], (k, v, key_local, value_local, *suffix), 2 * unit
    )
    return (normed_out, query_grad, key_grad, value_grad)


def solution(mesh):
    spec = P("seq", "tp")
    return jax.shard_map(body, mesh=mesh, in_specs=(spec,) * 4, out_specs=(spec,) * 4, check_vma=False)
```

```python
import functools

import jax
import jax.numpy as jnp
from jax import lax
from jax.experimental import pallas as pl
from jax.experimental.pallas import tpu as pltpu
from jax.sharding import PartitionSpec as P

DH = 128
EPSILON = 1e-06
QUAD = 4
OPS = (0, 1, 2, 3)
CHUNKS = 4
LOW, WIDE = jnp.bfloat16, jnp.float32


def dot(a, b, contract):
    return lax.dot_general(a, b, ((contract[0], contract[1]), ((), ())), preferred_element_type=WIDE)


def head(ref, h):
    return ref.at[:, pl.ds(pl.multiple_of(h * DH, DH), DH)]


def fixed(ref, h):
    return ref.at[:, h * DH : (h + 1) * DH]


def causal_mask(count):
    row = lax.broadcasted_iota(jnp.int32, (count, count), 0)
    col = lax.broadcasted_iota(jnp.int32, (count, count), 1)
    return row >= col


def member_of_quad():
    return lax.axis_index("seq") % QUAD


FIRST = (((3, 2, 1, 0), (2, 3, 0, 1), (1, 0, 3, 2)), ((3, 2, 1, 0), (1, 3, 0, 2), (2, 0, 3, 1)))
BACK = (((3, 2, 1, 0), (2, 0, 3, 1), (1, 3, 0, 2)), ((2, 3, 0, 1), (3, 2, 1, 0), (1, 0, 3, 2)))
FIRST_GRAD = (((1, 0, 3, 2), (3, 2, 0, 1), (2, 3, 1, 0)), ((1, 3, 0, 2), (3, 2, 1, 0), (2, 0, 3, 1)))
BACK_GRAD = (((3, 2, 1, 0), (1, 3, 0, 2), (2, 0, 3, 1)), ((2, 3, 1, 0), (1, 0, 3, 2), (3, 2, 0, 1)))
SAME = (0, 1, 2, 3)


def targets(wave, odd, op):
    return SAME if op == 3 else wave[odd][op]


def look_up(table):
    packed = 0
    for odd in range(2):
        for member in range(QUAD):
            packed |= table[odd][member] << 2 * (QUAD * odd + member)
    place = QUAD * (lax.axis_index("tp") % 2) + member_of_quad()
    return (packed >> (2 * place)) & 3


def sent(wave, op):
    return look_up([targets(wave, odd, op) for odd in range(2)])


def came(wave, op):
    return look_up([[targets(wave, 1 - odd, op).index(m) for m in SAME] for odd in range(2)])


def call(kernel, outs, args, flops, in_specs=None, out_specs=None, scratch_shapes=(), room=32):
    size = sum(x.size * x.dtype.itemsize for x in list(args) + list(outs))
    return pl.pallas_call(
        kernel,
        out_shape=outs,
        in_specs=in_specs or [pl.BlockSpec(memory_space=pltpu.VMEM)] * len(args),
        out_specs=out_specs or [pl.BlockSpec(memory_space=pltpu.VMEM)] * len(outs),
        scratch_shapes=scratch_shapes,
        cost_estimate=pl.CostEstimate(flops=flops, bytes_accessed=size, transcendentals=0),
        compiler_params=pltpu.CompilerParams(vmem_limit_bytes=int(room * 1024 * 1024)),
    )(*args)


def state_kernel(k_ref, v_ref, o0, o1, o2, o3, k_buf, v_buf, sems):
    rows = k_ref.shape[0] // CHUNKS
    copies = []
    for i in range(CHUNKS):
        for n, (ref, buf) in enumerate(((k_ref, k_buf), (v_ref, v_buf))):
            part = pl.ds(i * rows, rows)
            copies.append(pltpu.make_async_copy(ref.at[part], buf.at[part], sems.at[n, i]))
            copies[-1].start()
    states = [0.0] * QUAD
    half = rows * CHUNKS // 2
    for part in range(2):
        for copy in copies[part * CHUNKS : (part + 1) * CHUNKS]:
            copy.wait()
        tokens = pl.ds(part * half, half)
        for op in OPS:
            cols = pl.ds(pl.multiple_of(sent(FIRST, op) * DH, DH), DH)
            states[op] = states[op] + dot(k_buf[tokens, cols], v_buf[tokens, cols], ((0,), (0,)))
    for op, out in enumerate((o0, o1, o2, o3)):
        out[...] = states[op].astype(LOW)


def local_kernel(q_ref, k_ref, v_ref, scores_ref, mixed_ref):
    mask = causal_mask(q_ref.shape[0])
    for h in range(QUAD):
        raw = dot(fixed(q_ref, h)[...], fixed(k_ref, h)[...], ((1,), (1,)))
        scores = jnp.where(mask, raw, 0.0).astype(LOW)
        scores_ref[h] = scores
        fixed(mixed_ref, h)[...] = dot(scores, fixed(v_ref, h)[...], ((1,), (0,)))


def mixed_kernel(local_ref, q_ref, c_ref, p0, p1, p2, p3, mixed_ref, sums_ref):
    count = q_ref.shape[0]
    square = jnp.zeros((count, DH), WIDE)
    product = jnp.zeros((count, DH), WIDE)
    for op, p_ref in enumerate((p0, p1, p2, p3)):
        h = came(BACK, op)
        mixed = head(local_ref, h)[...] + dot(head(q_ref, h)[...], p_ref[...], ((1,), (0,)))
        head(mixed_ref, h)[...] = mixed
        square = square + mixed * mixed
        product = product + mixed * head(c_ref, h)[...].astype(WIDE)
    sums_ref[0:1, :] = jnp.sum(square.T, axis=0, keepdims=True)
    sums_ref[1:2, :] = jnp.sum(product.T, axis=0, keepdims=True)


def token_scales(sums_ref, features, count):
    inverse = lax.rsqrt(sums_ref[0:1, :] * (1.0 / features) + EPSILON)
    projection = inverse * sums_ref[1:2, :] * (1.0 / features)
    inverse = jnp.broadcast_to(inverse, (DH, count)).T
    projection = jnp.broadcast_to(projection, (DH, count)).T
    return inverse, projection


def grad_kernel(features, mixed_ref, c_ref, q_ref, sums_ref, o0, o1, o2, o3, g_ref):
    inverse, projection = token_scales(sums_ref, features, q_ref.shape[0])
    for op, out in enumerate((o0, o1, o2, o3)):
        h = sent(FIRST_GRAD, op)
        normed = head(mixed_ref, h)[...] * inverse
        grad = (inverse * (head(c_ref, h)[...].astype(WIDE) - normed * projection)).astype(LOW)
        head(g_ref, h)[...] = grad
        out[...] = dot(head(q_ref, h)[...], grad, ((0,), (0,))).astype(LOW)


def back_kernel(features, q_ref, k_ref, v_ref, g_ref, scores_ref, mixed_ref, sums_ref, p0, p1, p2, p3,
                normed_ref, query_ref, key_ref, value_ref):
    count = q_ref.shape[0]
    mask = causal_mask(count)
    inverse, _ = token_scales(sums_ref, features, count)
    for op, p_ref in enumerate((p0, p1, p2, p3)):
        h = came(BACK, op)
        grad = head(g_ref, h)[...]
        head(normed_ref, h)[...] = (head(mixed_ref, h)[...] * inverse).astype(LOW)
        raw = dot(grad, head(v_ref, h)[...], ((1,), (1,)))
        coefs = jnp.where(mask, raw, 0.0).astype(LOW)
        query = dot(coefs, head(k_ref, h)[...], ((1,), (0,))) + dot(grad, p_ref[...], ((1,), (1,)))
        head(query_ref, h)[...] = query.astype(LOW)
        head(key_ref, h)[...] = dot(coefs, head(q_ref, h)[...], ((0,), (0,)))
        head(value_ref, h)[...] = dot(scores_ref[h], grad, ((0,), (0,)))


def last_kernel(k_ref, v_ref, key_local, value_local, p0, p1, p2, p3, key_ref, value_ref):
    for op, p_ref in enumerate((p0, p1, p2, p3)):
        h = came(BACK_GRAD, op)
        suffix = p_ref[...]
        key = head(key_local, h)[...] + dot(head(v_ref, h)[...], suffix, ((1,), (1,)))
        head(key_ref, h)[...] = key.astype(LOW)
        value = head(value_local, h)[...] + dot(head(k_ref, h)[...], suffix, ((1,), (0,)))
        head(value_ref, h)[...] = value.astype(LOW)


def quad_steps(quads, before):
    return (2, 3, 1) if quads == 4 and before else range(quads - 1, 0, -1)


def quad_targets(quads, step, before):
    targets = [z ^ step for z in range(quads)]
    if quads == 4 and step == 3:
        targets = [3, 2, 0, 1] if before else [2, 3, 1, 0]
    return targets


def sums_kernel(before, quads, *refs):
    index = lax.axis_index("seq")
    quad = index // QUAD
    first, back = (FIRST, BACK) if before else (FIRST_GRAD, BACK_GRAD)
    held, got, outs = refs[:QUAD], refs[QUAD : QUAD + quads - 1], refs[-QUAD:]

    def counts(a, b):
        return jnp.where(a < b if before else a > b, 1.0, 0.0).astype(WIDE)

    outer = jnp.zeros((DH, DH), WIDE)
    for step, total in zip(quad_steps(quads, before), got):
        outer = outer + total[...].astype(WIDE) * counts(quad ^ step, quad)
    pieces = [piece[...].astype(WIDE) for piece in held]
    for to in OPS:
        inner = outer
        for op in OPS:
            inner = inner + pieces[op] * counts(came(first, op), sent(back, to))
        outs[to][...] = inner.astype(LOW)


def exchange(value, axis, bits):
    size = lax.axis_size(axis)
    return lax.ppermute(value, axis, [(i, i ^ bits) for i in range(size)])


def cross(value, wave, op):
    cores = lax.axis_size("tp")
    pairs = []
    for i in range(lax.axis_size("seq")):
        for t in range(cores):
            member = targets(wave, t % 2, op)[i % QUAD]
            pairs.append((i * cores + t, (i - i % QUAD + member) * cores + (t ^ 1)))
    return lax.ppermute(value, ("seq", "tp"), pairs)


def exclusive_sum(held, before, *after):
    first, back = (FIRST, BACK) if before else (FIRST_GRAD, BACK_GRAD)
    held = [cross(held[op], first, op) for op in OPS]
    total = sum(piece.astype(WIDE) for piece in held).astype(LOW)
    quads = lax.axis_size("seq") // QUAD
    got = []
    for step in quad_steps(quads, before):
        targets = quad_targets(quads, step, before)
        pairs = [(z * QUAD + i, targets[z] * QUAD + i) for z in range(quads) for i in range(QUAD)]
        got.append(lax.ppermute(total, "seq", pairs))
    vmem = [pl.BlockSpec(memory_space=pltpu.VMEM)] * (QUAD + len(got))
    sums = call(
        functools.partial(sums_kernel, before, quads),
        [jax.ShapeDtypeStruct(x.shape, x.dtype) for x in held],
        (*held, *got, *after),
        0,
        in_specs=vmem + [pl.BlockSpec(memory_space=pl.ANY)] * len(after),
    )
    return [cross(sums[op], back, op) for op in OPS]


def sum_over_heads(value):
    bit = 1
    while bit < lax.axis_size("tp"):
        value = value + exchange(value, "tp", bit)
        bit *= 2
    return value


def body(q, k, v, c):
    count, width = q.shape
    features = width * lax.axis_size("tp")
    shape = jax.ShapeDtypeStruct
    state = shape((DH, DH), LOW)
    wide = shape((count, width), WIDE)
    low = shape((count, width), LOW)
    unit = 2 * count * DH * DH * QUAD
    buffers = [pltpu.VMEM(k.shape, LOW)] * 2 + [pltpu.SemaphoreType.DMA((2, CHUNKS))]
    held = call(
        state_kernel, [state] * QUAD, (k, v), unit, room=53.75,
        in_specs=[pl.BlockSpec(memory_space=pltpu.HBM)] * 2,
        scratch_shapes=buffers,
    )
    scores, local = call(
        local_kernel, [shape((QUAD, count, count), LOW), wide], (q, k, v), 4 * unit
    )
    prefix = exclusive_sum(held, True)
    mixed, sums = call(
        mixed_kernel, [wide, shape((2, count), WIDE)], (local, q, c, *prefix), unit
    )
    sums = sum_over_heads(sums)
    *terms, g = call(
        functools.partial(grad_kernel, features), [state] * QUAD + [low], (mixed, c, q, sums), unit
    )
    normed_out, query_grad, key_local, value_local = call(
        functools.partial(back_kernel, features),
        [low, low, wide, wide],
        (q, k, v, g, scores, mixed, sums, *prefix),
        9 * unit,
    )
    suffix = exclusive_sum(terms, False, key_local)
    key_grad, value_grad = call(
        last_kernel, [low, low], (k, v, key_local, value_local, *suffix), 2 * unit
    )
    return (normed_out, query_grad, key_grad, value_grad)


def solution(mesh):
    spec = P("seq", "tp")
    return jax.shard_map(body, mesh=mesh, in_specs=(spec,) * 4, out_specs=(spec,) * 4, check_vma=False)
```

```python
import functools

import jax
import jax.numpy as jnp
from jax import lax
from jax.experimental import pallas as pl
from jax.experimental.pallas import tpu as pltpu
from jax.sharding import PartitionSpec as P

DH = 128
EPSILON = 1e-06
QUAD = 4
OPS = (0, 1, 2, 3)
CHUNKS = 4
LOW, WIDE = jnp.bfloat16, jnp.float32


def dot(a, b, contract):
    return lax.dot_general(a, b, ((contract[0], contract[1]), ((), ())), preferred_element_type=WIDE)


def head(ref, h):
    return ref.at[:, pl.ds(pl.multiple_of(h * DH, DH), DH)]


def fixed(ref, h):
    return ref.at[:, h * DH : (h + 1) * DH]


def causal_mask(count):
    row = lax.broadcasted_iota(jnp.int32, (count, count), 0)
    col = lax.broadcasted_iota(jnp.int32, (count, count), 1)
    return row >= col


def member_of_quad():
    return lax.axis_index("seq") % QUAD


FIRST = (((3, 2, 1, 0), (1, 3, 0, 2), (2, 0, 3, 1)), ((2, 3, 1, 0), (3, 2, 0, 1), (1, 0, 3, 2)))
BACK = (((3, 2, 1, 0), (2, 3, 0, 1), (1, 0, 3, 2)), ((3, 2, 0, 1), (2, 3, 1, 0), (1, 0, 3, 2)))
FIRST_GRAD = (((3, 2, 1, 0), (2, 3, 0, 1), (1, 0, 3, 2)), ((3, 2, 1, 0), (1, 0, 3, 2), (2, 3, 0, 1)))
BACK_GRAD = (((3, 2, 1, 0), (2, 3, 0, 1), (1, 0, 3, 2)), ((2, 3, 0, 1), (1, 2, 3, 0), (3, 0, 1, 2)))
SAME = (0, 1, 2, 3)


def targets(wave, odd, op):
    return SAME if op == 3 else wave[odd][op]


def look_up(table):
    packed = 0
    for odd in range(2):
        for member in range(QUAD):
            packed |= table[odd][member] << 2 * (QUAD * odd + member)
    place = QUAD * (lax.axis_index("tp") % 2) + member_of_quad()
    return (packed >> (2 * place)) & 3


def sent(wave, op):
    return look_up([targets(wave, odd, op) for odd in range(2)])


def came(wave, op):
    return look_up([[targets(wave, 1 - odd, op).index(m) for m in SAME] for odd in range(2)])


def call(kernel, outs, args, flops, in_specs=None, out_specs=None, scratch_shapes=(), room=32):
    size = sum(x.size * x.dtype.itemsize for x in list(args) + list(outs))
    return pl.pallas_call(
        kernel,
        out_shape=outs,
        in_specs=in_specs or [pl.BlockSpec(memory_space=pltpu.VMEM)] * len(args),
        out_specs=out_specs or [pl.BlockSpec(memory_space=pltpu.VMEM)] * len(outs),
        scratch_shapes=scratch_shapes,
        cost_estimate=pl.CostEstimate(flops=flops, bytes_accessed=size, transcendentals=0),
        compiler_params=pltpu.CompilerParams(vmem_limit_bytes=int(room * 1024 * 1024)),
    )(*args)


def state_kernel(k_ref, v_ref, o0, o1, o2, o3, k_buf, v_buf, sems):
    rows = k_ref.shape[0] // CHUNKS
    copies = []
    for i in range(CHUNKS):
        for n, (ref, buf) in enumerate(((k_ref, k_buf), (v_ref, v_buf))):
            part = pl.ds(i * rows, rows)
            copies.append(pltpu.make_async_copy(ref.at[part], buf.at[part], sems.at[n, i]))
            copies[-1].start()
    states = [0.0] * QUAD
    half = rows * CHUNKS // 2
    for part in range(2):
        for copy in copies[part * CHUNKS : (part + 1) * CHUNKS]:
            copy.wait()
        tokens = pl.ds(part * half, half)
        for op in OPS:
            cols = pl.ds(pl.multiple_of(sent(FIRST, op) * DH, DH), DH)
            states[op] = states[op] + dot(k_buf[tokens, cols], v_buf[tokens, cols], ((0,), (0,)))
    for op, out in enumerate((o0, o1, o2, o3)):
        out[...] = states[op].astype(LOW)


def local_kernel(q_ref, k_ref, v_ref, scores_ref, mixed_ref, turned_ref):
    mask = causal_mask(q_ref.shape[0])
    for h in range(QUAD):
        turned_ref[h] = fixed(q_ref, h)[...].T
        raw = dot(fixed(q_ref, h)[...], fixed(k_ref, h)[...], ((1,), (1,)))
        scores = jnp.where(mask, raw, 0.0).astype(LOW)
        scores_ref[h] = scores
        fixed(mixed_ref, h)[...] = dot(scores, fixed(v_ref, h)[...], ((1,), (0,)))


def mixed_kernel(local_ref, q_ref, c_ref, p0, p1, p2, p3, mixed_ref, sums_ref):
    count = q_ref.shape[0]
    square = jnp.zeros((count, DH), WIDE)
    product = jnp.zeros((count, DH), WIDE)
    for op, p_ref in enumerate((p0, p1, p2, p3)):
        h = came(BACK, op)
        mixed = head(local_ref, h)[...] + dot(head(q_ref, h)[...], p_ref[...], ((1,), (0,)))
        head(mixed_ref, h)[...] = mixed
        square = square + mixed * mixed
        product = product + mixed * head(c_ref, h)[...].astype(WIDE)
    sums_ref[0:1, :] = jnp.sum(square.T, axis=0, keepdims=True)
    sums_ref[1:2, :] = jnp.sum(product.T, axis=0, keepdims=True)


def token_scales(sums_ref, features, count):
    inverse = lax.rsqrt(sums_ref[0:1, :] * (1.0 / features) + EPSILON)
    projection = inverse * sums_ref[1:2, :] * (1.0 / features)
    inverse = jnp.broadcast_to(inverse, (DH, count)).T
    projection = jnp.broadcast_to(projection, (DH, count)).T
    return inverse, projection


def grad_kernel(features, mixed_ref, c_ref, turned_ref, sums_ref, o0, o1, o2, o3, g_ref):
    count = c_ref.shape[0]
    inverse = lax.rsqrt(sums_ref[0:1, :] * (1.0 / features) + EPSILON)
    share = inverse * inverse * (inverse * sums_ref[1:2, :] * (1.0 / features))
    inverse = jnp.broadcast_to(inverse, (DH, count)).T
    share = jnp.broadcast_to(share, (DH, count)).T
    for op, out in enumerate((o0, o1, o2, o3)):
        h = sent(FIRST_GRAD, op)
        grad = (inverse * head(c_ref, h)[...].astype(WIDE) - share * head(mixed_ref, h)[...]).astype(LOW)
        head(g_ref, h)[...] = grad
        out[...] = dot(turned_ref[h], grad, ((1,), (0,))).astype(LOW)


def back_kernel(features, q_ref, k_ref, v_ref, g_ref, scores_ref, mixed_ref, sums_ref, p0, p1, p2, p3,
                normed_ref, query_ref, key_ref, value_ref):
    count = q_ref.shape[0]
    mask = causal_mask(count)
    inverse, _ = token_scales(sums_ref, features, count)
    for op, p_ref in enumerate((p0, p1, p2, p3)):
        h = came(BACK, op)
        grad = head(g_ref, h)[...]
        head(normed_ref, h)[...] = (head(mixed_ref, h)[...] * inverse).astype(LOW)
        raw = dot(grad, head(v_ref, h)[...], ((1,), (1,)))
        coefs = jnp.where(mask, raw, 0.0).astype(LOW)
        query = dot(coefs, head(k_ref, h)[...], ((1,), (0,))) + dot(grad, p_ref[...], ((1,), (1,)))
        head(query_ref, h)[...] = query.astype(LOW)
        head(key_ref, h)[...] = dot(coefs, head(q_ref, h)[...], ((0,), (0,)))
        head(value_ref, h)[...] = dot(scores_ref[h], grad, ((0,), (0,)))


def last_kernel(k_ref, v_ref, key_local, value_local, p0, p1, p2, p3, key_ref, value_ref):
    for op, p_ref in enumerate((p0, p1, p2, p3)):
        h = came(BACK_GRAD, op)
        suffix = p_ref[...]
        key = head(key_local, h)[...] + dot(head(v_ref, h)[...], suffix, ((1,), (1,)))
        head(key_ref, h)[...] = key.astype(LOW)
        value = head(value_local, h)[...] + dot(head(k_ref, h)[...], suffix, ((1,), (0,)))
        head(value_ref, h)[...] = value.astype(LOW)


def quad_steps(quads, before):
    return (2, 3, 1) if quads == 4 and before else range(quads - 1, 0, -1)


def quad_targets(quads, step, before):
    targets = [z ^ step for z in range(quads)]
    if quads == 4 and step == 3:
        targets = [3, 2, 0, 1] if before else [2, 3, 1, 0]
    return targets


def sums_kernel(before, quads, *refs):
    index = lax.axis_index("seq")
    quad = index // QUAD
    first, back = (FIRST, BACK) if before else (FIRST_GRAD, BACK_GRAD)
    held, got, outs = refs[:QUAD], refs[QUAD : QUAD + quads - 1], refs[-QUAD:]

    def counts(a, b):
        return jnp.where(a < b if before else a > b, 1.0, 0.0).astype(WIDE)

    outer = jnp.zeros((DH, DH), WIDE)
    for step, total in zip(quad_steps(quads, before), got):
        outer = outer + total[...].astype(WIDE) * counts(quad ^ step, quad)
    pieces = [piece[...].astype(WIDE) for piece in held]
    for to in OPS:
        inner = outer
        for op in OPS:
            inner = inner + pieces[op] * counts(came(first, op), sent(back, to))
        outs[to][...] = inner.astype(LOW)


def exchange(value, axis, bits):
    size = lax.axis_size(axis)
    return lax.ppermute(value, axis, [(i, i ^ bits) for i in range(size)])


def cross(value, wave, op):
    cores = lax.axis_size("tp")
    pairs = []
    for i in range(lax.axis_size("seq")):
        for t in range(cores):
            member = targets(wave, t % 2, op)[i % QUAD]
            pairs.append((i * cores + t, (i - i % QUAD + member) * cores + (t ^ 1)))
    return lax.ppermute(value, ("seq", "tp"), pairs)


def exclusive_sum(held, before, *after):
    first, back = (FIRST, BACK) if before else (FIRST_GRAD, BACK_GRAD)
    held = [cross(held[op], first, op) for op in OPS]
    total = sum(piece.astype(WIDE) for piece in held).astype(LOW)
    quads = lax.axis_size("seq") // QUAD
    got = []
    for step in quad_steps(quads, before):
        targets = quad_targets(quads, step, before)
        pairs = [(z * QUAD + i, targets[z] * QUAD + i) for z in range(quads) for i in range(QUAD)]
        got.append(lax.ppermute(total, "seq", pairs))
    vmem = [pl.BlockSpec(memory_space=pltpu.VMEM)] * (QUAD + len(got))
    sums = call(
        functools.partial(sums_kernel, before, quads),
        [jax.ShapeDtypeStruct(x.shape, x.dtype) for x in held],
        (*held, *got, *after),
        0,
        in_specs=vmem + [pl.BlockSpec(memory_space=pl.ANY)] * len(after),
    )
    return [cross(sums[op], back, op) for op in OPS]


def sum_over_heads(value):
    bit = 1
    while bit < lax.axis_size("tp"):
        value = value + exchange(value, "tp", bit)
        bit *= 2
    return value


def body(q, k, v, c):
    count, width = q.shape
    features = width * lax.axis_size("tp")
    shape = jax.ShapeDtypeStruct
    state = shape((DH, DH), LOW)
    wide = shape((count, width), WIDE)
    low = shape((count, width), LOW)
    unit = 2 * count * DH * DH * QUAD
    buffers = [pltpu.VMEM(k.shape, LOW)] * 2 + [pltpu.SemaphoreType.DMA((2, CHUNKS))]
    held = call(
        state_kernel, [state] * QUAD, (k, v), unit, room=53.75,
        in_specs=[pl.BlockSpec(memory_space=pltpu.HBM)] * 2,
        scratch_shapes=buffers,
    )
    scores, local, turned = call(
        local_kernel,
        [shape((QUAD, count, count), LOW), wide, shape((QUAD, DH, count), LOW)],
        (q, k, v),
        4 * unit,
    )
    prefix = exclusive_sum(held, True)
    mixed, sums = call(
        mixed_kernel, [wide, shape((2, count), WIDE)], (local, q, c, *prefix), unit
    )
    sums = sum_over_heads(sums)
    *terms, g = call(
        functools.partial(grad_kernel, features), [state] * QUAD + [low], (mixed, c, turned, sums), unit
    )
    normed_out, query_grad, key_local, value_local = call(
        functools.partial(back_kernel, features),
        [low, low, wide, wide],
        (q, k, v, g, scores, mixed, sums, *prefix),
        9 * unit,
    )
    suffix = exclusive_sum(terms, False, key_local)
    key_grad, value_grad = call(
        last_kernel, [low, low], (k, v, key_local, value_local, *suffix), 2 * unit
    )
    return (normed_out, query_grad, key_grad, value_grad)


def solution(mesh):
    spec = P("seq", "tp")
    return jax.shard_map(body, mesh=mesh, in_specs=(spec,) * 4, out_specs=(spec,) * 4, check_vma=False)
```

```python
import functools

import jax
import jax.numpy as jnp
from jax import lax
from jax.experimental import pallas as pl
from jax.experimental.pallas import tpu as pltpu
from jax.sharding import PartitionSpec as P

DH = 128
EPSILON = 1e-06
QUAD = 4
OPS = (0, 1, 2, 3)
CHUNKS = 4
LOW, WIDE = jnp.bfloat16, jnp.float32


def dot(a, b, contract):
    return lax.dot_general(a, b, ((contract[0], contract[1]), ((), ())), preferred_element_type=WIDE)


def head(ref, h):
    return ref.at[:, pl.ds(pl.multiple_of(h * DH, DH), DH)]


def fixed(ref, h):
    return ref.at[:, h * DH : (h + 1) * DH]


def causal_mask(count):
    row = lax.broadcasted_iota(jnp.int32, (count, count), 0)
    col = lax.broadcasted_iota(jnp.int32, (count, count), 1)
    return row >= col


def member_of_quad():
    return lax.axis_index("seq") % QUAD


FIRST = (((3, 2, 1, 0), (1, 3, 0, 2), (2, 0, 3, 1)), ((2, 3, 1, 0), (3, 2, 0, 1), (1, 0, 3, 2)))
BACK = (((3, 2, 1, 0), (2, 3, 0, 1), (1, 0, 3, 2)), ((3, 2, 0, 1), (2, 3, 1, 0), (1, 0, 3, 2)))
FIRST_GRAD = (((3, 2, 1, 0), (2, 3, 0, 1), (1, 0, 3, 2)), ((3, 2, 1, 0), (1, 0, 3, 2), (2, 3, 0, 1)))
BACK_GRAD = (((3, 2, 1, 0), (2, 3, 0, 1), (1, 0, 3, 2)), ((2, 3, 0, 1), (1, 2, 3, 0), (3, 0, 1, 2)))
SAME = (0, 1, 2, 3)
EARLY, LATE = (0, 1), (2, 3)


def targets(wave, odd, op):
    return SAME if op == 3 else wave[odd][op]


def look_up(table):
    packed = 0
    for odd in range(2):
        for member in range(QUAD):
            packed |= table[odd][member] << 2 * (QUAD * odd + member)
    place = QUAD * (lax.axis_index("tp") % 2) + member_of_quad()
    return (packed >> (2 * place)) & 3


def sent(wave, op):
    return look_up([targets(wave, odd, op) for odd in range(2)])


def came(wave, op):
    return look_up([[targets(wave, 1 - odd, op).index(m) for m in SAME] for odd in range(2)])


def call(kernel, outs, args, flops, in_specs=None, out_specs=None, scratch_shapes=(), room=32):
    size = sum(x.size * x.dtype.itemsize for x in list(args) + list(outs))
    return pl.pallas_call(
        kernel,
        out_shape=outs,
        in_specs=in_specs or [pl.BlockSpec(memory_space=pltpu.VMEM)] * len(args),
        out_specs=out_specs or [pl.BlockSpec(memory_space=pltpu.VMEM)] * len(outs),
        scratch_shapes=scratch_shapes,
        cost_estimate=pl.CostEstimate(flops=flops, bytes_accessed=size, transcendentals=0),
        compiler_params=pltpu.CompilerParams(vmem_limit_bytes=int(room * 1024 * 1024)),
    )(*args)


def state_kernel(k_ref, v_ref, o0, o1, o2, o3, k_buf, v_buf, sems):
    rows = k_ref.shape[0] // CHUNKS
    copies = []
    for i in range(CHUNKS):
        for n, (ref, buf) in enumerate(((k_ref, k_buf), (v_ref, v_buf))):
            part = pl.ds(i * rows, rows)
            copies.append(pltpu.make_async_copy(ref.at[part], buf.at[part], sems.at[n, i]))
            copies[-1].start()
    states = [0.0] * QUAD
    half = rows * CHUNKS // 2
    for part in range(2):
        for copy in copies[part * CHUNKS : (part + 1) * CHUNKS]:
            copy.wait()
        tokens = pl.ds(part * half, half)
        for op in OPS:
            cols = pl.ds(pl.multiple_of(sent(FIRST, op) * DH, DH), DH)
            states[op] = states[op] + dot(k_buf[tokens, cols], v_buf[tokens, cols], ((0,), (0,)))
    for op, out in enumerate((o0, o1, o2, o3)):
        out[...] = states[op].astype(LOW)


def local_kernel(q_ref, k_ref, v_ref, scores_ref, mixed_ref, turned_ref):
    mask = causal_mask(q_ref.shape[0])
    for h in range(QUAD):
        turned_ref[h] = fixed(q_ref, h)[...].T
        raw = dot(fixed(q_ref, h)[...], fixed(k_ref, h)[...], ((1,), (1,)))
        scores = jnp.where(mask, raw, 0.0).astype(LOW)
        scores_ref[h] = scores
        fixed(mixed_ref, h)[...] = dot(scores, fixed(v_ref, h)[...], ((1,), (0,)))


def mixed_kernel(ops, *refs):
    local_ref, q_ref, c_ref = refs[:3]
    mixed_ref, square_ref, product_ref = refs[-3:]
    for n, op in enumerate(ops):
        h = came(BACK, op)
        mixed = head(local_ref, h)[...] + dot(head(q_ref, h)[...], refs[3 + n][...], ((1,), (0,)))
        mixed_ref[n] = mixed
        square = mixed * mixed
        product = mixed * head(c_ref, h)[...].astype(WIDE)
        square_ref[...] = square if n == 0 else square_ref[...] + square
        product_ref[...] = product if n == 0 else product_ref[...] + product


def sums_of_tokens_kernel(local_ref, q_ref, c_ref, p2, p3, square_ref, product_ref, mixed_ref, sums_ref):
    square, product = square_ref[...], product_ref[...]
    for n, (op, p_ref) in enumerate(zip(LATE, (p2, p3))):
        h = came(BACK, op)
        mixed = head(local_ref, h)[...] + dot(head(q_ref, h)[...], p_ref[...], ((1,), (0,)))
        mixed_ref[n] = mixed
        square = square + mixed * mixed
        product = product + mixed * head(c_ref, h)[...].astype(WIDE)
    sums_ref[0:1, :] = jnp.sum(square.T, axis=0, keepdims=True)
    sums_ref[1:2, :] = jnp.sum(product.T, axis=0, keepdims=True)


def token_scales(sums_ref, features, count):
    inverse = lax.rsqrt(sums_ref[0:1, :] * (1.0 / features) + EPSILON)
    projection = inverse * sums_ref[1:2, :] * (1.0 / features)
    inverse = jnp.broadcast_to(inverse, (DH, count)).T
    projection = jnp.broadcast_to(projection, (DH, count)).T
    return inverse, projection


def grad_kernel(features, mixed_ref, late_ref, c_ref, turned_ref, sums_ref, o0, o1, o2, o3, g_ref, terms_ref):
    count = c_ref.shape[0]
    inverse = lax.rsqrt(sums_ref[0:1, :] * (1.0 / features) + EPSILON)
    share = inverse * inverse * (inverse * sums_ref[1:2, :] * (1.0 / features))
    inverse = jnp.broadcast_to(inverse, (DH, count)).T
    share = jnp.broadcast_to(share, (DH, count)).T
    for op in EARLY + LATE:
        h = came(BACK, op)
        mixed = late_ref[LATE.index(op)] if op in LATE else mixed_ref[EARLY.index(op)]
        grad = (inverse * head(c_ref, h)[...].astype(WIDE) - share * mixed).astype(LOW)
        head(g_ref, h)[...] = grad
        terms_ref[h] = dot(turned_ref[h], grad, ((1,), (0,))).astype(LOW)
    for op, out in enumerate((o0, o1, o2, o3)):
        out[...] = terms_ref[sent(FIRST_GRAD, op)]


def back_kernel(features, q_ref, k_ref, v_ref, g_ref, scores_ref, mixed_ref, late_ref, sums_ref, p0, p1, p2, p3,
                normed_ref, query_ref, key_ref, value_ref):
    count = q_ref.shape[0]
    mask = causal_mask(count)
    inverse, _ = token_scales(sums_ref, features, count)
    for op, p_ref in enumerate((p0, p1, p2, p3)):
        h = came(BACK, op)
        grad = head(g_ref, h)[...]
        head(normed_ref, h)[...] = ((late_ref[LATE.index(op)] if op in LATE else mixed_ref[EARLY.index(op)]) * inverse).astype(LOW)
        raw = dot(grad, head(v_ref, h)[...], ((1,), (1,)))
        coefs = jnp.where(mask, raw, 0.0).astype(LOW)
        query = dot(coefs, head(k_ref, h)[...], ((1,), (0,))) + dot(grad, p_ref[...], ((1,), (1,)))
        head(query_ref, h)[...] = query.astype(LOW)
        head(key_ref, h)[...] = dot(coefs, head(q_ref, h)[...], ((0,), (0,)))
        head(value_ref, h)[...] = dot(scores_ref[h], grad, ((0,), (0,)))


def grads_of(k_ref, v_ref, key_local, value_local, suffix, h):
    key = head(key_local, h)[...] + dot(head(v_ref, h)[...], suffix, ((1,), (1,)))
    value = head(value_local, h)[...] + dot(head(k_ref, h)[...], suffix, ((1,), (0,)))
    return key.astype(LOW), value.astype(LOW)


def early_kernel(k_ref, v_ref, key_local, value_local, p0, p1, key_ref, value_ref):
    for n, (op, p_ref) in enumerate(zip(EARLY, (p0, p1))):
        h = came(BACK_GRAD, op)
        key_ref[n], value_ref[n] = grads_of(k_ref, v_ref, key_local, value_local, p_ref[...], h)


def last_kernel(k_ref, v_ref, key_local, value_local, p2, p3, key_early, value_early, key_ref, value_ref):
    for n, op in enumerate(EARLY):
        h = came(BACK_GRAD, op)
        head(key_ref, h)[...] = key_early[n]
        head(value_ref, h)[...] = value_early[n]
    for op, p_ref in zip(LATE, (p2, p3)):
        h = came(BACK_GRAD, op)
        key, value = grads_of(k_ref, v_ref, key_local, value_local, p_ref[...], h)
        head(key_ref, h)[...] = key
        head(value_ref, h)[...] = value


def quad_steps(quads, before):
    return (2, 3, 1) if quads == 4 and before else range(quads - 1, 0, -1)


def quad_targets(quads, step, before):
    targets = [z ^ step for z in range(quads)]
    if quads == 4 and step == 3:
        targets = [3, 2, 0, 1] if before else [2, 3, 1, 0]
    return targets


def sums_kernel(before, quads, *refs):
    index = lax.axis_index("seq")
    quad = index // QUAD
    first, back = (FIRST, BACK) if before else (FIRST_GRAD, BACK_GRAD)
    held, got, outs = refs[:QUAD], refs[QUAD : QUAD + quads - 1], refs[-QUAD:]

    def counts(a, b):
        return jnp.where(a < b if before else a > b, 1.0, 0.0).astype(WIDE)

    outer = jnp.zeros((DH, DH), WIDE)
    for step, total in zip(quad_steps(quads, before), got):
        outer = outer + total[...].astype(WIDE) * counts(quad ^ step, quad)
    pieces = [piece[...].astype(WIDE) for piece in held]
    for to in OPS:
        inner = outer
        for op in OPS:
            inner = inner + pieces[op] * counts(came(first, op), sent(back, to))
        outs[to][...] = inner.astype(LOW)


def exchange(value, axis, bits):
    size = lax.axis_size(axis)
    return lax.ppermute(value, axis, [(i, i ^ bits) for i in range(size)])


def cross(value, wave, op):
    cores = lax.axis_size("tp")
    pairs = []
    for i in range(lax.axis_size("seq")):
        for t in range(cores):
            member = targets(wave, t % 2, op)[i % QUAD]
            pairs.append((i * cores + t, (i - i % QUAD + member) * cores + (t ^ 1)))
    return lax.ppermute(value, ("seq", "tp"), pairs)


def exclusive_sum(held, before, *after):
    first, back = (FIRST, BACK) if before else (FIRST_GRAD, BACK_GRAD)
    held = [cross(held[op], first, op) for op in OPS]
    total = sum(piece.astype(WIDE) for piece in held).astype(LOW)
    quads = lax.axis_size("seq") // QUAD
    got = []
    for step in quad_steps(quads, before):
        targets = quad_targets(quads, step, before)
        pairs = [(z * QUAD + i, targets[z] * QUAD + i) for z in range(quads) for i in range(QUAD)]
        got.append(lax.ppermute(total, "seq", pairs))
    vmem = [pl.BlockSpec(memory_space=pltpu.VMEM)] * (QUAD + len(got))
    sums = call(
        functools.partial(sums_kernel, before, quads),
        [jax.ShapeDtypeStruct(x.shape, x.dtype) for x in held],
        (*held, *got, *after),
        0,
        in_specs=vmem + [pl.BlockSpec(memory_space=pl.ANY)] * len(after),
    )
    return [cross(sums[op], back, op) for op in OPS]


def sum_over_heads(value):
    bit = 1
    while bit < lax.axis_size("tp"):
        value = value + exchange(value, "tp", bit)
        bit *= 2
    return value


def body(q, k, v, c):
    count, width = q.shape
    features = width * lax.axis_size("tp")
    shape = jax.ShapeDtypeStruct
    state = shape((DH, DH), LOW)
    wide = shape((count, width), WIDE)
    low = shape((count, width), LOW)
    unit = 2 * count * DH * DH * QUAD
    buffers = [pltpu.VMEM(k.shape, LOW)] * 2 + [pltpu.SemaphoreType.DMA((2, CHUNKS))]
    held = call(
        state_kernel, [state] * QUAD, (k, v), unit, room=53.75,
        in_specs=[pl.BlockSpec(memory_space=pltpu.HBM)] * 2,
        scratch_shapes=buffers,
    )
    scores, local, turned = call(
        local_kernel,
        [shape((QUAD, count, count), LOW), wide, shape((QUAD, DH, count), LOW)],
        (q, k, v),
        4 * unit,
    )
    prefix = exclusive_sum(held, True)
    part = shape((count, DH), WIDE)
    mixed, square, product = call(
        functools.partial(mixed_kernel, EARLY),
        [shape((2, count, DH), WIDE), part, part],
        (local, q, c, *[prefix[op] for op in EARLY]),
        unit,
    )
    late, sums = call(
        sums_of_tokens_kernel,
        [shape((2, count, DH), WIDE), shape((2, count), WIDE)],
        (local, q, c, *[prefix[op] for op in LATE], square, product),
        unit,
    )
    sums = sum_over_heads(sums)
    *terms, g = call(
        functools.partial(grad_kernel, features),
        [state] * QUAD + [low],
        (mixed, late, c, turned, sums),
        unit,
        scratch_shapes=[pltpu.VMEM((QUAD, DH, DH), LOW)],
    )
    normed_out, query_grad, key_local, value_local = call(
        functools.partial(back_kernel, features),
        [low, low, wide, wide],
        (q, k, v, g, scores, mixed, late, sums, *prefix),
        9 * unit,
    )
    suffix = exclusive_sum(terms, False, key_local)
    early = shape((2, count, DH), LOW)
    key_early, value_early = call(
        early_kernel, [early] * 2, (k, v, key_local, value_local, *[suffix[op] for op in EARLY]), 2 * unit
    )
    key_grad, value_grad = call(
        last_kernel, [low, low], (k, v, key_local, value_local, *[suffix[op] for op in LATE], key_early, value_early), unit
    )
    return (normed_out, query_grad, key_grad, value_grad)


def solution(mesh):
    spec = P("seq", "tp")
    return jax.shard_map(body, mesh=mesh, in_specs=(spec,) * 4, out_specs=(spec,) * 4, check_vma=False)
```

```python
import functools

import jax
import jax.numpy as jnp
from jax import lax
from jax.experimental import pallas as pl
from jax.experimental.pallas import tpu as pltpu
from jax.sharding import PartitionSpec as P

DH = 128
EPSILON = 1e-06
QUAD = 4
OPS = (0, 1, 2, 3)
CHUNKS = 4
LOW, WIDE = jnp.bfloat16, jnp.float32


def dot(a, b, contract):
    return lax.dot_general(a, b, ((contract[0], contract[1]), ((), ())), preferred_element_type=WIDE)


def head(ref, h):
    return ref.at[:, pl.ds(pl.multiple_of(h * DH, DH), DH)]


def fixed(ref, h):
    return ref.at[:, h * DH : (h + 1) * DH]


def causal_mask(count):
    row = lax.broadcasted_iota(jnp.int32, (count, count), 0)
    col = lax.broadcasted_iota(jnp.int32, (count, count), 1)
    return row >= col


def member_of_quad():
    return lax.axis_index("seq") % QUAD


FIRST = (((3, 2, 1, 0), (1, 0, 3, 2), (2, 3, 0, 1)), ((1, 2, 3, 0), (3, 0, 1, 2), (2, 3, 0, 1)))
BACK = (((3, 2, 1, 0), (2, 3, 0, 1), (1, 0, 3, 2)), ((3, 2, 0, 1), (2, 3, 1, 0), (1, 0, 3, 2)))
FIRST_GRAD = (((3, 2, 1, 0), (2, 0, 3, 1), (1, 3, 0, 2)), ((3, 0, 1, 2), (1, 2, 3, 0), (2, 3, 0, 1)))
BACK_GRAD = (((3, 2, 1, 0), (1, 3, 0, 2), (2, 0, 3, 1)), ((2, 3, 1, 0), (1, 0, 3, 2), (3, 2, 0, 1)))
SAME = (0, 1, 2, 3)
EARLY, LATE = (0, 1), (2, 3)


def targets(wave, odd, op):
    return SAME if op == 3 else wave[odd][op]


def look_up(table):
    packed = 0
    for odd in range(2):
        for member in range(QUAD):
            packed |= table[odd][member] << 2 * (QUAD * odd + member)
    place = QUAD * (lax.axis_index("tp") % 2) + member_of_quad()
    return (packed >> (2 * place)) & 3


def sent(wave, op):
    return look_up([targets(wave, odd, op) for odd in range(2)])


def came(wave, op):
    return look_up([[targets(wave, 1 - odd, op).index(m) for m in SAME] for odd in range(2)])


def call(kernel, outs, args, flops, in_specs=None, out_specs=None, scratch_shapes=(), room=32):
    size = sum(x.size * x.dtype.itemsize for x in list(args) + list(outs))
    return pl.pallas_call(
        kernel,
        out_shape=outs,
        in_specs=in_specs or [pl.BlockSpec(memory_space=pltpu.VMEM)] * len(args),
        out_specs=out_specs or [pl.BlockSpec(memory_space=pltpu.VMEM)] * len(outs),
        scratch_shapes=scratch_shapes,
        cost_estimate=pl.CostEstimate(flops=flops, bytes_accessed=size, transcendentals=0),
        compiler_params=pltpu.CompilerParams(vmem_limit_bytes=int(room * 1024 * 1024)),
    )(*args)


def state_kernel(k_ref, v_ref, o0, o1, o2, o3, k_buf, v_buf, sems):
    rows = k_ref.shape[0] // CHUNKS
    copies = []
    for i in range(CHUNKS):
        for n, (ref, buf) in enumerate(((k_ref, k_buf), (v_ref, v_buf))):
            part = pl.ds(i * rows, rows)
            copies.append(pltpu.make_async_copy(ref.at[part], buf.at[part], sems.at[n, i]))
            copies[-1].start()
    states = [0.0] * QUAD
    half = rows * CHUNKS // 2
    for part in range(2):
        for copy in copies[part * CHUNKS : (part + 1) * CHUNKS]:
            copy.wait()
        tokens = pl.ds(part * half, half)
        for op in OPS:
            cols = pl.ds(pl.multiple_of(sent(FIRST, op) * DH, DH), DH)
            states[op] = states[op] + dot(k_buf[tokens, cols], v_buf[tokens, cols], ((0,), (0,)))
    for op, out in enumerate((o0, o1, o2, o3)):
        out[...] = states[op].astype(LOW)


def local_kernel(q_ref, k_ref, v_ref, scores_ref, mixed_ref, turned_ref):
    mask = causal_mask(q_ref.shape[0])
    for h in range(QUAD):
        turned_ref[h] = fixed(q_ref, h)[...].T
        raw = dot(fixed(q_ref, h)[...], fixed(k_ref, h)[...], ((1,), (1,)))
        scores = jnp.where(mask, raw, 0.0).astype(LOW)
        scores_ref[h] = scores
        fixed(mixed_ref, h)[...] = dot(scores, fixed(v_ref, h)[...], ((1,), (0,)))


def mixed_kernel(ops, *refs):
    local_ref, q_ref, c_ref = refs[:3]
    mixed_ref, square_ref, product_ref = refs[-3:]
    for n, op in enumerate(ops):
        h = came(BACK, op)
        mixed = head(local_ref, h)[...] + dot(head(q_ref, h)[...], refs[3 + n][...], ((1,), (0,)))
        mixed_ref[n] = mixed
        square = mixed * mixed
        product = mixed * head(c_ref, h)[...].astype(WIDE)
        square_ref[...] = square if n == 0 else square_ref[...] + square
        product_ref[...] = product if n == 0 else product_ref[...] + product


def sums_of_tokens_kernel(local_ref, q_ref, c_ref, p2, p3, square_ref, product_ref, mixed_ref, sums_ref):
    square, product = square_ref[...], product_ref[...]
    for n, (op, p_ref) in enumerate(zip(LATE, (p2, p3))):
        h = came(BACK, op)
        mixed = head(local_ref, h)[...] + dot(head(q_ref, h)[...], p_ref[...], ((1,), (0,)))
        mixed_ref[n] = mixed
        square = square + mixed * mixed
        product = product + mixed * head(c_ref, h)[...].astype(WIDE)
    sums_ref[0:1, :] = jnp.sum(square.T, axis=0, keepdims=True)
    sums_ref[1:2, :] = jnp.sum(product.T, axis=0, keepdims=True)


def token_scales(sums_ref, features, count):
    inverse = lax.rsqrt(sums_ref[0:1, :] * (1.0 / features) + EPSILON)
    projection = inverse * sums_ref[1:2, :] * (1.0 / features)
    inverse = jnp.broadcast_to(inverse, (DH, count)).T
    projection = jnp.broadcast_to(projection, (DH, count)).T
    return inverse, projection


def grad_kernel(features, mixed_ref, late_ref, c_ref, turned_ref, sums_ref, o0, o1, o2, o3, g_ref, terms_ref):
    count = c_ref.shape[0]
    inverse = lax.rsqrt(sums_ref[0:1, :] * (1.0 / features) + EPSILON)
    share = inverse * inverse * (inverse * sums_ref[1:2, :] * (1.0 / features))
    inverse = jnp.broadcast_to(inverse, (DH, count)).T
    share = jnp.broadcast_to(share, (DH, count)).T
    for op in EARLY + LATE:
        h = came(BACK, op)
        mixed = late_ref[LATE.index(op)] if op in LATE else mixed_ref[EARLY.index(op)]
        grad = (inverse * head(c_ref, h)[...].astype(WIDE) - share * mixed).astype(LOW)
        head(g_ref, h)[...] = grad
        terms_ref[h] = dot(turned_ref[h], grad, ((1,), (0,))).astype(LOW)
    for op, out in enumerate((o0, o1, o2, o3)):
        out[...] = terms_ref[sent(FIRST_GRAD, op)]


def back_kernel(features, q_ref, k_ref, v_ref, g_ref, scores_ref, mixed_ref, late_ref, sums_ref, p0, p1, p2, p3,
                normed_ref, query_ref, key_ref, value_ref):
    count = q_ref.shape[0]
    mask = causal_mask(count)
    inverse, _ = token_scales(sums_ref, features, count)
    for op, p_ref in enumerate((p0, p1, p2, p3)):
        h = came(BACK, op)
        grad = head(g_ref, h)[...]
        head(normed_ref, h)[...] = ((late_ref[LATE.index(op)] if op in LATE else mixed_ref[EARLY.index(op)]) * inverse).astype(LOW)
        raw = dot(grad, head(v_ref, h)[...], ((1,), (1,)))
        coefs = jnp.where(mask, raw, 0.0).astype(LOW)
        query = dot(coefs, head(k_ref, h)[...], ((1,), (0,))) + dot(grad, p_ref[...], ((1,), (1,)))
        head(query_ref, h)[...] = query.astype(LOW)
        head(key_ref, h)[...] = dot(coefs, head(q_ref, h)[...], ((0,), (0,)))
        head(value_ref, h)[...] = dot(scores_ref[h], grad, ((0,), (0,)))


def grads_of(k_ref, v_ref, key_local, value_local, suffix, h):
    key = head(key_local, h)[...] + dot(head(v_ref, h)[...], suffix, ((1,), (1,)))
    value = head(value_local, h)[...] + dot(head(k_ref, h)[...], suffix, ((1,), (0,)))
    return key.astype(LOW), value.astype(LOW)


def early_kernel(k_ref, v_ref, key_local, value_local, p0, p1, key_ref, value_ref):
    for n, (op, p_ref) in enumerate(zip(EARLY, (p0, p1))):
        h = came(BACK_GRAD, op)
        key_ref[n], value_ref[n] = grads_of(k_ref, v_ref, key_local, value_local, p_ref[...], h)


def last_kernel(k_ref, v_ref, key_local, value_local, p2, p3, key_early, value_early, key_ref, value_ref):
    for n, op in enumerate(EARLY):
        h = came(BACK_GRAD, op)
        head(key_ref, h)[...] = key_early[n]
        head(value_ref, h)[...] = value_early[n]
    for op, p_ref in zip(LATE, (p2, p3)):
        h = came(BACK_GRAD, op)
        key, value = grads_of(k_ref, v_ref, key_local, value_local, p_ref[...], h)
        head(key_ref, h)[...] = key
        head(value_ref, h)[...] = value


def quad_steps(quads, before):
    return (2, 3, 1) if quads == 4 and before else range(quads - 1, 0, -1)


def quad_targets(quads, step, before):
    targets = [z ^ step for z in range(quads)]
    if quads == 4 and step == 3:
        targets = [3, 2, 0, 1] if before else [2, 3, 1, 0]
    return targets


def sums_kernel(before, quads, *refs):
    index = lax.axis_index("seq")
    quad = index // QUAD
    first, back = (FIRST, BACK) if before else (FIRST_GRAD, BACK_GRAD)
    held, got, outs = refs[:QUAD], refs[QUAD : QUAD + quads - 1], refs[-QUAD:]

    def counts(a, b):
        return jnp.where(a < b if before else a > b, 1.0, 0.0).astype(WIDE)

    outer = jnp.zeros((DH, DH), WIDE)
    for step, total in zip(quad_steps(quads, before), got):
        outer = outer + total[...].astype(WIDE) * counts(quad ^ step, quad)
    pieces = [piece[...].astype(WIDE) for piece in held]
    for to in OPS:
        inner = outer
        for op in OPS:
            inner = inner + pieces[op] * counts(came(first, op), sent(back, to))
        outs[to][...] = inner.astype(LOW)


def exchange(value, axis, bits):
    size = lax.axis_size(axis)
    return lax.ppermute(value, axis, [(i, i ^ bits) for i in range(size)])


def cross(value, wave, op):
    cores = lax.axis_size("tp")
    pairs = []
    for i in range(lax.axis_size("seq")):
        for t in range(cores):
            member = targets(wave, t % 2, op)[i % QUAD]
            pairs.append((i * cores + t, (i - i % QUAD + member) * cores + (t ^ 1)))
    return lax.ppermute(value, ("seq", "tp"), pairs)


def exclusive_sum(held, before, *after):
    first, back = (FIRST, BACK) if before else (FIRST_GRAD, BACK_GRAD)
    held = [cross(held[op], first, op) for op in OPS]
    total = sum(piece.astype(WIDE) for piece in held).astype(LOW)
    quads = lax.axis_size("seq") // QUAD
    got = []
    for step in quad_steps(quads, before):
        targets = quad_targets(quads, step, before)
        pairs = [(z * QUAD + i, targets[z] * QUAD + i) for z in range(quads) for i in range(QUAD)]
        got.append(lax.ppermute(total, "seq", pairs))
    vmem = [pl.BlockSpec(memory_space=pltpu.VMEM)] * (QUAD + len(got))
    sums = call(
        functools.partial(sums_kernel, before, quads),
        [jax.ShapeDtypeStruct(x.shape, x.dtype) for x in held],
        (*held, *got, *after),
        0,
        in_specs=vmem + [pl.BlockSpec(memory_space=pl.ANY)] * len(after),
    )
    return [cross(sums[op], back, op) for op in OPS]


def sum_over_heads(value):
    bit = 1
    while bit < lax.axis_size("tp"):
        value = value + exchange(value, "tp", bit)
        bit *= 2
    return value


def body(q, k, v, c):
    count, width = q.shape
    features = width * lax.axis_size("tp")
    shape = jax.ShapeDtypeStruct
    state = shape((DH, DH), LOW)
    wide = shape((count, width), WIDE)
    low = shape((count, width), LOW)
    unit = 2 * count * DH * DH * QUAD
    buffers = [pltpu.VMEM(k.shape, LOW)] * 2 + [pltpu.SemaphoreType.DMA((2, CHUNKS))]
    held = call(
        state_kernel, [state] * QUAD, (k, v), unit, room=53.75,
        in_specs=[pl.BlockSpec(memory_space=pltpu.HBM)] * 2,
        scratch_shapes=buffers,
    )
    scores, local, turned = call(
        local_kernel,
        [shape((QUAD, count, count), LOW), wide, shape((QUAD, DH, count), LOW)],
        (q, k, v),
        4 * unit,
    )
    prefix = exclusive_sum(held, True)
    part = shape((count, DH), WIDE)
    mixed, square, product = call(
        functools.partial(mixed_kernel, EARLY),
        [shape((2, count, DH), WIDE), part, part],
        (local, q, c, *[prefix[op] for op in EARLY]),
        unit,
    )
    late, sums = call(
        sums_of_tokens_kernel,
        [shape((2, count, DH), WIDE), shape((2, count), WIDE)],
        (local, q, c, *[prefix[op] for op in LATE], square, product),
        unit,
    )
    sums = sum_over_heads(sums)
    *terms, g = call(
        functools.partial(grad_kernel, features),
        [state] * QUAD + [low],
        (mixed, late, c, turned, sums),
        unit,
        scratch_shapes=[pltpu.VMEM((QUAD, DH, DH), LOW)],
    )
    normed_out, query_grad, key_local, value_local = call(
        functools.partial(back_kernel, features),
        [low, low, wide, wide],
        (q, k, v, g, scores, mixed, late, sums, *prefix),
        9 * unit,
    )
    suffix = exclusive_sum(terms, False, key_local)
    early = shape((2, count, DH), LOW)
    key_early, value_early = call(
        early_kernel, [early] * 2, (k, v, key_local, value_local, *[suffix[op] for op in EARLY]), 2 * unit
    )
    key_grad, value_grad = call(
        last_kernel, [low, low], (k, v, key_local, value_local, *[suffix[op] for op in LATE], key_early, value_early), unit
    )
    return (normed_out, query_grad, key_grad, value_grad)


def solution(mesh):
    spec = P("seq", "tp")
    return jax.shard_map(body, mesh=mesh, in_specs=(spec,) * 4, out_specs=(spec,) * 4, check_vma=False)
```

```python
import functools

import jax
import jax.numpy as jnp
from jax import lax
from jax.experimental import pallas as pl
from jax.experimental.pallas import tpu as pltpu
from jax.sharding import PartitionSpec as P

DH = 128
EPSILON = 1e-06
QUAD = 4
OPS = (0, 1, 2, 3)
CHUNKS = 2
LOW, WIDE = jnp.bfloat16, jnp.float32


def dot(a, b, contract):
    return lax.dot_general(a, b, ((contract[0], contract[1]), ((), ())), preferred_element_type=WIDE)


def head(ref, h):
    return ref.at[:, pl.ds(pl.multiple_of(h * DH, DH), DH)]


def fixed(ref, h):
    return ref.at[:, h * DH : (h + 1) * DH]


def causal_mask(count):
    row = lax.broadcasted_iota(jnp.int32, (count, count), 0)
    col = lax.broadcasted_iota(jnp.int32, (count, count), 1)
    return row >= col


def member_of_quad():
    return lax.axis_index("seq") % QUAD


FIRST = (((3, 2, 1, 0), (1, 3, 0, 2), (2, 0, 3, 1)), ((2, 3, 1, 0), (3, 2, 0, 1), (1, 0, 3, 2)))
BACK = (((3, 2, 1, 0), (2, 3, 0, 1), (1, 0, 3, 2)), ((3, 2, 0, 1), (2, 3, 1, 0), (1, 0, 3, 2)))
FIRST_GRAD = (((3, 2, 1, 0), (2, 3, 0, 1), (1, 0, 3, 2)), ((3, 2, 1, 0), (1, 0, 3, 2), (2, 3, 0, 1)))
BACK_GRAD = (((3, 2, 1, 0), (2, 3, 0, 1), (1, 0, 3, 2)), ((2, 3, 0, 1), (1, 2, 3, 0), (3, 0, 1, 2)))
SAME = (0, 1, 2, 3)
EARLY, LATE = (0, 1), (2, 3)


def targets(wave, odd, op):
    return SAME if op == 3 else wave[odd][op]


def look_up(table):
    packed = 0
    for odd in range(2):
        for member in range(QUAD):
            packed |= table[odd][member] << 2 * (QUAD * odd + member)
    place = QUAD * (lax.axis_index("tp") % 2) + member_of_quad()
    return (packed >> (2 * place)) & 3


def sent(wave, op):
    return look_up([targets(wave, odd, op) for odd in range(2)])


def came(wave, op):
    return look_up([[targets(wave, 1 - odd, op).index(m) for m in SAME] for odd in range(2)])


def call(kernel, outs, args, flops, in_specs=None, out_specs=None, scratch_shapes=(), room=32):
    size = sum(x.size * x.dtype.itemsize for x in list(args) + list(outs))
    return pl.pallas_call(
        kernel,
        out_shape=outs,
        in_specs=in_specs or [pl.BlockSpec(memory_space=pltpu.VMEM)] * len(args),
        out_specs=out_specs or [pl.BlockSpec(memory_space=pltpu.VMEM)] * len(outs),
        scratch_shapes=scratch_shapes,
        cost_estimate=pl.CostEstimate(flops=flops, bytes_accessed=size, transcendentals=0),
        compiler_params=pltpu.CompilerParams(vmem_limit_bytes=int(room * 1024 * 1024)),
    )(*args)


def state_kernel(k_ref, v_ref, o0, o1, o2, o3, k_buf, v_buf, sems):
    rows = k_ref.shape[0] // CHUNKS
    copies = []
    for i in range(CHUNKS):
        for n, (ref, buf) in enumerate(((k_ref, k_buf), (v_ref, v_buf))):
            part = pl.ds(i * rows, rows)
            copies.append(pltpu.make_async_copy(ref.at[part], buf.at[part], sems.at[n, i]))
            copies[-1].start()
    states = [0.0] * QUAD
    half = rows * CHUNKS // 2
    for part in range(2):
        for copy in copies[part * CHUNKS : (part + 1) * CHUNKS]:
            copy.wait()
        tokens = pl.ds(part * half, half)
        for op in OPS:
            cols = pl.ds(pl.multiple_of(sent(FIRST, op) * DH, DH), DH)
            states[op] = states[op] + dot(k_buf[tokens, cols], v_buf[tokens, cols], ((0,), (0,)))
    for op, out in enumerate((o0, o1, o2, o3)):
        out[...] = states[op].astype(LOW)


def local_kernel(q_ref, k_ref, v_ref, scores_ref, mixed_ref, turned_ref):
    mask = causal_mask(q_ref.shape[0])
    for h in range(QUAD):
        turned_ref[h] = fixed(q_ref, h)[...].T
        raw = dot(fixed(q_ref, h)[...], fixed(k_ref, h)[...], ((1,), (1,)))
        scores = jnp.where(mask, raw, 0.0).astype(LOW)
        scores_ref[h] = scores
        fixed(mixed_ref, h)[...] = dot(scores, fixed(v_ref, h)[...], ((1,), (0,)))


def mixed_kernel(ops, *refs):
    local_ref, q_ref, c_ref = refs[:3]
    mixed_ref, square_ref, product_ref = refs[-3:]
    for n, op in enumerate(ops):
        h = came(BACK, op)
        mixed = head(local_ref, h)[...] + dot(head(q_ref, h)[...], refs[3 + n][...], ((1,), (0,)))
        mixed_ref[n] = mixed
        square = mixed * mixed
        product = mixed * head(c_ref, h)[...].astype(WIDE)
        square_ref[...] = square if n == 0 else square_ref[...] + square
        product_ref[...] = product if n == 0 else product_ref[...] + product


def sums_of_tokens_kernel(local_ref, q_ref, c_ref, p2, p3, square_ref, product_ref, mixed_ref, sums_ref):
    square, product = square_ref[...], product_ref[...]
    for n, (op, p_ref) in enumerate(zip(LATE, (p2, p3))):
        h = came(BACK, op)
        mixed = head(local_ref, h)[...] + dot(head(q_ref, h)[...], p_ref[...], ((1,), (0,)))
        mixed_ref[n] = mixed
        square = square + mixed * mixed
        product = product + mixed * head(c_ref, h)[...].astype(WIDE)
    sums_ref[0:1, :] = jnp.sum(square.T, axis=0, keepdims=True)
    sums_ref[1:2, :] = jnp.sum(product.T, axis=0, keepdims=True)


def token_scales(sums_ref, features, count):
    inverse = lax.rsqrt(sums_ref[0:1, :] * (1.0 / features) + EPSILON)
    projection = inverse * sums_ref[1:2, :] * (1.0 / features)
    inverse = jnp.broadcast_to(inverse, (DH, count)).T
    projection = jnp.broadcast_to(projection, (DH, count)).T
    return inverse, projection


def grad_kernel(features, mixed_ref, late_ref, c_ref, turned_ref, sums_ref, o0, o1, o2, o3, g_ref, terms_ref):
    count = c_ref.shape[0]
    inverse = lax.rsqrt(sums_ref[0:1, :] * (1.0 / features) + EPSILON)
    share = inverse * inverse * (inverse * sums_ref[1:2, :] * (1.0 / features))
    inverse = jnp.broadcast_to(inverse, (DH, count)).T
    share = jnp.broadcast_to(share, (DH, count)).T
    for op in EARLY + LATE:
        h = came(BACK, op)
        mixed = late_ref[LATE.index(op)] if op in LATE else mixed_ref[EARLY.index(op)]
        grad = (inverse * head(c_ref, h)[...].astype(WIDE) - share * mixed).astype(LOW)
        head(g_ref, h)[...] = grad
        terms_ref[h] = dot(turned_ref[h], grad, ((1,), (0,))).astype(LOW)
    for op, out in enumerate((o0, o1, o2, o3)):
        out[...] = terms_ref[sent(FIRST_GRAD, op)]


def back_kernel(features, q_ref, k_ref, v_ref, g_ref, scores_ref, mixed_ref, late_ref, sums_ref, p0, p1, p2, p3,
                normed_ref, query_ref, key_ref, value_ref):
    count = q_ref.shape[0]
    mask = causal_mask(count)
    inverse, _ = token_scales(sums_ref, features, count)
    for op, p_ref in enumerate((p0, p1, p2, p3)):
        h = came(BACK, op)
        grad = head(g_ref, h)[...]
        head(normed_ref, h)[...] = ((late_ref[LATE.index(op)] if op in LATE else mixed_ref[EARLY.index(op)]) * inverse).astype(LOW)
        raw = dot(grad, head(v_ref, h)[...], ((1,), (1,)))
        coefs = jnp.where(mask, raw, 0.0).astype(LOW)
        query = dot(coefs, head(k_ref, h)[...], ((1,), (0,))) + dot(grad, p_ref[...], ((1,), (1,)))
        head(query_ref, h)[...] = query.astype(LOW)
        head(key_ref, h)[...] = dot(coefs, head(q_ref, h)[...], ((0,), (0,)))
        head(value_ref, h)[...] = dot(scores_ref[h], grad, ((0,), (0,)))


def grads_of(k_ref, v_ref, key_local, value_local, suffix, h):
    key = head(key_local, h)[...] + dot(head(v_ref, h)[...], suffix, ((1,), (1,)))
    value = head(value_local, h)[...] + dot(head(k_ref, h)[...], suffix, ((1,), (0,)))
    return key.astype(LOW), value.astype(LOW)


def early_kernel(k_ref, v_ref, key_local, value_local, p0, p1, key_ref, value_ref):
    for n, (op, p_ref) in enumerate(zip(EARLY, (p0, p1))):
        h = came(BACK_GRAD, op)
        key_ref[n], value_ref[n] = grads_of(k_ref, v_ref, key_local, value_local, p_ref[...], h)


def last_kernel(k_ref, v_ref, key_local, value_local, p2, p3, key_early, value_early, key_ref, value_ref):
    for n, op in enumerate(EARLY):
        h = came(BACK_GRAD, op)
        head(key_ref, h)[...] = key_early[n]
        head(value_ref, h)[...] = value_early[n]
    for op, p_ref in zip(LATE, (p2, p3)):
        h = came(BACK_GRAD, op)
        key, value = grads_of(k_ref, v_ref, key_local, value_local, p_ref[...], h)
        head(key_ref, h)[...] = key
        head(value_ref, h)[...] = value


def quad_steps(quads, before):
    return (2, 3, 1) if quads == 4 and before else range(quads - 1, 0, -1)


def quad_targets(quads, step, before):
    targets = [z ^ step for z in range(quads)]
    if quads == 4 and step == 3:
        targets = [3, 2, 0, 1] if before else [2, 3, 1, 0]
    return targets


def sums_kernel(before, quads, *refs):
    index = lax.axis_index("seq")
    quad = index // QUAD
    first, back = (FIRST, BACK) if before else (FIRST_GRAD, BACK_GRAD)
    held, got, outs = refs[:QUAD], refs[QUAD : QUAD + quads - 1], refs[-QUAD:]

    def counts(a, b):
        return jnp.where(a < b if before else a > b, 1.0, 0.0).astype(WIDE)

    outer = jnp.zeros((DH, DH), WIDE)
    for step, total in zip(quad_steps(quads, before), got):
        outer = outer + total[...].astype(WIDE) * counts(quad ^ step, quad)
    pieces = [piece[...].astype(WIDE) for piece in held]
    for to in OPS:
        inner = outer
        for op in OPS:
            inner = inner + pieces[op] * counts(came(first, op), sent(back, to))
        outs[to][...] = inner.astype(LOW)


def exchange(value, axis, bits):
    size = lax.axis_size(axis)
    return lax.ppermute(value, axis, [(i, i ^ bits) for i in range(size)])


def cross(value, wave, op):
    cores = lax.axis_size("tp")
    pairs = []
    for i in range(lax.axis_size("seq")):
        for t in range(cores):
            member = targets(wave, t % 2, op)[i % QUAD]
            pairs.append((i * cores + t, (i - i % QUAD + member) * cores + (t ^ 1)))
    return lax.ppermute(value, ("seq", "tp"), pairs)


def exclusive_sum(held, before, *after):
    first, back = (FIRST, BACK) if before else (FIRST_GRAD, BACK_GRAD)
    held = [cross(held[op], first, op) for op in OPS]
    total = sum(piece.astype(WIDE) for piece in held).astype(LOW)
    quads = lax.axis_size("seq") // QUAD
    got = []
    for step in quad_steps(quads, before):
        targets = quad_targets(quads, step, before)
        pairs = [(z * QUAD + i, targets[z] * QUAD + i) for z in range(quads) for i in range(QUAD)]
        got.append(lax.ppermute(total, "seq", pairs))
    vmem = [pl.BlockSpec(memory_space=pltpu.VMEM)] * (QUAD + len(got))
    sums = call(
        functools.partial(sums_kernel, before, quads),
        [jax.ShapeDtypeStruct(x.shape, x.dtype) for x in held],
        (*held, *got, *after),
        0,
        in_specs=vmem + [pl.BlockSpec(memory_space=pl.ANY)] * len(after),
    )
    return [cross(sums[op], back, op) for op in OPS]


def sum_over_heads(value):
    bit = 1
    while bit < lax.axis_size("tp"):
        value = value + exchange(value, "tp", bit)
        bit *= 2
    return value


def body(q, k, v, c):
    count, width = q.shape
    features = width * lax.axis_size("tp")
    shape = jax.ShapeDtypeStruct
    state = shape((DH, DH), LOW)
    wide = shape((count, width), WIDE)
    low = shape((count, width), LOW)
    unit = 2 * count * DH * DH * QUAD
    buffers = [pltpu.VMEM(k.shape, LOW)] * 2 + [pltpu.SemaphoreType.DMA((2, CHUNKS))]
    held = call(
        state_kernel, [state] * QUAD, (k, v), unit, room=53.75,
        in_specs=[pl.BlockSpec(memory_space=pltpu.HBM)] * 2,
        scratch_shapes=buffers,
    )
    scores, local, turned = call(
        local_kernel,
        [shape((QUAD, count, count), LOW), wide, shape((QUAD, DH, count), LOW)],
        (q, k, v),
        4 * unit,
    )
    prefix = exclusive_sum(held, True)
    part = shape((count, DH), WIDE)
    mixed, square, product = call(
        functools.partial(mixed_kernel, EARLY),
        [shape((2, count, DH), WIDE), part, part],
        (local, q, c, *[prefix[op] for op in EARLY]),
        unit,
    )
    late, sums = call(
        sums_of_tokens_kernel,
        [shape((2, count, DH), WIDE), shape((2, count), WIDE)],
        (local, q, c, *[prefix[op] for op in LATE], square, product),
        unit,
    )
    sums = sum_over_heads(sums)
    *terms, g = call(
        functools.partial(grad_kernel, features),
        [state] * QUAD + [low],
        (mixed, late, c, turned, sums),
        unit,
        scratch_shapes=[pltpu.VMEM((QUAD, DH, DH), LOW)],
    )
    normed_out, query_grad, key_local, value_local = call(
        functools.partial(back_kernel, features),
        [low, low, wide, wide],
        (q, k, v, g, scores, mixed, late, sums, *prefix),
        9 * unit,
    )
    suffix = exclusive_sum(terms, False, key_local)
    early = shape((2, count, DH), LOW)
    key_early, value_early = call(
        early_kernel, [early] * 2, (k, v, key_local, value_local, *[suffix[op] for op in EARLY]), 2 * unit
    )
    key_grad, value_grad = call(
        last_kernel, [low, low], (k, v, key_local, value_local, *[suffix[op] for op in LATE], key_early, value_early), unit
    )
    return (normed_out, query_grad, key_grad, value_grad)


def solution(mesh):
    spec = P("seq", "tp")
    return jax.shard_map(body, mesh=mesh, in_specs=(spec,) * 4, out_specs=(spec,) * 4, check_vma=False)
```

```python
import functools

import jax
import jax.numpy as jnp
from jax import lax
from jax.experimental import pallas as pl
from jax.experimental.pallas import tpu as pltpu
from jax.sharding import PartitionSpec as P

DH = 128
EPSILON = 1e-06
QUAD = 4
OPS = (0, 1, 2, 3)
CHUNKS = 4
LOW, WIDE = jnp.bfloat16, jnp.float32


def dot(a, b, contract):
    return lax.dot_general(a, b, ((contract[0], contract[1]), ((), ())), preferred_element_type=WIDE)


def head(ref, h):
    return ref.at[:, pl.ds(pl.multiple_of(h * DH, DH), DH)]


def fixed(ref, h):
    return ref.at[:, h * DH : (h + 1) * DH]


def causal_mask(count):
    row = lax.broadcasted_iota(jnp.int32, (count, count), 0)
    col = lax.broadcasted_iota(jnp.int32, (count, count), 1)
    return row >= col


def member_of_quad():
    return lax.axis_index("seq") % QUAD


FIRST = (((3, 2, 1, 0), (1, 3, 0, 2), (2, 0, 3, 1)), ((2, 3, 1, 0), (3, 2, 0, 1), (1, 0, 3, 2)))
BACK = (((3, 2, 1, 0), (2, 3, 0, 1), (1, 0, 3, 2)), ((3, 2, 0, 1), (2, 3, 1, 0), (1, 0, 3, 2)))
FIRST_GRAD = (((3, 2, 1, 0), (2, 3, 0, 1), (1, 0, 3, 2)), ((3, 2, 1, 0), (1, 0, 3, 2), (2, 3, 0, 1)))
BACK_GRAD = (((3, 2, 1, 0), (2, 3, 0, 1), (1, 0, 3, 2)), ((2, 3, 0, 1), (1, 2, 3, 0), (3, 0, 1, 2)))
SAME = (0, 1, 2, 3)


def targets(wave, odd, op):
    return SAME if op == 3 else wave[odd][op]


def look_up(table):
    packed = 0
    for odd in range(2):
        for member in range(QUAD):
            packed |= table[odd][member] << 2 * (QUAD * odd + member)
    place = QUAD * (lax.axis_index("tp") % 2) + member_of_quad()
    return (packed >> (2 * place)) & 3


def sent(wave, op):
    return look_up([targets(wave, odd, op) for odd in range(2)])


def came(wave, op):
    return look_up([[targets(wave, 1 - odd, op).index(m) for m in SAME] for odd in range(2)])


def call(kernel, outs, args, flops, in_specs=None, out_specs=None, scratch_shapes=(), room=32):
    size = sum(x.size * x.dtype.itemsize for x in list(args) + list(outs))
    return pl.pallas_call(
        kernel,
        out_shape=outs,
        in_specs=in_specs or [pl.BlockSpec(memory_space=pltpu.VMEM)] * len(args),
        out_specs=out_specs or [pl.BlockSpec(memory_space=pltpu.VMEM)] * len(outs),
        scratch_shapes=scratch_shapes,
        cost_estimate=pl.CostEstimate(flops=flops, bytes_accessed=size, transcendentals=0),
        compiler_params=pltpu.CompilerParams(vmem_limit_bytes=int(room * 1024 * 1024)),
    )(*args)


def state_kernel(k_ref, v_ref, o0, o1, o2, o3, k_buf, v_buf, sems):
    rows = k_ref.shape[0] // CHUNKS
    copies = []
    for i in range(CHUNKS):
        for n, (ref, buf) in enumerate(((k_ref, k_buf), (v_ref, v_buf))):
            part = pl.ds(i * rows, rows)
            copies.append(pltpu.make_async_copy(ref.at[part], buf.at[part], sems.at[n, i]))
            copies[-1].start()
    states = [0.0] * QUAD
    half = rows * CHUNKS // 2
    for part in range(2):
        for copy in copies[part * CHUNKS : (part + 1) * CHUNKS]:
            copy.wait()
        tokens = pl.ds(part * half, half)
        for op in OPS:
            cols = pl.ds(pl.multiple_of(sent(FIRST, op) * DH, DH), DH)
            states[op] = states[op] + dot(k_buf[tokens, cols], v_buf[tokens, cols], ((0,), (0,)))
    for op, out in enumerate((o0, o1, o2, o3)):
        out[...] = states[op].astype(LOW)


def local_kernel(q_ref, k_ref, v_ref, scores_ref, mixed_ref, turned_ref):
    mask = causal_mask(q_ref.shape[0])
    for h in range(QUAD):
        turned_ref[h] = fixed(q_ref, h)[...].T
        raw = dot(fixed(q_ref, h)[...], fixed(k_ref, h)[...], ((1,), (1,)))
        scores = jnp.where(mask, raw, 0.0).astype(LOW)
        scores_ref[h] = scores
        fixed(mixed_ref, h)[...] = dot(scores, fixed(v_ref, h)[...], ((1,), (0,)))


def mixed_kernel(local_ref, q_ref, c_ref, p0, p1, p2, p3, mixed_ref, sums_ref):
    count = q_ref.shape[0]
    square = jnp.zeros((count, DH), WIDE)
    product = jnp.zeros((count, DH), WIDE)
    for op, p_ref in enumerate((p0, p1, p2, p3)):
        h = came(BACK, op)
        mixed = head(local_ref, h)[...] + dot(head(q_ref, h)[...], p_ref[...], ((1,), (0,)))
        head(mixed_ref, h)[...] = mixed
        square = square + mixed * mixed
        product = product + mixed * head(c_ref, h)[...].astype(WIDE)
    sums_ref[0:1, :] = jnp.sum(square.T, axis=0, keepdims=True)
    sums_ref[1:2, :] = jnp.sum(product.T, axis=0, keepdims=True)


def token_scales(sums_ref, features, count):
    inverse = lax.rsqrt(sums_ref[0:1, :] * (1.0 / features) + EPSILON)
    projection = inverse * sums_ref[1:2, :] * (1.0 / features)
    inverse = jnp.broadcast_to(inverse, (DH, count)).T
    projection = jnp.broadcast_to(projection, (DH, count)).T
    return inverse, projection


def grad_kernel(features, mixed_ref, c_ref, turned_ref, sums_ref, o0, o1, o2, o3, g_ref):
    count = c_ref.shape[0]
    inverse = lax.rsqrt(sums_ref[0:1, :] * (1.0 / features) + EPSILON)
    share = inverse * inverse * (inverse * sums_ref[1:2, :] * (1.0 / features))
    inverse = jnp.broadcast_to(inverse, (DH, count)).T
    share = jnp.broadcast_to(share, (DH, count)).T
    for op, out in enumerate((o0, o1, o2, o3)):
        h = sent(FIRST_GRAD, op)
        grad = (inverse * head(c_ref, h)[...].astype(WIDE) - share * head(mixed_ref, h)[...]).astype(LOW)
        head(g_ref, h)[...] = grad
        out[...] = dot(turned_ref[h], grad, ((1,), (0,))).astype(LOW)


def back_kernel(features, q_ref, k_ref, v_ref, g_ref, scores_ref, mixed_ref, sums_ref, p0, p1, p2, p3,
                normed_ref, query_ref, key_ref, value_ref):
    count = q_ref.shape[0]
    mask = causal_mask(count)
    inverse, _ = token_scales(sums_ref, features, count)
    for op, p_ref in enumerate((p0, p1, p2, p3)):
        h = came(BACK, op)
        grad = head(g_ref, h)[...]
        head(normed_ref, h)[...] = (head(mixed_ref, h)[...] * inverse).astype(LOW)
        raw = dot(grad, head(v_ref, h)[...], ((1,), (1,)))
        coefs = jnp.where(mask, raw, 0.0).astype(LOW)
        query = dot(coefs, head(k_ref, h)[...], ((1,), (0,))) + dot(grad, p_ref[...], ((1,), (1,)))
        head(query_ref, h)[...] = query.astype(LOW)
        head(key_ref, h)[...] = dot(coefs, head(q_ref, h)[...], ((0,), (0,)))
        head(value_ref, h)[...] = dot(scores_ref[h], grad, ((0,), (0,)))


def last_kernel(k_ref, v_ref, key_local, value_local, p0, p1, p2, p3, key_ref, value_ref):
    for op, p_ref in enumerate((p0, p1, p2, p3)):
        h = came(BACK_GRAD, op)
        suffix = p_ref[...]
        key = head(key_local, h)[...] + dot(head(v_ref, h)[...], suffix, ((1,), (1,)))
        head(key_ref, h)[...] = key.astype(LOW)
        value = head(value_local, h)[...] + dot(head(k_ref, h)[...], suffix, ((1,), (0,)))
        head(value_ref, h)[...] = value.astype(LOW)


def ring(quads, before):
    return quads == 4 and before


def quad_steps(quads, before):
    return (1, 2, 3) if ring(quads, before) else range(quads - 1, 0, -1)


def quad_targets(quads, step, before):
    if ring(quads, before):
        return [(z + step) % quads for z in range(quads)]
    return [2, 3, 1, 0] if quads == 4 and step == 3 else [z ^ step for z in range(quads)]


def quad_source(quads, step, before, quad):
    return (quad + quads - step) % quads if ring(quads, before) else quad ^ step


def sums_kernel(before, quads, *refs):
    index = lax.axis_index("seq")
    quad = index // QUAD
    first, back = (FIRST, BACK) if before else (FIRST_GRAD, BACK_GRAD)
    held, got, outs = refs[:QUAD], refs[QUAD : QUAD + quads - 1], refs[-QUAD:]

    def counts(a, b):
        return jnp.where(a < b if before else a > b, 1.0, 0.0).astype(WIDE)

    outer = jnp.zeros((DH, DH), WIDE)
    for step, total in zip(quad_steps(quads, before), got):
        outer = outer + total[...].astype(WIDE) * counts(quad_source(quads, step, before, quad), quad)
    pieces = [piece[...].astype(WIDE) for piece in held]
    for to in OPS:
        inner = outer
        for op in OPS:
            inner = inner + pieces[op] * counts(came(first, op), sent(back, to))
        outs[to][...] = inner.astype(LOW)


def exchange(value, axis, bits):
    size = lax.axis_size(axis)
    return lax.ppermute(value, axis, [(i, i ^ bits) for i in range(size)])


def cross(value, wave, op):
    cores = lax.axis_size("tp")
    pairs = []
    for i in range(lax.axis_size("seq")):
        for t in range(cores):
            member = targets(wave, t % 2, op)[i % QUAD]
            pairs.append((i * cores + t, (i - i % QUAD + member) * cores + (t ^ 1)))
    return lax.ppermute(value, ("seq", "tp"), pairs)


def exclusive_sum(held, before, *after):
    first, back = (FIRST, BACK) if before else (FIRST_GRAD, BACK_GRAD)
    held = [cross(held[op], first, op) for op in OPS]
    total = sum(piece.astype(WIDE) for piece in held).astype(LOW)
    quads = lax.axis_size("seq") // QUAD
    got = []
    for step in quad_steps(quads, before):
        targets = quad_targets(quads, step, before)
        pairs = [(z * QUAD + i, targets[z] * QUAD + i) for z in range(quads) for i in range(QUAD)]
        got.append(lax.ppermute(total, "seq", pairs))
    vmem = [pl.BlockSpec(memory_space=pltpu.VMEM)] * (QUAD + len(got))
    sums = call(
        functools.partial(sums_kernel, before, quads),
        [jax.ShapeDtypeStruct(x.shape, x.dtype) for x in held],
        (*held, *got, *after),
        0,
        in_specs=vmem + [pl.BlockSpec(memory_space=pl.ANY)] * len(after),
    )
    return [cross(sums[op], back, op) for op in OPS]


def sum_over_heads(value):
    bit = 1
    while bit < lax.axis_size("tp"):
        value = value + exchange(value, "tp", bit)
        bit *= 2
    return value


def body(q, k, v, c):
    count, width = q.shape
    features = width * lax.axis_size("tp")
    shape = jax.ShapeDtypeStruct
    state = shape((DH, DH), LOW)
    wide = shape((count, width), WIDE)
    low = shape((count, width), LOW)
    unit = 2 * count * DH * DH * QUAD
    buffers = [pltpu.VMEM(k.shape, LOW)] * 2 + [pltpu.SemaphoreType.DMA((2, CHUNKS))]
    held = call(
        state_kernel, [state] * QUAD, (k, v), unit, room=53.75,
        in_specs=[pl.BlockSpec(memory_space=pltpu.HBM)] * 2,
        scratch_shapes=buffers,
    )
    scores, local, turned = call(
        local_kernel,
        [shape((QUAD, count, count), LOW), wide, shape((QUAD, DH, count), LOW)],
        (q, k, v),
        4 * unit,
    )
    prefix = exclusive_sum(held, True)
    mixed, sums = call(
        mixed_kernel, [wide, shape((2, count), WIDE)], (local, q, c, *prefix), unit
    )
    sums = sum_over_heads(sums)
    *terms, g = call(
        functools.partial(grad_kernel, features), [state] * QUAD + [low], (mixed, c, turned, sums), unit
    )
    normed_out, query_grad, key_local, value_local = call(
        functools.partial(back_kernel, features),
        [low, low, wide, wide],
        (q, k, v, g, scores, mixed, sums, *prefix),
        9 * unit,
    )
    suffix = exclusive_sum(terms, False, key_local)
    key_grad, value_grad = call(
        last_kernel, [low, low], (k, v, key_local, value_local, *suffix), 2 * unit
    )
    return (normed_out, query_grad, key_grad, value_grad)


def solution(mesh):
    spec = P("seq", "tp")
    return jax.shard_map(body, mesh=mesh, in_specs=(spec,) * 4, out_specs=(spec,) * 4, check_vma=False)
```

```python
import functools

import jax
import jax.numpy as jnp
from jax import lax
from jax.experimental import pallas as pl
from jax.experimental.pallas import tpu as pltpu
from jax.sharding import PartitionSpec as P

DH = 128
EPSILON = 1e-06
QUAD = 4
OPS = (0, 1, 2, 3)
CHUNKS = 2
LOW, WIDE = jnp.bfloat16, jnp.float32


def dot(a, b, contract):
    return lax.dot_general(a, b, ((contract[0], contract[1]), ((), ())), preferred_element_type=WIDE)


def head(ref, h):
    return ref.at[:, pl.ds(pl.multiple_of(h * DH, DH), DH)]


def fixed(ref, h):
    return ref.at[:, h * DH : (h + 1) * DH]


def causal_mask(count):
    row = lax.broadcasted_iota(jnp.int32, (count, count), 0)
    col = lax.broadcasted_iota(jnp.int32, (count, count), 1)
    return row >= col


def member_of_quad():
    return lax.axis_index("seq") % QUAD


FIRST = (((3, 2, 1, 0), (1, 0, 3, 2), (2, 3, 0, 1)), ((1, 2, 3, 0), (3, 0, 1, 2), (2, 3, 0, 1)))
BACK = (((3, 2, 1, 0), (2, 3, 0, 1), (1, 0, 3, 2)), ((3, 2, 0, 1), (2, 3, 1, 0), (1, 0, 3, 2)))
FIRST_GRAD = (((3, 2, 1, 0), (2, 3, 0, 1), (1, 0, 3, 2)), ((3, 2, 1, 0), (1, 0, 3, 2), (2, 3, 0, 1)))
BACK_GRAD = (((3, 2, 1, 0), (2, 3, 0, 1), (1, 0, 3, 2)), ((2, 3, 0, 1), (1, 2, 3, 0), (3, 0, 1, 2)))
SAME = (0, 1, 2, 3)
EARLY, LATE = (0, 1), (2, 3)


def targets(wave, odd, op):
    return SAME if op == 3 else wave[odd][op]


def look_up(table):
    packed = 0
    for odd in range(2):
        for member in range(QUAD):
            packed |= table[odd][member] << 2 * (QUAD * odd + member)
    place = QUAD * (lax.axis_index("tp") % 2) + member_of_quad()
    return (packed >> (2 * place)) & 3


def sent(wave, op):
    return look_up([targets(wave, odd, op) for odd in range(2)])


def came(wave, op):
    return look_up([[targets(wave, 1 - odd, op).index(m) for m in SAME] for odd in range(2)])


def call(kernel, outs, args, flops, in_specs=None, out_specs=None, scratch_shapes=(), room=32):
    size = sum(x.size * x.dtype.itemsize for x in list(args) + list(outs))
    return pl.pallas_call(
        kernel,
        out_shape=outs,
        in_specs=in_specs or [pl.BlockSpec(memory_space=pltpu.VMEM)] * len(args),
        out_specs=out_specs or [pl.BlockSpec(memory_space=pltpu.VMEM)] * len(outs),
        scratch_shapes=scratch_shapes,
        cost_estimate=pl.CostEstimate(flops=flops, bytes_accessed=size, transcendentals=0),
        compiler_params=pltpu.CompilerParams(vmem_limit_bytes=int(room * 1024 * 1024)),
    )(*args)


def state_kernel(k_ref, v_ref, o0, o1, o2, o3, k_buf, v_buf, sems):
    rows = k_ref.shape[0] // CHUNKS
    copies = []
    for i in range(CHUNKS):
        for n, (ref, buf) in enumerate(((k_ref, k_buf), (v_ref, v_buf))):
            part = pl.ds(i * rows, rows)
            copies.append(pltpu.make_async_copy(ref.at[part], buf.at[part], sems.at[n, i]))
            copies[-1].start()
    states = [0.0] * QUAD
    half = rows * CHUNKS // 2
    for part in range(2):
        for copy in copies[part * CHUNKS : (part + 1) * CHUNKS]:
            copy.wait()
        tokens = pl.ds(part * half, half)
        for op in OPS:
            cols = pl.ds(pl.multiple_of(sent(FIRST, op) * DH, DH), DH)
            states[op] = states[op] + dot(k_buf[tokens, cols], v_buf[tokens, cols], ((0,), (0,)))
    for op, out in enumerate((o0, o1, o2, o3)):
        out[...] = states[op].astype(LOW)


def local_kernel(q_ref, k_ref, v_ref, scores_ref, mixed_ref, turned_ref):
    mask = causal_mask(q_ref.shape[0])
    for h in range(QUAD):
        turned_ref[h] = fixed(q_ref, h)[...].T
        raw = dot(fixed(q_ref, h)[...], fixed(k_ref, h)[...], ((1,), (1,)))
        scores = jnp.where(mask, raw, 0.0).astype(LOW)
        scores_ref[h] = scores
        fixed(mixed_ref, h)[...] = dot(scores, fixed(v_ref, h)[...], ((1,), (0,)))


def mixed_kernel(ops, *refs):
    local_ref, q_ref, c_ref = refs[:3]
    mixed_ref, square_ref, product_ref = refs[-3:]
    for n, op in enumerate(ops):
        h = came(BACK, op)
        mixed = head(local_ref, h)[...] + dot(head(q_ref, h)[...], refs[3 + n][...], ((1,), (0,)))
        mixed_ref[n] = mixed
        square = mixed * mixed
        product = mixed * head(c_ref, h)[...].astype(WIDE)
        square_ref[...] = square if n == 0 else square_ref[...] + square
        product_ref[...] = product if n == 0 else product_ref[...] + product


def sums_of_tokens_kernel(local_ref, q_ref, c_ref, p2, p3, square_ref, product_ref, mixed_ref, sums_ref):
    square, product = square_ref[...], product_ref[...]
    for n, (op, p_ref) in enumerate(zip(LATE, (p2, p3))):
        h = came(BACK, op)
        mixed = head(local_ref, h)[...] + dot(head(q_ref, h)[...], p_ref[...], ((1,), (0,)))
        mixed_ref[n] = mixed
        square = square + mixed * mixed
        product = product + mixed * head(c_ref, h)[...].astype(WIDE)
    sums_ref[0:1, :] = jnp.sum(square.T, axis=0, keepdims=True)
    sums_ref[1:2, :] = jnp.sum(product.T, axis=0, keepdims=True)


def token_scales(sums_ref, features, count):
    inverse = lax.rsqrt(sums_ref[0:1, :] * (1.0 / features) + EPSILON)
    projection = inverse * sums_ref[1:2, :] * (1.0 / features)
    inverse = jnp.broadcast_to(inverse, (DH, count)).T
    projection = jnp.broadcast_to(projection, (DH, count)).T
    return inverse, projection


def grad_kernel(features, mixed_ref, late_ref, c_ref, turned_ref, sums_ref, o0, o1, o2, o3, g_ref, terms_ref):
    count = c_ref.shape[0]
    inverse = lax.rsqrt(sums_ref[0:1, :] * (1.0 / features) + EPSILON)
    share = inverse * inverse * (inverse * sums_ref[1:2, :] * (1.0 / features))
    inverse = jnp.broadcast_to(inverse, (DH, count)).T
    share = jnp.broadcast_to(share, (DH, count)).T
    for op in EARLY + LATE:
        h = came(BACK, op)
        mixed = late_ref[LATE.index(op)] if op in LATE else mixed_ref[EARLY.index(op)]
        grad = (inverse * head(c_ref, h)[...].astype(WIDE) - share * mixed).astype(LOW)
        head(g_ref, h)[...] = grad
        terms_ref[h] = dot(turned_ref[h], grad, ((1,), (0,))).astype(LOW)
    for op, out in enumerate((o0, o1, o2, o3)):
        out[...] = terms_ref[sent(FIRST_GRAD, op)]


def back_kernel(features, q_ref, k_ref, v_ref, g_ref, scores_ref, mixed_ref, late_ref, sums_ref, p0, p1, p2, p3,
                normed_ref, query_ref, key_ref, value_ref):
    count = q_ref.shape[0]
    mask = causal_mask(count)
    inverse, _ = token_scales(sums_ref, features, count)
    for op, p_ref in enumerate((p0, p1, p2, p3)):
        h = came(BACK, op)
        grad = head(g_ref, h)[...]
        head(normed_ref, h)[...] = ((late_ref[LATE.index(op)] if op in LATE else mixed_ref[EARLY.index(op)]) * inverse).astype(LOW)
        raw = dot(grad, head(v_ref, h)[...], ((1,), (1,)))
        coefs = jnp.where(mask, raw, 0.0).astype(LOW)
        query = dot(coefs, head(k_ref, h)[...], ((1,), (0,))) + dot(grad, p_ref[...], ((1,), (1,)))
        head(query_ref, h)[...] = query.astype(LOW)
        head(key_ref, h)[...] = dot(coefs, head(q_ref, h)[...], ((0,), (0,)))
        head(value_ref, h)[...] = dot(scores_ref[h], grad, ((0,), (0,)))


def grads_of(k_ref, v_ref, key_local, value_local, suffix, h):
    key = head(key_local, h)[...] + dot(head(v_ref, h)[...], suffix, ((1,), (1,)))
    value = head(value_local, h)[...] + dot(head(k_ref, h)[...], suffix, ((1,), (0,)))
    return key.astype(LOW), value.astype(LOW)


def early_kernel(k_ref, v_ref, key_local, value_local, p0, p1, key_ref, value_ref):
    for n, (op, p_ref) in enumerate(zip(EARLY, (p0, p1))):
        h = came(BACK_GRAD, op)
        key_ref[n], value_ref[n] = grads_of(k_ref, v_ref, key_local, value_local, p_ref[...], h)


def last_kernel(k_ref, v_ref, key_local, value_local, p2, p3, key_early, value_early, key_ref, value_ref):
    for n, op in enumerate(EARLY):
        h = came(BACK_GRAD, op)
        head(key_ref, h)[...] = key_early[n]
        head(value_ref, h)[...] = value_early[n]
    for op, p_ref in zip(LATE, (p2, p3)):
        h = came(BACK_GRAD, op)
        key, value = grads_of(k_ref, v_ref, key_local, value_local, p_ref[...], h)
        head(key_ref, h)[...] = key
        head(value_ref, h)[...] = value


def quad_steps(quads, before):
    return (2, 3, 1) if quads == 4 and before else range(quads - 1, 0, -1)


def quad_targets(quads, step, before):
    targets = [z ^ step for z in range(quads)]
    if quads == 4 and step == 3:
        targets = [3, 2, 0, 1] if before else [2, 3, 1, 0]
    return targets


def sums_kernel(before, quads, *refs):
    index = lax.axis_index("seq")
    quad = index // QUAD
    first, back = (FIRST, BACK) if before else (FIRST_GRAD, BACK_GRAD)
    held, got, outs = refs[:QUAD], refs[QUAD : QUAD + quads - 1], refs[-QUAD:]

    def counts(a, b):
        return jnp.where(a < b if before else a > b, 1.0, 0.0).astype(WIDE)

    outer = jnp.zeros((DH, DH), WIDE)
    for step, total in zip(quad_steps(quads, before), got):
        outer = outer + total[...].astype(WIDE) * counts(quad ^ step, quad)
    pieces = [piece[...].astype(WIDE) for piece in held]
    for to in OPS:
        inner = outer
        for op in OPS:
            inner = inner + pieces[op] * counts(came(first, op), sent(back, to))
        outs[to][...] = inner.astype(LOW)


def exchange(value, axis, bits):
    size = lax.axis_size(axis)
    return lax.ppermute(value, axis, [(i, i ^ bits) for i in range(size)])


def cross(value, wave, op):
    cores = lax.axis_size("tp")
    pairs = []
    for i in range(lax.axis_size("seq")):
        for t in range(cores):
            member = targets(wave, t % 2, op)[i % QUAD]
            pairs.append((i * cores + t, (i - i % QUAD + member) * cores + (t ^ 1)))
    return lax.ppermute(value, ("seq", "tp"), pairs)


def exclusive_sum(held, before, *after):
    first, back = (FIRST, BACK) if before else (FIRST_GRAD, BACK_GRAD)
    held = [cross(held[op], first, op) for op in OPS]
    total = sum(piece.astype(WIDE) for piece in held).astype(LOW)
    quads = lax.axis_size("seq") // QUAD
    got = []
    for step in quad_steps(quads, before):
        targets = quad_targets(quads, step, before)
        pairs = [(z * QUAD + i, targets[z] * QUAD + i) for z in range(quads) for i in range(QUAD)]
        got.append(lax.ppermute(total, "seq", pairs))
    vmem = [pl.BlockSpec(memory_space=pltpu.VMEM)] * (QUAD + len(got))
    sums = call(
        functools.partial(sums_kernel, before, quads),
        [jax.ShapeDtypeStruct(x.shape, x.dtype) for x in held],
        (*held, *got, *after),
        0,
        in_specs=vmem + [pl.BlockSpec(memory_space=pl.ANY)] * len(after),
    )
    return [cross(sums[op], back, op) for op in OPS]


def sum_over_heads(value):
    bit = 1
    while bit < lax.axis_size("tp"):
        value = value + exchange(value, "tp", bit)
        bit *= 2
    return value


def body(q, k, v, c):
    count, width = q.shape
    features = width * lax.axis_size("tp")
    shape = jax.ShapeDtypeStruct
    state = shape((DH, DH), LOW)
    wide = shape((count, width), WIDE)
    low = shape((count, width), LOW)
    unit = 2 * count * DH * DH * QUAD
    buffers = [pltpu.VMEM(k.shape, LOW)] * 2 + [pltpu.SemaphoreType.DMA((2, CHUNKS))]
    held = call(
        state_kernel, [state] * QUAD, (k, v), unit, room=53.75,
        in_specs=[pl.BlockSpec(memory_space=pltpu.HBM)] * 2,
        scratch_shapes=buffers,
    )
    scores, local, turned = call(
        local_kernel,
        [shape((QUAD, count, count), LOW), wide, shape((QUAD, DH, count), LOW)],
        (q, k, v),
        4 * unit,
    )
    prefix = exclusive_sum(held, True)
    part = shape((count, DH), WIDE)
    mixed, square, product = call(
        functools.partial(mixed_kernel, EARLY),
        [shape((2, count, DH), WIDE), part, part],
        (local, q, c, *[prefix[op] for op in EARLY]),
        unit,
    )
    late, sums = call(
        sums_of_tokens_kernel,
        [shape((2, count, DH), WIDE), shape((2, count), WIDE)],
        (local, q, c, *[prefix[op] for op in LATE], square, product),
        unit,
    )
    sums = sum_over_heads(sums)
    *terms, g = call(
        functools.partial(grad_kernel, features),
        [state] * QUAD + [low],
        (mixed, late, c, turned, sums),
        unit,
        scratch_shapes=[pltpu.VMEM((QUAD, DH, DH), LOW)],
    )
    normed_out, query_grad, key_local, value_local = call(
        functools.partial(back_kernel, features),
        [low, low, wide, wide],
        (q, k, v, g, scores, mixed, late, sums, *prefix),
        9 * unit,
    )
    suffix = exclusive_sum(terms, False, key_local)
    early = shape((2, count, DH), LOW)
    key_early, value_early = call(
        early_kernel, [early] * 2, (k, v, key_local, value_local, *[suffix[op] for op in EARLY]), 2 * unit
    )
    key_grad, value_grad = call(
        last_kernel, [low, low], (k, v, key_local, value_local, *[suffix[op] for op in LATE], key_early, value_early), unit
    )
    return (normed_out, query_grad, key_grad, value_grad)


def solution(mesh):
    spec = P("seq", "tp")
    return jax.shard_map(body, mesh=mesh, in_specs=(spec,) * 4, out_specs=(spec,) * 4, check_vma=False)
```
